32 devices in a mesh: stream: 4 (over y, core), seq: 8 (over z, x).
Axes of the slice: x: 2, y: 2, z: 4, core: 2. Of those that a mesh axis runs over, the one named last changes fastest.
Arguments:
- step_codes: int32 [1024, 16, 64], P('seq', None, 'stream'), may hold values from 0 to 254, as said below
- segments: int32 [1024, 16], P('seq'), may hold values from 0 to 15, as said below
- embed_table: float32 [1297, 256], replicated, may hold values from -1.5 to 1.5
- qkv_weight: float32 [2, 256, 768], replicated, may hold values from -0.375 to 0.375
- square_weight: float32 [2, 2, 256, 256], replicated, may hold values from -1 to 1
- up_weight: float32 [2, 256, 1024], replicated, may hold values from -0.375 to 0.375
- down_weight: float32 [2, 1024, 256], replicated, may hold values from -0.1875 to 0.1875
- small_params: float32 [9, 256], replicated, may hold values from 0.5 to 1.5
- head_weight: float32 [256, 1280], replicated, may hold values from -0.375 to 0.375
- moment_table: float32 [1297, 256], replicated, may hold values from -5.722046e-06 to 5.722046e-06
- moment_qkv: float32 [2, 256, 768], replicated, may hold values from -5.722046e-06 to 5.722046e-06
- moment_square: float32 [2, 2, 256, 256], replicated, may hold values from -5.722046e-06 to 5.722046e-06
- moment_up: float32 [2, 256, 1024], replicated, may hold values from -5.722046e-06 to 5.722046e-06
- moment_down: float32 [2, 1024, 256], replicated, may hold values from -5.722046e-06 to 5.722046e-06
- moment_small: float32 [9, 256], replicated, may hold values from -1.9073486e-05 to 1.9073486e-05
- moment_head: float32 [256, 1280], replicated, may hold values from -5.722046e-06 to 5.722046e-06
- average_table: float32 [1297, 256], replicated, may hold values from -1.5 to 1.5
- average_qkv: float32 [2, 256, 768], replicated, may hold values from -0.375 to 0.375
- average_square: float32 [2, 2, 256, 256], replicated, may hold values from -1 to 1
- average_up: float32 [2, 256, 1024], replicated, may hold values from -0.375 to 0.375
- average_down: float32 [2, 1024, 256], replicated, may hold values from -0.1875 to 0.1875
- average_small: float32 [9, 256], replicated, may hold values from 0.5 to 1.5
- average_head: float32 [256, 1280], replicated, may hold values from -0.375 to 0.375
Outputs:
- loss_sum: float32 [], replicated
- term_count: float32 [], replicated
- grad_norm: float32 [], replicated
- new_table: float32 [1297, 256], replicated
- new_qkv: float32 [2, 256, 768], replicated
- new_square: float32 [2, 2, 256, 256], replicated
- new_up: float32 [2, 256, 1024], replicated
- new_down: float32 [2, 1024, 256], replicated
- new_small: float32 [9, 256], replicated
- new_head: float32 [256, 1280], replicated
- next_moment_table: float32 [1297, 256], replicated
- next_moment_qkv: float32 [2, 256, 768], replicated
- next_moment_square: float32 [2, 2, 256, 256], replicated
- next_moment_up: float32 [2, 256, 1024], replicated
- next_moment_down: float32 [2, 1024, 256], replicated
- next_moment_small: float32 [9, 256], replicated
- next_moment_head: float32 [256, 1280], replicated
- next_average_table: float32 [1297, 256], replicated
- next_average_qkv: float32 [2, 256, 768], replicated
- next_average_square: float32 [2, 2, 256, 256], replicated
- next_average_up: float32 [2, 256, 1024], replicated
- next_average_down: float32 [2, 1024, 256], replicated
- next_average_small: float32 [9, 256], replicated
- next_average_head: float32 [256, 1280], replicated
The draws below stay inside these ranges and needn't reach their ends.
Inputs may be any that keep to these rules, and one draw needn't show every extreme that they name: `step_codes`: columns j < 32 hold latent codes below 32; column 32 an action below 18, column 33 a discount of 0 or 1, column 48 a reward class below 255; all other columns are 0. `segments`: each sequence's ids start at 0 and rise by 0 or 1 from step to step.
All inputs are finite; a program needn't handle non-finite values.
Results may differ from the reference program's by a relative error of at most 0.014.
Values may be sent and summed in bfloat16 or wider, within the bound.
A program may use at most 256 MiB of HBM per device.

```python
import math
import jax
import jax.numpy as jnp
from jax import lax

D = 256
HEADS = 8
HD = 32
FF = 1024
CATS = 32
CLASSES = 32
NA = 18
RB = 255
LAYERS = 2
STEPS = 16
TOKS = 48
GROUP = 128
SEQS = 1024
ROWS = 1297
HCOLS = 1280
PARAMS = 2365952


def draw_step_codes(key, part):
    half_cols = CATS // 2
    keys = jax.random.split(key, 4)
    latent = jax.random.randint(keys[0], (SEQS, STEPS, CATS), 0, CLASSES, dtype=jnp.int32)
    action = jax.random.randint(keys[1], (SEQS, STEPS, 1), 0, NA, dtype=jnp.int32)
    discount = jax.random.randint(keys[2], (SEQS, STEPS, 1), 0, 2, dtype=jnp.int32)
    reward = jax.random.randint(keys[3], (SEQS, STEPS, 1), 0, RB, dtype=jnp.int32)
    reward = reward.at[0, 0, 0].set(RB - 1)
    action = action.at[0, 0, 0].set(NA - 1)
    latent = latent.at[0, 0, 0].set(CLASSES - 1)
    padding = jnp.zeros((SEQS, STEPS, half_cols - 2), jnp.int32)
    tail_cols = jnp.zeros((SEQS, STEPS, half_cols - 1), jnp.int32)
    return jnp.concatenate([latent, action, discount, padding, reward, tail_cols], axis=2)


def draw_segments(key, part):
    key = jax.random.fold_in(key, 7)
    spread = 20 * max(SEQS - 1, 1)
    drawn = jax.random.randint(key, (SEQS, STEPS), 0, spread, dtype=jnp.int32)
    rank = jnp.arange(SEQS, dtype=jnp.int32)[:, None]
    starts = (drawn >= 19 * rank).astype(jnp.int32)
    starts = starts * (jnp.arange(STEPS, dtype=jnp.int32)[None, :] > 0).astype(jnp.int32)
    return jnp.cumsum(starts, axis=1).astype(jnp.int32)


def noise(stream_key, dims, deviation, most, kind=jnp.bfloat16):
    values = deviation * jax.random.normal(stream_key, dims, jnp.float32)
    return jnp.clip(values, min=-most, max=most).astype(kind)


def setup_inputs(seed: int = 0) -> dict:
    key_list = jax.random.split(jax.random.key(seed), 24)
    return {
        "step_codes": draw_step_codes(jax.random.fold_in(key_list[23], 71), 0),
        "segments": draw_segments(jax.random.fold_in(key_list[23], 71), 0),
        "embed_table": noise(key_list[2], (ROWS, D), 0.25, 1.5, jnp.float32),
        "qkv_weight": noise(key_list[3], (LAYERS, D, 3 * D), D ** -0.5, 0.375, jnp.float32),
        "square_weight": noise(key_list[4], (LAYERS, 2, D, D), (D // 8) ** -0.5, 1.0, jnp.float32),
        "up_weight": noise(key_list[5], (LAYERS, D, FF), D ** -0.5, 0.375, jnp.float32),
        "down_weight": noise(key_list[6], (LAYERS, FF, D), FF ** -0.5, 0.1875, jnp.float32),
        "small_params": jnp.clip(1.0 + 0.1 * jax.random.normal(key_list[7], (4 * LAYERS + 1, D), jnp.float32), 0.5, 1.5),
        "head_weight": noise(key_list[8], (D, HCOLS), D ** -0.5, 0.375, jnp.float32),
        "moment_table": noise(key_list[9], (ROWS, D), (0.2 * (SEQS * STEPS * PARAMS) ** -0.5), 5.7220458984375e-06, jnp.float32),
        "moment_qkv": noise(key_list[10], (LAYERS, D, 3 * D), (0.2 * (SEQS * STEPS * PARAMS) ** -0.5), 5.7220458984375e-06, jnp.float32),
        "moment_square": noise(key_list[11], (LAYERS, 2, D, D), (0.2 * (SEQS * STEPS * PARAMS) ** -0.5), 5.7220458984375e-06, jnp.float32),
        "moment_up": noise(key_list[12], (LAYERS, D, FF), (0.2 * (SEQS * STEPS * PARAMS) ** -0.5), 5.7220458984375e-06, jnp.float32),
        "moment_down": noise(key_list[13], (LAYERS, FF, D), (0.2 * (SEQS * STEPS * PARAMS) ** -0.5), 5.7220458984375e-06, jnp.float32),
        "moment_small": noise(key_list[14], (4 * LAYERS + 1, D), (0.6 * (SEQS * STEPS * PARAMS) ** -0.5), 1.9073486328125e-05, jnp.float32),
        "moment_head": noise(key_list[15], (D, HCOLS), (0.2 * (SEQS * STEPS * PARAMS) ** -0.5), 5.7220458984375e-06, jnp.float32),
        "average_table": noise(key_list[16], (ROWS, D), 0.25, 1.5, jnp.float32),
        "average_qkv": noise(key_list[17], (LAYERS, D, 3 * D), D ** -0.5, 0.375, jnp.float32),
        "average_square": noise(key_list[18], (LAYERS, 2, D, D), (D // 8) ** -0.5, 1.0, jnp.float32),
        "average_up": noise(key_list[19], (LAYERS, D, FF), D ** -0.5, 0.375, jnp.float32),
        "average_down": noise(key_list[20], (LAYERS, FF, D), FF ** -0.5, 0.1875, jnp.float32),
        "average_small": jnp.clip(1.0 + 0.1 * jax.random.normal(key_list[21], (4 * LAYERS + 1, D), jnp.float32), 0.5, 1.5),
        "average_head": noise(key_list[22], (D, HCOLS), D ** -0.5, 0.375, jnp.float32),
    }


@jax.custom_vjp
def low(v):
    return lax.optimization_barrier(v.astype(jnp.bfloat16)).astype(jnp.float32)

@jax.custom_vjp
def low_back(v):
    return v

def low_keep(v):
    return (low(v), None)

def low_pass(kept, grad):
    return (grad,)

def back_keep(v):
    return (v, None)

def back_low(kept, grad):
    return (low(grad),)
low.defvjp(low_keep, low_pass)
low_back.defvjp(back_keep, back_low)
HIGHEST = lax.Precision.HIGHEST
EPSILON = 1e-06
MOMENTUM_RATE = 0.9
AVERAGE_RATE = 0.7
CLIP_SCALE = 0.2
STEP_SCALE = 0.03
MASKED = -1e+30
POSITION_SCALE = 0.5

def matmul_high(left, right):
    return jnp.dot(left, right, precision=HIGHEST, preferred_element_type=jnp.float32)

def scaled_norm(values, gain):
    return values * lax.rsqrt(lax.optimization_barrier(jnp.mean(values * values, axis=-1, keepdims=True)) + EPSILON) * gain

def valid_steps(segments):
    same = (segments[:, 1:] == segments[:, :-1]).astype(jnp.float32)
    return jnp.concatenate([same, jnp.zeros((segments.shape[0], 1), jnp.float32)], axis=1)

def position_table():
    distance = jnp.arange(TOKS, dtype=jnp.float32)[:, None]
    rates = jnp.exp(jnp.arange(D // 2, dtype=jnp.float32) * (-2.0 * math.log(10000.0) / D))
    angle = distance * rates[None, :]
    return POSITION_SCALE * jnp.concatenate([jnp.sin(angle), jnp.cos(angle)], axis=1)

def shift_index():
    places = jnp.arange(TOKS, dtype=jnp.int32)
    return jnp.maximum(places[:, None] - places[None, :], 0).reshape(-1)

def sent_piece(values):
    return low_back(low(values))

def embed_tokens(table_low, step_codes):
    half_cols = CATS // 2
    offsets = jnp.arange(half_cols, dtype=jnp.int32) * CLASSES
    first = lax.optimization_barrier(jnp.sum(jnp.take(table_low, offsets + step_codes[..., :half_cols], axis=0), axis=2))
    second = lax.optimization_barrier(jnp.sum(jnp.take(table_low, half_cols * CLASSES + offsets + step_codes[..., half_cols:CATS], axis=0), axis=2))
    action = jnp.take(table_low, CATS * CLASSES + step_codes[..., CATS], axis=0)
    reward = jnp.take(table_low, CATS * CLASSES + NA + step_codes[..., 3 * half_cols], axis=0)
    tokens = jnp.stack([sent_piece(first) + sent_piece(second), sent_piece(action), sent_piece(reward)], axis=2)
    return tokens.reshape(-1, D)

def attention_mask(segments):
    token_seg = jnp.repeat(segments, 3, axis=1)
    causal = jnp.arange(TOKS)[:, None] >= jnp.arange(TOKS)[None, :]
    return (token_seg[:, :, None] == token_seg[:, None, :]) & causal[None]

def block_layer(hidden, qkv_w, out_w, rel_w, up_w, down_w, gain_a, gain_b, bias_u, bias_v, attend_mask):
    seq_count = attend_mask.shape[0]
    normed_a = low(scaled_norm(hidden, gain_a))
    qkv = low(low_back(matmul_high(normed_a, low(qkv_w))))
    query_rows, key_rows, value_rows = [p.reshape(seq_count, TOKS, HEADS, HD) for p in jnp.split(qkv, 3, axis=1)]
    pos_keys = low(low_back(matmul_high(low(position_table()), low(rel_w))))
    rel_keys = jnp.take(pos_keys, shift_index(), axis=0).reshape(TOKS, TOKS, HEADS, HD)
    query_u = low(query_rows + bias_u.reshape(HEADS, HD))
    query_v = low(query_rows + bias_v.reshape(HEADS, HD))
    content = jnp.einsum('bqhd,bkhd->bhqk', query_u, key_rows, precision=HIGHEST)
    place = jnp.einsum('bqhd,qkhd->bhqk', query_v, rel_keys, precision=HIGHEST)
    scores = (content + place) * HD ** (-0.5)
    scores = low_back(jnp.where(attend_mask[:, None], scores, MASKED))
    log_total = jax.nn.logsumexp(scores, axis=-1, keepdims=True)
    attention = low(jnp.exp(scores - log_total))
    mixed = jnp.einsum('bhqk,bkhd->bqhd', attention, value_rows, precision=HIGHEST).reshape(seq_count * TOKS, D)
    mixed = low(low_back(mixed))
    hidden = hidden + low_back(matmul_high(mixed, low(out_w)))
    normed_b = low(scaled_norm(hidden, gain_b))
    inner_act = low_back(matmul_high(normed_b, low(up_w)))
    active = low(jax.nn.gelu(inner_act, approximate=True))
    return hidden + low_back(matmul_high(active, low(down_w)))

def head_loss(hidden, final_gain, head_low, step_codes, segments):
    seq_count = segments.shape[0]
    features = scaled_norm(hidden, final_gain).reshape(seq_count, STEPS, 3, D)[:, :, 1].reshape(seq_count * STEPS, D)
    logits = low_back(matmul_high(low(features), head_low))
    latent_cols = CATS * CLASSES
    latent = logits[:, :latent_cols].reshape(-1, CATS, CLASSES)
    following = jnp.concatenate([step_codes[:, 1:, :CATS], jnp.zeros((seq_count, 1, CATS), jnp.int32)], axis=1).reshape(-1, CATS)
    picked = jnp.take_along_axis(latent, following[..., None], axis=-1)[..., 0]
    latent_terms = lax.optimization_barrier(jnp.sum(jax.nn.logsumexp(latent, axis=-1) - picked, axis=-1))
    result = jnp.sum(latent_terms * valid_steps(segments).reshape(-1))
    discount = logits[:, latent_cols]
    target = step_codes[:, :, CATS + 1].reshape(-1).astype(jnp.float32)
    result = result + jnp.sum(jax.nn.softplus(discount) - target * discount)
    reward = logits[:, latent_cols + 1:]
    reward_class = step_codes[:, :, 3 * (CATS // 2)].reshape(-1)
    chosen = jnp.take_along_axis(reward, reward_class[:, None], axis=-1)[:, 0]
    return result + jnp.sum(jax.nn.logsumexp(reward, axis=-1) - chosen)

def group_loss(params, step_codes, segments):
    table, qkv_w, square_w, up_w, down_w, smalls, head = params
    hidden = embed_tokens(low(table), step_codes)
    attend_mask = attention_mask(segments)
    for layer_id in range(LAYERS):
        hidden = block_layer(hidden, qkv_w[layer_id], square_w[layer_id, 0], square_w[layer_id, 1], up_w[layer_id], down_w[layer_id], smalls[4 * layer_id], smalls[4 * layer_id + 1], smalls[4 * layer_id + 2], smalls[4 * layer_id + 3], attend_mask)
    return head_loss(hidden, smalls[4 * LAYERS], low(head), step_codes, segments)

def advance(weight, moment, average, gradient, factor, step_rate):
    clipped = gradient * factor
    moment_new = MOMENTUM_RATE * moment + clipped
    weight_new = weight - step_rate * (clipped + MOMENTUM_RATE * moment_new)
    average_new = AVERAGE_RATE * average + (1.0 - AVERAGE_RATE) * weight_new
    return (weight_new, moment_new, average_new)

def reference(step_codes, segments, embed_table, qkv_weight, square_weight, up_weight, down_weight, small_params, head_weight, moment_table, moment_qkv, moment_square, moment_up, moment_down, moment_small, moment_head, average_table, average_qkv, average_square, average_up, average_down, average_small, average_head):
    weights = (embed_table, qkv_weight, square_weight, up_weight, down_weight, small_params, head_weight)
    moments = (moment_table, moment_qkv, moment_square, moment_up, moment_down, moment_small, moment_head)
    averages = (average_table, average_qkv, average_square, average_up, average_down, average_small, average_head)
    groups = SEQS // GROUP
    code_blocks = step_codes.reshape(groups, GROUP, STEPS, 2 * CATS)
    seg_blocks = segments.reshape(groups, GROUP, STEPS)
    term_count = CATS * jnp.sum(valid_steps(segments)) + 2.0 * SEQS * STEPS

    def loss_of(params):

        def one_group(carry, inputs):
            return (carry + jax.checkpoint(group_loss)(params, inputs[0], inputs[1]), None)
        summed, _ = lax.scan(one_group, jnp.zeros((), jnp.float32), (code_blocks, seg_blocks))
        return (summed / term_count, summed)
    loss_value, pullback, loss_sum = jax.vjp(loss_of, weights, has_aux=True)
    gradients = pullback(jnp.ones((), loss_value.dtype))[0]
    grad_norm = jnp.sqrt(sum((jnp.sum(g * g) for g in gradients)))
    clip_value = CLIP_SCALE * (SEQS * STEPS) ** (-0.5)
    step_rate = STEP_SCALE * PARAMS ** 0.5 / clip_value
    factor = clip_value / jnp.maximum(grad_norm, clip_value)
    updated = [advance(w, m, e, g, factor, step_rate) for w, m, e, g in zip(weights, moments, averages, gradients)]
    return (loss_sum, term_count, grad_norm, updated[0][0], updated[1][0], updated[2][0], updated[3][0], updated[4][0], updated[5][0], updated[6][0], updated[0][1], updated[1][1], updated[2][1], updated[3][1], updated[4][1], updated[5][1], updated[6][1], updated[0][2], updated[1][2], updated[2][2], updated[3][2], updated[4][2], updated[5][2], updated[6][2])
```

```python
import math

import jax
import jax.numpy as jnp
import numpy as np
from jax import lax
from jax.experimental import pallas as pl
from jax.experimental.pallas import tpu as pltpu
from jax.sharding import PartitionSpec as P

D = 256
HEADS = 8
HD = 32
FF = 1024
CATS = 32
CLASSES = 32
NA = 18
STEPS = 16
TOKS = 48
HK = HEADS * TOKS
LAYERS = 2
HCOLS = 1280
TROWS = 1408
CHUNK = 8
EPSILON = 1e-06
MOMENTUM_RATE = 0.9
AVERAGE_RATE = 0.7
CLIP_SCALE = 0.2
STEP_SCALE = 0.03
MASKED = -1e30
POSITION_SCALE = 0.5
SCALE = HD ** (-0.5)
BF = jnp.bfloat16
F32 = jnp.float32
VMEM_LIMIT = 63 * 1000 * 1000


def dot_nn(a, b):
    return lax.dot_general(a, b, (((1,), (0,)), ((), ())), preferred_element_type=F32)


def dot_nt(a, b):
    return lax.dot_general(a, b, (((1,), (1,)), ((), ())), preferred_element_type=F32)


def dot_tn(a, b):
    return lax.dot_general(a, b, (((0,), (0,)), ((), ())), preferred_element_type=F32)


def iota(shape, dim):
    return lax.broadcasted_iota(jnp.int32, shape, dim)


def position_rows():
    distance = np.arange(TOKS, dtype=np.float32)[:, None]
    rates = np.exp(np.arange(D // 2, dtype=np.float32) * np.float32(-2.0 * math.log(10000.0) / D))
    angle = (distance * rates[None, :].astype(np.float32)).astype(np.float32)
    table = np.float32(POSITION_SCALE) * np.concatenate([np.sin(angle), np.cos(angle)], axis=1)
    rows = np.zeros((3, TOKS, D), np.float32)
    for i in range(3):
        for j in range(3):
            for e in range(STEPS):
                d = 3 * (STEPS - 1 - e) + i - j
                if d >= 0:
                    rows[i, j * STEPS + e] = table[d]
    return rows.reshape(3 * TOKS, D)


def rms(values):
    return lax.rsqrt(jnp.mean(values * values, axis=-1, keepdims=True) + EPSILON)


def head_mask(h, rows):
    lane = iota((rows, 128), 1)
    low = (h % 4) * HD
    return ((lane >= low) & (lane < low + HD)).astype(F32).astype(BF)


def expand(rows):
    zero = jnp.zeros((TOKS, 128), BF)
    parts = []
    for h in range(HEADS):
        half = rows[:, 128 * (h // 4) : 128 * (h // 4) + 128] * head_mask(h, TOKS)
        parts.append(jnp.concatenate([half, zero] if h < 4 else [zero, half], axis=1))
    return jnp.concatenate(parts, axis=0)


def fold(values):
    lane = iota((TOKS, 128), 1)
    halves = []
    for g in range(2):
        total = None
        for h in range(4):
            part = values[(4 * g + h) * TOKS : (4 * g + h + 1) * TOKS, 128 * g : 128 * g + 128]
            total = part if total is None else jnp.where(lane >= h * HD, part, total)
        halves.append(total)
    return jnp.concatenate(halves, axis=1)


def spans(tile):
    found = []
    for h in range(HEADS):
        low, high = max(TOKS * h - 128 * tile, 0), min(TOKS * (h + 1) - 128 * tile, 128)
        if low < high:
            found.append((h, low, high))
    return found


def segment_max(scores):
    rows = scores.shape[0]
    lane = iota((rows, 128), 1)
    tiles = [scores[:, 128 * t : 128 * t + 128] for t in range(3)]
    best = {}
    for t in range(3):
        for h, low, high in spans(t):
            part = jnp.where((lane >= low) & (lane < high), tiles[t], -3e38)
            best[h] = part if h not in best else jnp.maximum(best[h], part)
    best = {h: jnp.max(v, axis=1, keepdims=True) for h, v in best.items()}
    outs = []
    for t in range(3):
        total = None
        for h, low, high in spans(t):
            wide = jnp.broadcast_to(best[h], (rows, 128))
            total = wide if total is None else jnp.where(lane >= low, wide, total)
        outs.append(total)
    return jnp.concatenate(outs, axis=1)


def unskew(values):
    row = iota((STEPS, HK), 0)
    values = jnp.concatenate(
        [pltpu.roll(values[:8], 15, 1), pltpu.roll(values[8:], 7, 1)], axis=0
    )
    for bit in (1, 2, 4):
        values = jnp.where((row & bit) > 0, pltpu.roll(values, HK - bit, 1), values)
    return values


def compute_kernel(
    codes_ref,
    seg_ref,
    pos_ref,
    small_ref,
    table_ref,
    wqkv_ref,
    wsq_ref,
    wup_ref,
    wdown_ref,
    whead_ref,
    g_ref,
    e_ref,
    x_s,
    att_s,
    pu_s,
    r_s,
    o_s,
    mid_s,
    hb_s,
    gp_s,
    a_s,
    b_s,
    dyl_s,
    dml_s,
    dx_s,
    rk_s,
    start_s,
    l_s,
    slope_s,
):
    seqs = codes_ref.shape[1]
    steps_all = seqs * STEPS
    toks = seqs * TOKS
    chunks = seqs // CHUNK
    rows_c = CHUNK * TOKS

    seg = seg_ref[...].astype(F32)
    seg3 = jnp.broadcast_to(seg[:, None, :], (seqs, STEPS, STEPS))
    i1, i2 = iota((seqs, STEPS, STEPS), 1), iota((seqs, STEPS, STEPS), 2)
    seg_col = jnp.sum(jnp.where(i1 == i2, seg3, 0.0), axis=2, keepdims=True)
    start = jnp.sum(jnp.where(seg3 < seg_col, 1.0, 0.0), axis=2, keepdims=True)
    start_s[...] = jnp.broadcast_to(start, (seqs, STEPS, 128))
    follow = jnp.where((i2 == i1 + 1) & (seg3 == seg_col), 1.0, 0.0).reshape(steps_all, STEPS)
    valid_row = dot_nt(jnp.ones((8, STEPS), BF), follow.astype(BF))[:1]

    codes = [codes_ref[k].reshape(steps_all, STEPS).astype(F32) for k in range(4)]
    spread = (iota((STEPS, 512), 1) // CLASSES == iota((STEPS, 512), 0)).astype(F32).astype(BF)
    class_lane = (iota((128, 512), 1) % CLASSES).astype(F32)
    for c in range(steps_all // 128):
        rows = slice(128 * c, 128 * c + 128)
        seq_rows = slice(8 * c, 8 * c + 8)
        halves = []
        for k in range(2):
            hot = (dot_nn(codes[k][rows].astype(BF), spread) == class_lane).astype(F32).astype(BF)
            piece = dot_nn(hot, table_ref[512 * k : 512 * k + 512]).astype(BF).astype(F32)
            halves.append(piece)
        x_s[0, seq_rows, 0] = (halves[0] + halves[1]).reshape(8, STEPS, D)
        lane = iota((128, 128), 1).astype(F32)
        hot = (codes[2][rows, 0:1] == lane).astype(F32).astype(BF)
        x_s[0, seq_rows, 1] = (
            dot_nn(hot, table_ref[1024:1152]).astype(BF).astype(F32).reshape(8, STEPS, D)
        )
        lane = iota((128, 384), 1).astype(F32)
        hot = (codes[3][rows, 0:1] + NA == lane).astype(F32).astype(BF)
        x_s[0, seq_rows, 2] = (
            dot_nn(hot, table_ref[1024:1408]).astype(BF).astype(F32).reshape(8, STEPS, D)
        )

    for layer in range(LAYERS):
        rk = dot_nn(pos_ref[...], wsq_ref[layer, 1]).astype(BF)
        for k in range(3):
            rk_s[layer, k] = expand(rk[TOKS * k : TOKS * k + TOKS])

    lane_hk = iota((TOKS, HK), 1) % TOKS
    key_step = lane_hk % STEPS
    key_time = 3 * key_step + lane_hk // STEPS
    row_tok = iota((TOKS, HK), 0)
    query_time = 3 * (row_tok % STEPS) + row_tok // STEPS
    causal = key_time <= query_time
    key_step_f = key_step.astype(F32)
    sum_hd = (iota((HK, D), 0) // TOKS == iota((HK, D), 1) // HD).astype(F32).astype(BF)
    sum_hk = (iota((D, HK), 0) // HD == iota((D, HK), 1) // TOKS).astype(F32).astype(BF)

    for layer in range(LAYERS):
        gain_a = small_ref[4 * layer : 4 * layer + 1]
        gain_b = small_ref[4 * layer + 1 : 4 * layer + 2]
        bias_u = small_ref[4 * layer + 2 : 4 * layer + 3]
        bias_v = small_ref[4 * layer + 3 : 4 * layer + 4]

        @pl.loop(0, chunks)
        def _(c):
            rows = pl.ds(pl.multiple_of(c * rows_c, rows_c), rows_c)
            x = x_s[layer, pl.ds(c * CHUNK, CHUNK)].reshape(rows_c, D)
            low = (x * rms(x) * gain_a).astype(BF)
            a_s[layer, rows] = low
            q = dot_nn(low, wqkv_ref[layer, :, :256]).astype(BF).astype(F32)
            qu = (q + bias_u).astype(BF)
            qv = (q + bias_v).astype(BF)
            key = dot_nn(low, wqkv_ref[layer, :, 256:512]).astype(BF)
            val = dot_nn(low, wqkv_ref[layer, :, 512:]).astype(BF)
            att_s[layer, rows, 0:256] = qu
            att_s[layer, rows, 256:512] = qv
            att_s[layer, rows, 512:768] = key
            att_s[layer, rows, 768:1024] = val
            qv4 = qv.reshape(CHUNK, 3, STEPS, D)
            place = [
                dot_nt(qv4[:, k].reshape(CHUNK * STEPS, D), rk_s[layer, k]) for k in range(3)
            ]
            start_c = start_s[pl.ds(c * CHUNK, CHUNK)]
            for b in range(CHUNK):
                span = slice(TOKS * b, TOKS * b + TOKS)
                score = dot_nt(qu[span], expand(key[span]))
                shifted = [
                    pltpu.roll(
                        place[k][STEPS * b : STEPS * b + STEPS],
                        HK - (STEPS - 1),
                        1,
                        stride=1,
                        stride_axis=0,
                    )
                    for k in range(3)
                ]
                begin = jnp.concatenate([start_c[b]] * 3, axis=0)
                begin = jnp.concatenate([begin] * 3, axis=1)
                score = (score + jnp.concatenate(shifted, axis=0)) * SCALE
                score = jnp.where(causal & (key_step_f >= begin), score, MASKED)
                probs = jnp.exp(score - segment_max(score)).astype(BF)
                pu_s[layer, pl.ds(pl.multiple_of(c * rows_c + TOKS * b, TOKS), TOKS)] = probs
                l_s[span] = dot_nn(probs, expand(val[span]))
            recip = 1.0 / dot_nn(pu_s[layer, rows], sum_hd)
            out = l_s[...] * recip
            r_s[layer, rows] = recip
            o_s[layer, rows] = out
            mid = x + dot_nn(out.astype(BF), wsq_ref[layer, 0])
            mid_s[layer, rows] = mid
            low = (mid * rms(mid) * gain_b).astype(BF)
            b_s[layer, rows] = low
            for j in range(FF // 256):
                cols = slice(256 * j, 256 * j + 256)
                inner = dot_nn(low, wup_ref[layer, :, cols])
                square = inner * inner
                c0 = math.sqrt(2.0 / math.pi)
                tanh = jnp.tanh(c0 * inner * (1.0 + 0.044715 * square))
                half = 0.5 * (1.0 + tanh)
                hb_s[layer, rows, cols] = (inner * half).astype(BF)
                gp_s[layer, rows, cols] = (
                    half
                    + (0.5 * c0) * inner * (1.0 - tanh * tanh) * (1.0 + (3 * 0.044715) * square)
                ).astype(BF)
            nxt = mid + dot_nn(hb_s[layer, rows], wdown_ref[layer])
            x_s[layer + 1, pl.ds(c * CHUNK, CHUNK)] = nxt.reshape(CHUNK, 3, STEPS, D)

    gain_f = small_ref[4 * LAYERS : 4 * LAYERS + 1]
    xf = x_s[LAYERS, :, 1].reshape(steps_all, D)
    feat = (xf * rms(xf) * gain_f).astype(BF)
    spread_t = (iota((512, STEPS), 0) // CLASSES == iota((512, STEPS), 1)).astype(F32).astype(BF)
    class_row = iota((4, CLASSES, steps_all), 1).astype(F32)
    loss = jnp.zeros((4, steps_all), F32)
    for k in range(2):
        follow_codes = pltpu.roll(codes[k], steps_all - 1, 0).astype(BF)
        for j in range(4):
            base = 512 * k + 128 * j
            logits = dot_nt(whead_ref[base : base + 128], feat).reshape(4, CLASSES, steps_all)
            target = dot_nt(spread_t[128 * j : 128 * j + 128], follow_codes)
            hot = target.reshape(4, CLASSES, steps_all) == class_row
            top = jnp.max(logits, axis=1, keepdims=True)
            grown = jnp.exp(logits - top)
            total = jnp.sum(grown, axis=1, keepdims=True)
            picked = jnp.sum(jnp.where(hot, logits, 0.0), axis=1)
            loss = loss + valid_row * (jnp.log(total[:, 0]) + top[:, 0] - picked)
            slope = (grown * (1.0 / total) - jnp.where(hot, 1.0, 0.0)) * valid_row[None]
            slope_s[base : base + 128] = slope.reshape(128, steps_all).astype(BF)
    pick0 = (iota((8, STEPS), 1) == 0).astype(F32).astype(BF)
    pick1 = (iota((8, STEPS), 1) == 1).astype(F32).astype(BF)
    action_row = dot_nt(pick0, codes[2].astype(BF))[:1]
    discount_row = dot_nt(pick1, codes[2].astype(BF))[:1]
    reward_row = dot_nt(pick0, codes[3].astype(BF))[:1]
    logits = dot_nt(whead_ref[1024:1280], feat)
    row = iota((256, steps_all), 0)
    hot = row == (reward_row + 1.0).astype(jnp.int32)
    disc = logits[:1]
    masked = jnp.where(row == 0, -3e38, logits)
    top = jnp.max(masked, axis=0, keepdims=True)
    grown = jnp.exp(masked - top)
    total = jnp.sum(grown, axis=0, keepdims=True)
    picked = jnp.sum(jnp.where(hot, logits, 0.0), axis=0, keepdims=True)
    fade = jnp.exp(-jnp.abs(disc))
    soft = jnp.maximum(disc, 0.0) + jnp.log(1.0 + fade)
    sigm = jnp.where(disc >= 0.0, 1.0, fade) / (1.0 + fade)
    loss_row = (
        jnp.sum(loss, axis=0, keepdims=True)
        + jnp.log(total)
        + top
        - picked
        + soft
        - discount_row * disc
    )
    slope = grown * (1.0 / total) - jnp.where(hot, 1.0, 0.0)
    slope = jnp.where(row == 0, sigm - discount_row, slope)
    slope_s[1024:1280] = slope.astype(BF)
    loss_sum = jnp.sum(loss_row)
    count = jnp.sum(valid_row) * CATS + 2.0 * steps_all
    e_ref[9:10] = jnp.full((1, D), loss_sum, F32)
    e_ref[10:11] = jnp.full((1, D), count, F32)
    e_ref[11:16] = jnp.zeros((5, D), F32)

    feat_t = feat.astype(F32).T.astype(BF)
    for j in range(5):
        part = dot_nt(feat_t, slope_s[256 * j : 256 * j + 256])
        for k in range(2):
            base = 256 * (2 * j + k)
            g_ref[base : base + 256] = part[:, 128 * k : 128 * k + 128].astype(BF)
    dfeat = dot_tn(slope_s[...], whead_ref[...])
    scale_f = rms(xf)
    hat = xf * scale_f
    e_ref[8:9] = jnp.sum(dfeat * hat, axis=0, keepdims=True)
    inner = dfeat * gain_f
    dxf = scale_f * (inner - hat * jnp.mean(inner * hat, axis=-1, keepdims=True))
    dx_s[...] = jnp.zeros(dx_s.shape, F32)
    dx_s[:, 1] = dxf.reshape(seqs, STEPS, D)

    for layer in reversed(range(LAYERS)):
        gain_a = small_ref[4 * layer : 4 * layer + 1]
        gain_b = small_ref[4 * layer + 1 : 4 * layer + 2]
        e_ref[4 * layer : 4 * layer + 4] = jnp.zeros((4, D), F32)

        @pl.loop(0, chunks)
        def _(c):
            rows = pl.ds(pl.multiple_of(c * rows_c, rows_c), rows_c)
            dy = dx_s[pl.ds(c * CHUNK, CHUNK)].reshape(rows_c, D)
            dyl = dy.astype(BF)
            dyl_s[rows] = dyl
            for j in range(FF // 256):
                cols = slice(256 * j, 256 * j + 256)
                dact = dot_nt(dyl, wdown_ref[layer, cols])
                gp_s[layer, rows, cols] = (dact * gp_s[layer, rows, cols].astype(F32)).astype(BF)
            dlow = dot_nt(gp_s[layer, rows], wup_ref[layer])
            mid = mid_s[layer, rows]
            scale = rms(mid)
            hat = mid * scale
            dgain = jnp.sum(dlow * hat, axis=0, keepdims=True)
            inner = dlow * gain_b
            dmid = scale * (inner - hat * jnp.mean(inner * hat, axis=-1, keepdims=True)) + dy
            e_ref[4 * layer + 1 : 4 * layer + 2] += dgain
            dml = dmid.astype(BF)
            dml_s[rows] = dml
            do = dot_nt(dml, wsq_ref[layer, 0]).astype(BF).astype(F32)
            do = (do * r_s[layer, rows]).astype(BF)
            mass = do.astype(F32) * o_s[layer, rows]
            mass_hi = mass.astype(BF)
            mass_lo = (mass - mass_hi.astype(F32)).astype(BF)
            delta = dot_nn(mass_hi, sum_hk) + dot_nn(mass_lo, sum_hk)
            qu = att_s[layer, rows, 0:256]
            key = att_s[layer, rows, 512:768]
            val = att_s[layer, rows, 768:1024]
            draws = []
            for b in range(CHUNK):
                span = slice(TOKS * b, TOKS * b + TOKS)
                probs = pu_s[layer, pl.ds(pl.multiple_of(c * rows_c + TOKS * b, TOKS), TOKS)]
                dprob = dot_nt(do[span], expand(val[span]))
                dscore = (probs.astype(F32) * (dprob - delta[span])).astype(BF)
                wide = dscore.astype(F32)
                draws.append(
                    [unskew(wide[STEPS * k : STEPS * k + STEPS]).astype(BF) for k in range(3)]
                )
                dval = fold(dot_tn(probs, do[span])).astype(BF)
                dkey = (fold(dot_tn(dscore, qu[span])) * SCALE).astype(BF)
                l_s[span] = dot_nn(dscore, expand(key[span])) * SCALE
                out_rows = pl.ds(pl.multiple_of(c * rows_c + TOKS * b, TOKS), TOKS)
                pu_s[layer, out_rows] = jnp.concatenate(draws[b], axis=0)
                att_s[layer, out_rows, 512:768] = dkey
                att_s[layer, out_rows, 768:1024] = dval
            dqv = [
                dot_nn(
                    jnp.concatenate([draws[b][k] for b in range(CHUNK)], axis=0), rk_s[layer, k]
                ).reshape(CHUNK, 1, STEPS, D)
                for k in range(3)
            ]
            dqv = jnp.concatenate(dqv, axis=1).reshape(rows_c, D) * SCALE
            dqu = l_s[...]
            e_ref[4 * layer + 2 : 4 * layer + 3] += jnp.sum(dqu, axis=0, keepdims=True)
            e_ref[4 * layer + 3 : 4 * layer + 4] += jnp.sum(dqv, axis=0, keepdims=True)
            dq = (dqu + dqv).astype(BF)
            att_s[layer, rows, 0:256] = dq
            dlow = (
                dot_nt(dq, wqkv_ref[layer, :, :256])
                + dot_nt(att_s[layer, rows, 512:768], wqkv_ref[layer, :, 256:512])
                + dot_nt(att_s[layer, rows, 768:1024], wqkv_ref[layer, :, 512:])
            )
            x = x_s[layer, pl.ds(c * CHUNK, CHUNK)].reshape(rows_c, D)
            scale = rms(x)
            hat = x * scale
            e_ref[4 * layer : 4 * layer + 1] += jnp.sum(dlow * hat, axis=0, keepdims=True)
            inner = dlow * gain_a
            dx = scale * (inner - hat * jnp.mean(inner * hat, axis=-1, keepdims=True)) + dmid
            dx_s[pl.ds(c * CHUNK, CHUNK)] = dx.reshape(CHUNK, 3, STEPS, D)

        base = 2560 + 6656 * (LAYERS - 1 - layer)

        def put(offset, value):
            size = value.shape[0]
            for k in range(2):
                at = base + offset + k * size
                if not isinstance(at, int):
                    at = pl.multiple_of(at, 256)
                g_ref[pl.ds(at, size)] = value[:, 128 * k : 128 * k + 128].astype(BF)

        for j in range(4):
            part = dot_tn(hb_s[layer, :, 256 * j : 256 * j + 256], dyl_s[...])
            for k in range(2):
                g_ref[base + 1024 * k + 256 * j : base + 1024 * k + 256 * j + 256] = part[
                    :, 128 * k : 128 * k + 128
                ].astype(BF)
        for j in range(4):
            put(2048 + 512 * j, dot_tn(b_s[layer], gp_s[layer, :, 256 * j : 256 * j + 256]))
        put(4096, dot_tn(o_s[layer].astype(BF), dml_s[...]))
        drk = []
        draw = pu_s[layer].reshape(seqs, 3, STEPS, HK)
        qv = att_s[layer, :, 256:512].reshape(seqs, 3, STEPS, D)
        for k in range(3):
            wide = dot_tn(
                draw[:, k].reshape(steps_all, HK), qv[:, k].reshape(steps_all, D)
            )
            drk.append(fold(wide) * SCALE)
        put(4608, dot_tn(pos_ref[...], jnp.concatenate(drk, axis=0).astype(BF)))
        put(5120, dot_tn(a_s[layer], att_s[layer, :, 0:256]))
        put(5632, dot_tn(a_s[layer], att_s[layer, :, 512:768]))
        put(6144, dot_tn(a_s[layer], att_s[layer, :, 768:1024]))

    dtok = [dx_s[:, k].reshape(steps_all, D).astype(BF) for k in range(3)]
    base = 2560 + 6656 * LAYERS
    class_row = (iota((256, steps_all), 0) % CLASSES).astype(F32)
    for k in range(2):
        for j in range(2):
            wide = dot_nt(spread_t[256 * j : 256 * j + 256], codes[k].astype(BF))
            hot = (wide == class_row).astype(F32).astype(BF)
            part = dot_nn(hot, dtok[0])
            for h in range(2):
                at = base + 1280 * h + 512 * k + 256 * j
                g_ref[at : at + 256] = part[:, 128 * h : 128 * h + 128].astype(BF)
    row = iota((288, steps_all), 0)
    hot_a = (row == action_row.astype(jnp.int32)).astype(F32).astype(BF)
    hot_r = (row == (reward_row + NA).astype(jnp.int32)).astype(F32).astype(BF)
    part = dot_nn(hot_a, dtok[1]) + dot_nn(hot_r, dtok[2])
    for h in range(2):
        at = base + 1280 * h + 1024
        g_ref[at : at + 256] = part[:256, 128 * h : 128 * h + 128].astype(BF)
    e_ref[16:40] = part[256:280]


def compute(codes, seg, pos, small, table, wqkv, wsq, wup, wdown, whead_t):
    seqs = codes.shape[1]
    toks = seqs * TOKS
    f32, bf = jnp.float32, jnp.bfloat16
    vmem = pltpu.VMEM
    return pl.pallas_call(
        compute_kernel,
        out_shape=(
            jax.ShapeDtypeStruct((2560 + 6656 * LAYERS + 2560, 128), bf),
            jax.ShapeDtypeStruct((40, D), f32),
        ),
        in_specs=[pl.BlockSpec(memory_space=vmem)] * 10,
        out_specs=[pl.BlockSpec(memory_space=vmem)] * 2,
        scratch_shapes=[
            vmem((LAYERS + 1, seqs, 3, STEPS, D), f32),
            vmem((LAYERS, toks, 1024), bf),
            vmem((LAYERS, toks, HK), bf),
            vmem((LAYERS, toks, D), f32),
            vmem((LAYERS, toks, D), f32),
            vmem((LAYERS, toks, D), f32),
            vmem((LAYERS, toks, FF), bf),
            vmem((LAYERS, toks, FF), bf),
            vmem((LAYERS, toks, D), bf),
            vmem((LAYERS, toks, D), bf),
            vmem((toks, D), bf),
            vmem((toks, D), bf),
            vmem((seqs, 3, STEPS, D), f32),
            vmem((LAYERS, 3, HK, D), bf),
            vmem((seqs, STEPS, 128), f32),
            vmem((CHUNK * TOKS, D), f32),
            vmem((HCOLS, seqs * STEPS), bf),
        ],
        compiler_params=pltpu.CompilerParams(vmem_limit_bytes=VMEM_LIMIT),
        name="step",
    )(codes, seg, pos, small, table, wqkv, wsq, wup, wdown, whead_t)


def advance(weight, moment, average, gradient, factor, step_rate):
    clipped = gradient * factor
    moment_new = MOMENTUM_RATE * moment + clipped
    weight_new = weight - step_rate * (clipped + MOMENTUM_RATE * moment_new)
    average_new = AVERAGE_RATE * average + (1.0 - AVERAGE_RATE) * weight_new
    return (weight_new, moment_new, average_new)


def unpack(g, extra):
    def block(at, rows, columns):
        n = columns // 128
        return (
            g[at : at + rows * n].reshape(n, rows, 128).transpose(1, 0, 2).reshape(rows, columns)
        )

    head = block(0, 256, 1280)
    per = {}
    for layer in range(LAYERS):
        base = 2560 + 6656 * (LAYERS - 1 - layer)
        per[layer] = dict(
            down=block(base, 1024, 256),
            up=jnp.concatenate([block(base + 2048 + 512 * j, 256, 256) for j in range(4)], 1),
            out=block(base + 4096, 256, 256),
            rel=block(base + 4608, 256, 256),
            qkv=jnp.concatenate([block(base + 5120 + 512 * j, 256, 256) for j in range(3)], 1),
        )
    table = jnp.concatenate([block(2560 + 6656 * LAYERS, 1280, 256), extra[16:33]], 0)
    return (
        table,
        jnp.stack([per[i]["qkv"] for i in range(LAYERS)]),
        jnp.stack([jnp.stack([per[i]["out"], per[i]["rel"]]) for i in range(LAYERS)]),
        jnp.stack([per[i]["up"] for i in range(LAYERS)]),
        jnp.stack([per[i]["down"] for i in range(LAYERS)]),
        extra[:9],
        head,
    )


def on_device(step_codes, segments, *arrays):
    weights, moments, averages = arrays[:7], arrays[7:14], arrays[14:]
    stream_id = lax.axis_index("stream")
    streams = lax.axis_size("stream")
    group_seqs = step_codes.shape[0]
    own = group_seqs // streams
    codes = lax.all_to_all(
        step_codes.reshape(streams, own, STEPS, -1), "stream", split_axis=0, concat_axis=0
    )
    seg = lax.dynamic_slice_in_dim(segments, stream_id * own, own, 0)
    table, qkv, square, up, down, small, head = weights
    bf = jnp.bfloat16
    table_low = jnp.pad(table.astype(bf), ((0, TROWS - table.shape[0]), (0, 0)))
    pos = jnp.asarray(position_rows()).astype(bf)
    grads, extra = compute(
        codes,
        seg,
        pos,
        small,
        table_low,
        qkv.astype(bf),
        square.astype(bf),
        up.astype(bf),
        down.astype(bf),
        head.astype(bf).T,
    )
    grads, extra = lax.psum((grads.astype(jnp.float32), extra), ("stream", "seq"))
    loss_total, term_count = extra[9, 0], extra[10, 0]
    inverse = 1.0 / term_count
    reduced = unpack(grads, extra)
    grad_norm = jnp.sqrt(sum(jnp.sum(g * g) for g in reduced)) * inverse
    params_total = sum(w.size for w in weights)
    clip_value = CLIP_SCALE * (group_seqs * lax.axis_size("seq") * STEPS) ** (-0.5)
    step_rate = STEP_SCALE * params_total**0.5 / clip_value
    factor = inverse * clip_value / jnp.maximum(grad_norm, clip_value)
    updated = [
        advance(w, m, e, g, factor, step_rate)
        for w, m, e, g in zip(weights, moments, averages, reduced)
    ]
    return (
        loss_total,
        term_count,
        grad_norm,
        *(u[0] for u in updated),
        *(u[1] for u in updated),
        *(u[2] for u in updated),
    )


def solution(mesh):
    return jax.shard_map(
        on_device,
        mesh=mesh,
        in_specs=(P("seq", None, "stream"), P("seq", None)) + (P(),) * 21,
        out_specs=(P(),) * 24,
        check_vma=False,
    )
```

```python
import math

import jax
import jax.numpy as jnp
import numpy as np
from jax import lax
from jax.experimental import pallas as pl
from jax.experimental.pallas import tpu as pltpu
from jax.sharding import PartitionSpec as P

D = 256
HEADS = 8
HD = 32
FF = 1024
CATS = 32
CLASSES = 32
NA = 18
STEPS = 16
TOKS = 48
HK = HEADS * TOKS
LAYERS = 2
HCOLS = 1280
TROWS = 1408
CHUNK = 8
EPSILON = 1e-06
MOMENTUM_RATE = 0.9
AVERAGE_RATE = 0.7
CLIP_SCALE = 0.2
STEP_SCALE = 0.03
MASKED = -1e30
POSITION_SCALE = 0.5
SCALE = HD ** (-0.5)
BF = jnp.bfloat16
F32 = jnp.float32
VMEM_LIMIT = 63 * 1000 * 1000


def dot_nn(a, b):
    return lax.dot_general(a, b, (((1,), (0,)), ((), ())), preferred_element_type=F32)


def dot_nt(a, b):
    return lax.dot_general(a, b, (((1,), (1,)), ((), ())), preferred_element_type=F32)


def dot_tn(a, b):
    return lax.dot_general(a, b, (((0,), (0,)), ((), ())), preferred_element_type=F32)


def iota(shape, dim):
    return lax.broadcasted_iota(jnp.int32, shape, dim)


def position_rows():
    distance = np.arange(TOKS, dtype=np.float32)[:, None]
    rates = np.exp(np.arange(D // 2, dtype=np.float32) * np.float32(-2.0 * math.log(10000.0) / D))
    angle = (distance * rates[None, :].astype(np.float32)).astype(np.float32)
    table = np.float32(POSITION_SCALE) * np.concatenate([np.sin(angle), np.cos(angle)], axis=1)
    rows = np.zeros((3, TOKS, D), np.float32)
    for i in range(3):
        for j in range(3):
            for e in range(STEPS):
                d = 3 * (STEPS - 1 - e) + i - j
                if d >= 0:
                    rows[i, j * STEPS + e] = table[d]
    return rows.reshape(3 * TOKS, D)


def rms(values):
    return lax.rsqrt(jnp.mean(values * values, axis=-1, keepdims=True) + EPSILON)


def head_mask(h, rows):
    lane = iota((rows, 128), 1)
    low = (h % 4) * HD
    return ((lane >= low) & (lane < low + HD)).astype(F32).astype(BF)


def expand(rows):
    zero = jnp.zeros((TOKS, 128), BF)
    parts = []
    for h in range(HEADS):
        half = rows[:, 128 * (h // 4) : 128 * (h // 4) + 128] * head_mask(h, TOKS)
        parts.append(jnp.concatenate([half, zero] if h < 4 else [zero, half], axis=1))
    return jnp.concatenate(parts, axis=0)


def fold(values):
    lane = iota((TOKS, 128), 1)
    halves = []
    for g in range(2):
        total = None
        for h in range(4):
            part = values[(4 * g + h) * TOKS : (4 * g + h + 1) * TOKS, 128 * g : 128 * g + 128]
            total = part if total is None else jnp.where(lane >= h * HD, part, total)
        halves.append(total)
    return jnp.concatenate(halves, axis=1)


def spans(tile):
    found = []
    for h in range(HEADS):
        low, high = max(TOKS * h - 128 * tile, 0), min(TOKS * (h + 1) - 128 * tile, 128)
        if low < high:
            found.append((h, low, high))
    return found


def segment_max(scores):
    rows = scores.shape[0]
    lane = iota((rows, 128), 1)
    tiles = [scores[:, 128 * t : 128 * t + 128] for t in range(3)]
    best = {}
    for t in range(3):
        for h, low, high in spans(t):
            part = jnp.where((lane >= low) & (lane < high), tiles[t], -3e38)
            best[h] = part if h not in best else jnp.maximum(best[h], part)
    best = {h: jnp.max(v, axis=1, keepdims=True) for h, v in best.items()}
    outs = []
    for t in range(3):
        total = None
        for h, low, high in spans(t):
            wide = jnp.broadcast_to(best[h], (rows, 128))
            total = wide if total is None else jnp.where(lane >= low, wide, total)
        outs.append(total)
    return jnp.concatenate(outs, axis=1)


def unskew(values):
    row = iota((STEPS, HK), 0)
    values = jnp.concatenate(
        [pltpu.roll(values[:8], 15, 1), pltpu.roll(values[8:], 7, 1)], axis=0
    )
    for bit in (1, 2, 4):
        values = jnp.where((row & bit) > 0, pltpu.roll(values, HK - bit, 1), values)
    return values


def compute_kernel(
    codes_ref,
    seg_ref,
    pos_ref,
    small_ref,
    table_ref,
    wqkv_ref,
    wsq_ref,
    wup_ref,
    wdown_ref,
    whead_ref,
    g_ref,
    e_ref,
    x_s,
    att_s,
    pu_s,
    r_s,
    o_s,
    mid_s,
    hb_s,
    gp_s,
    a_s,
    b_s,
    dyl_s,
    dml_s,
    dx_s,
    rk_s,
    start_s,
    l_s,
    slope_s,
):
    seqs = codes_ref.shape[1]
    steps_all = seqs * STEPS
    toks = seqs * TOKS
    chunks = seqs // CHUNK
    rows_c = CHUNK * TOKS

    seg = seg_ref[...].astype(F32)
    seg3 = jnp.broadcast_to(seg[:, None, :], (seqs, STEPS, STEPS))
    i1, i2 = iota((seqs, STEPS, STEPS), 1), iota((seqs, STEPS, STEPS), 2)
    seg_col = jnp.sum(jnp.where(i1 == i2, seg3, 0.0), axis=2, keepdims=True)
    start = jnp.sum(jnp.where(seg3 < seg_col, 1.0, 0.0), axis=2, keepdims=True)
    start_s[...] = jnp.broadcast_to(start, (seqs, STEPS, 128))
    follow = jnp.where((i2 == i1 + 1) & (seg3 == seg_col), 1.0, 0.0).reshape(steps_all, STEPS)
    valid_row = dot_nt(jnp.ones((8, STEPS), BF), follow.astype(BF))[:1]

    codes = [codes_ref[k].reshape(steps_all, STEPS).astype(F32) for k in range(4)]
    spread = (iota((STEPS, 512), 1) // CLASSES == iota((STEPS, 512), 0)).astype(F32).astype(BF)
    class_lane = (iota((128, 512), 1) % CLASSES).astype(F32)
    for c in range(steps_all // 128):
        rows = slice(128 * c, 128 * c + 128)
        seq_rows = slice(8 * c, 8 * c + 8)
        halves = []
        for k in range(2):
            hot = (dot_nn(codes[k][rows].astype(BF), spread) == class_lane).astype(F32).astype(BF)
            piece = dot_nn(hot, table_ref[512 * k : 512 * k + 512]).astype(BF).astype(F32)
            halves.append(piece)
        x_s[0, seq_rows, 0] = (halves[0] + halves[1]).reshape(8, STEPS, D)
        lane = iota((128, 128), 1).astype(F32)
        hot = (codes[2][rows, 0:1] == lane).astype(F32).astype(BF)
        x_s[0, seq_rows, 1] = (
            dot_nn(hot, table_ref[1024:1152]).astype(BF).astype(F32).reshape(8, STEPS, D)
        )
        lane = iota((128, 384), 1).astype(F32)
        hot = (codes[3][rows, 0:1] + NA == lane).astype(F32).astype(BF)
        x_s[0, seq_rows, 2] = (
            dot_nn(hot, table_ref[1024:1408]).astype(BF).astype(F32).reshape(8, STEPS, D)
        )

    for layer in range(LAYERS):
        rk = dot_nn(pos_ref[...], wsq_ref[layer, 1]).astype(BF)
        for k in range(3):
            rk_s[layer, k] = expand(rk[TOKS * k : TOKS * k + TOKS])

    lane_hk = iota((TOKS, HK), 1) % TOKS
    key_step = lane_hk % STEPS
    key_time = 3 * key_step + lane_hk // STEPS
    row_tok = iota((TOKS, HK), 0)
    query_time = 3 * (row_tok % STEPS) + row_tok // STEPS
    causal = key_time <= query_time
    key_step_f = key_step.astype(F32)
    sum_hd = (iota((HK, D), 0) // TOKS == iota((HK, D), 1) // HD).astype(F32).astype(BF)
    sum_hk = (iota((D, HK), 0) // HD == iota((D, HK), 1) // TOKS).astype(F32).astype(BF)

    for layer in range(LAYERS):
        gain_a = small_ref[4 * layer : 4 * layer + 1]
        gain_b = small_ref[4 * layer + 1 : 4 * layer + 2]
        bias_u = small_ref[4 * layer + 2 : 4 * layer + 3]
        bias_v = small_ref[4 * layer + 3 : 4 * layer + 4]

        @pl.loop(0, chunks)
        def _(c):
            rows = pl.ds(pl.multiple_of(c * rows_c, rows_c), rows_c)
            x = x_s[layer, pl.ds(c * CHUNK, CHUNK)].reshape(rows_c, D)
            low = (x * rms(x) * gain_a).astype(BF)
            a_s[layer, rows] = low
            q = dot_nn(low, wqkv_ref[layer, :, :256]).astype(BF).astype(F32)
            qu = (q + bias_u).astype(BF)
            qv = (q + bias_v).astype(BF)
            key = dot_nn(low, wqkv_ref[layer, :, 256:512]).astype(BF)
            val = dot_nn(low, wqkv_ref[layer, :, 512:]).astype(BF)
            att_s[layer, rows, 0:256] = qu
            att_s[layer, rows, 256:512] = qv
            att_s[layer, rows, 512:768] = key
            att_s[layer, rows, 768:1024] = val
            qv4 = qv.reshape(CHUNK, 3, STEPS, D)
            place = [
                dot_nt(qv4[:, k].reshape(CHUNK * STEPS, D), rk_s[layer, k]) for k in range(3)
            ]
            start_c = start_s[pl.ds(c * CHUNK, CHUNK)]
            for b in range(CHUNK):
                span = slice(TOKS * b, TOKS * b + TOKS)
                score = dot_nt(qu[span], expand(key[span]))
                shifted = [
                    pltpu.roll(
                        place[k][STEPS * b : STEPS * b + STEPS],
                        HK - (STEPS - 1),
                        1,
                        stride=1,
                        stride_axis=0,
                    )
                    for k in range(3)
                ]
                begin = jnp.concatenate([start_c[b]] * 3, axis=0)
                begin = jnp.concatenate([begin] * 3, axis=1)
                score = (score + jnp.concatenate(shifted, axis=0)) * SCALE
                score = jnp.where(causal & (key_step_f >= begin), score, MASKED)
                probs = jnp.exp(score - segment_max(score)).astype(BF)
                pu_s[layer, pl.ds(pl.multiple_of(c * rows_c + TOKS * b, TOKS), TOKS)] = probs
                l_s[span] = dot_nn(probs, expand(val[span]))
            recip = 1.0 / dot_nn(pu_s[layer, rows], sum_hd)
            out = l_s[...] * recip
            r_s[layer, rows] = recip
            o_s[layer, rows] = out
            mid = x + dot_nn(out.astype(BF), wsq_ref[layer, 0])
            mid_s[layer, rows] = mid
            low = (mid * rms(mid) * gain_b).astype(BF)
            b_s[layer, rows] = low
            for j in range(FF // 256):
                cols = slice(256 * j, 256 * j + 256)
                inner = dot_nn(low, wup_ref[layer, :, cols])
                square = inner * inner
                c0 = math.sqrt(2.0 / math.pi)
                tanh = jnp.tanh(c0 * inner * (1.0 + 0.044715 * square))
                half = 0.5 * (1.0 + tanh)
                hb_s[layer, rows, cols] = (inner * half).astype(BF)
                gp_s[layer, rows, cols] = (
                    half
                    + (0.5 * c0) * inner * (1.0 - tanh * tanh) * (1.0 + (3 * 0.044715) * square)
                ).astype(BF)
            nxt = mid + dot_nn(hb_s[layer, rows], wdown_ref[layer])
            x_s[layer + 1, pl.ds(c * CHUNK, CHUNK)] = nxt.reshape(CHUNK, 3, STEPS, D)

    gain_f = small_ref[4 * LAYERS : 4 * LAYERS + 1]
    xf = x_s[LAYERS, :, 1].reshape(steps_all, D)
    feat = (xf * rms(xf) * gain_f).astype(BF)
    spread_t = (iota((512, STEPS), 0) // CLASSES == iota((512, STEPS), 1)).astype(F32).astype(BF)
    class_row = iota((4, CLASSES, steps_all), 1).astype(F32)
    loss = jnp.zeros((4, steps_all), F32)
    for k in range(2):
        follow_codes = pltpu.roll(codes[k], steps_all - 1, 0).astype(BF)
        for j in range(4):
            base = 512 * k + 128 * j
            logits = dot_nt(whead_ref[base : base + 128], feat).reshape(4, CLASSES, steps_all)
            target = dot_nt(spread_t[128 * j : 128 * j + 128], follow_codes)
            hot = target.reshape(4, CLASSES, steps_all) == class_row
            top = jnp.max(logits, axis=1, keepdims=True)
            grown = jnp.exp(logits - top)
            total = jnp.sum(grown, axis=1, keepdims=True)
            picked = jnp.sum(jnp.where(hot, logits, 0.0), axis=1)
            loss = loss + valid_row * (jnp.log(total[:, 0]) + top[:, 0] - picked)
            slope = (grown * (1.0 / total) - jnp.where(hot, 1.0, 0.0)) * valid_row[None]
            slope_s[base : base + 128] = slope.reshape(128, steps_all).astype(BF)
    pick0 = (iota((8, STEPS), 1) == 0).astype(F32).astype(BF)
    pick1 = (iota((8, STEPS), 1) == 1).astype(F32).astype(BF)
    action_row = dot_nt(pick0, codes[2].astype(BF))[:1]
    discount_row = dot_nt(pick1, codes[2].astype(BF))[:1]
    reward_row = dot_nt(pick0, codes[3].astype(BF))[:1]
    logits = dot_nt(whead_ref[1024:1280], feat)
    row = iota((256, steps_all), 0)
    hot = row == (reward_row + 1.0).astype(jnp.int32)
    disc = logits[:1]
    masked = jnp.where(row == 0, -3e38, logits)
    top = jnp.max(masked, axis=0, keepdims=True)
    grown = jnp.exp(masked - top)
    total = jnp.sum(grown, axis=0, keepdims=True)
    picked = jnp.sum(jnp.where(hot, logits, 0.0), axis=0, keepdims=True)
    fade = jnp.exp(-jnp.abs(disc))
    soft = jnp.maximum(disc, 0.0) + jnp.log(1.0 + fade)
    sigm = jnp.where(disc >= 0.0, 1.0, fade) / (1.0 + fade)
    loss_row = (
        jnp.sum(loss, axis=0, keepdims=True)
        + jnp.log(total)
        + top
        - picked
        + soft
        - discount_row * disc
    )
    slope = grown * (1.0 / total) - jnp.where(hot, 1.0, 0.0)
    slope = jnp.where(row == 0, sigm - discount_row, slope)
    slope_s[1024:1280] = slope.astype(BF)
    loss_sum = jnp.sum(loss_row)
    count = jnp.sum(valid_row) * CATS + 2.0 * steps_all
    e_ref[9:10] = jnp.full((1, D), loss_sum, F32)
    e_ref[10:11] = jnp.full((1, D), count, F32)
    e_ref[11:16] = jnp.zeros((5, D), F32)

    feat_t = feat.astype(F32).T.astype(BF)
    for j in range(5):
        part = dot_nt(feat_t, slope_s[256 * j : 256 * j + 256])
        for k in range(2):
            base = 256 * (2 * j + k)
            g_ref[base : base + 256] = part[:, 128 * k : 128 * k + 128].astype(BF)
    dfeat = dot_tn(slope_s[...], whead_ref[...])
    scale_f = rms(xf)
    hat = xf * scale_f
    e_ref[8:9] = jnp.sum(dfeat * hat, axis=0, keepdims=True)
    inner = dfeat * gain_f
    dxf = scale_f * (inner - hat * jnp.mean(inner * hat, axis=-1, keepdims=True))
    dx_s[...] = jnp.zeros(dx_s.shape, F32)
    dx_s[:, 1] = dxf.reshape(seqs, STEPS, D)

    for layer in reversed(range(LAYERS)):
        gain_a = small_ref[4 * layer : 4 * layer + 1]
        gain_b = small_ref[4 * layer + 1 : 4 * layer + 2]
        e_ref[4 * layer : 4 * layer + 4] = jnp.zeros((4, D), F32)

        @pl.loop(0, chunks)
        def _(c):
            rows = pl.ds(pl.multiple_of(c * rows_c, rows_c), rows_c)
            dy = dx_s[pl.ds(c * CHUNK, CHUNK)].reshape(rows_c, D)
            dyl = dy.astype(BF)
            dyl_s[rows] = dyl
            for j in range(FF // 256):
                cols = slice(256 * j, 256 * j + 256)
                dact = dot_nt(dyl, wdown_ref[layer, cols])
                gp_s[layer, rows, cols] = (dact * gp_s[layer, rows, cols].astype(F32)).astype(BF)
            dlow = dot_nt(gp_s[layer, rows], wup_ref[layer])
            mid = mid_s[layer, rows]
            scale = rms(mid)
            hat = mid * scale
            dgain = jnp.sum(dlow * hat, axis=0, keepdims=True)
            inner = dlow * gain_b
            dmid = scale * (inner - hat * jnp.mean(inner * hat, axis=-1, keepdims=True)) + dy
            e_ref[4 * layer + 1 : 4 * layer + 2] += dgain
            dml = dmid.astype(BF)
            dml_s[rows] = dml
            do = dot_nt(dml, wsq_ref[layer, 0]).astype(BF).astype(F32)
            do = (do * r_s[layer, rows]).astype(BF)
            mass = do.astype(F32) * o_s[layer, rows]
            mass_hi = mass.astype(BF)
            mass_lo = (mass - mass_hi.astype(F32)).astype(BF)
            delta = dot_nn(mass_hi, sum_hk) + dot_nn(mass_lo, sum_hk)
            qu = att_s[layer, rows, 0:256]
            key = att_s[layer, rows, 512:768]
            val = att_s[layer, rows, 768:1024]
            draws = []
            for b in range(CHUNK):
                span = slice(TOKS * b, TOKS * b + TOKS)
                probs = pu_s[layer, pl.ds(pl.multiple_of(c * rows_c + TOKS * b, TOKS), TOKS)]
                dprob = dot_nt(do[span], expand(val[span]))
                dscore = (probs.astype(F32) * (dprob - delta[span])).astype(BF)
                wide = dscore.astype(F32)
                draws.append(
                    [unskew(wide[STEPS * k : STEPS * k + STEPS]).astype(BF) for k in range(3)]
                )
                dval = fold(dot_tn(probs, do[span])).astype(BF)
                dkey = (fold(dot_tn(dscore, qu[span])) * SCALE).astype(BF)
                l_s[span] = dot_nn(dscore, expand(key[span])) * SCALE
                out_rows = pl.ds(pl.multiple_of(c * rows_c + TOKS * b, TOKS), TOKS)
                pu_s[layer, out_rows] = jnp.concatenate(draws[b], axis=0)
                att_s[layer, out_rows, 512:768] = dkey
                att_s[layer, out_rows, 768:1024] = dval
            dqv = [
                dot_nn(
                    jnp.concatenate([draws[b][k] for b in range(CHUNK)], axis=0), rk_s[layer, k]
                ).reshape(CHUNK, 1, STEPS, D)
                for k in range(3)
            ]
            dqv = jnp.concatenate(dqv, axis=1).reshape(rows_c, D) * SCALE
            dqu = l_s[...]
            e_ref[4 * layer + 2 : 4 * layer + 3] += jnp.sum(dqu, axis=0, keepdims=True)
            e_ref[4 * layer + 3 : 4 * layer + 4] += jnp.sum(dqv, axis=0, keepdims=True)
            dq = (dqu + dqv).astype(BF)
            att_s[layer, rows, 0:256] = dq
            dlow = (
                dot_nt(dq, wqkv_ref[layer, :, :256])
                + dot_nt(att_s[layer, rows, 512:768], wqkv_ref[layer, :, 256:512])
                + dot_nt(att_s[layer, rows, 768:1024], wqkv_ref[layer, :, 512:])
            )
            x = x_s[layer, pl.ds(c * CHUNK, CHUNK)].reshape(rows_c, D)
            scale = rms(x)
            hat = x * scale
            e_ref[4 * layer : 4 * layer + 1] += jnp.sum(dlow * hat, axis=0, keepdims=True)
            inner = dlow * gain_a
            dx = scale * (inner - hat * jnp.mean(inner * hat, axis=-1, keepdims=True)) + dmid
            dx_s[pl.ds(c * CHUNK, CHUNK)] = dx.reshape(CHUNK, 3, STEPS, D)

        base = 2560 + 6656 * (LAYERS - 1 - layer)

        def put(offset, value):
            size = value.shape[0]
            for k in range(2):
                at = base + offset + k * size
                if not isinstance(at, int):
                    at = pl.multiple_of(at, 256)
                g_ref[pl.ds(at, size)] = value[:, 128 * k : 128 * k + 128].astype(BF)

        for j in range(4):
            part = dot_tn(hb_s[layer, :, 256 * j : 256 * j + 256], dyl_s[...])
            for k in range(2):
                g_ref[base + 1024 * k + 256 * j : base + 1024 * k + 256 * j + 256] = part[
                    :, 128 * k : 128 * k + 128
                ].astype(BF)
        for j in range(4):
            put(2048 + 512 * j, dot_tn(b_s[layer], gp_s[layer, :, 256 * j : 256 * j + 256]))
        put(4096, dot_tn(o_s[layer].astype(BF), dml_s[...]))
        drk = []
        draw = pu_s[layer].reshape(seqs, 3, STEPS, HK)
        qv = att_s[layer, :, 256:512].reshape(seqs, 3, STEPS, D)
        for k in range(3):
            wide = dot_tn(
                draw[:, k].reshape(steps_all, HK), qv[:, k].reshape(steps_all, D)
            )
            drk.append(fold(wide) * SCALE)
        put(4608, dot_tn(pos_ref[...], jnp.concatenate(drk, axis=0).astype(BF)))
        put(5120, dot_tn(a_s[layer], att_s[layer, :, 0:256]))
        put(5632, dot_tn(a_s[layer], att_s[layer, :, 512:768]))
        put(6144, dot_tn(a_s[layer], att_s[layer, :, 768:1024]))

    dtok = [dx_s[:, k].reshape(steps_all, D).astype(BF) for k in range(3)]
    base = 2560 + 6656 * LAYERS
    class_row = (iota((256, steps_all), 0) % CLASSES).astype(F32)
    for k in range(2):
        for j in range(2):
            wide = dot_nt(spread_t[256 * j : 256 * j + 256], codes[k].astype(BF))
            hot = (wide == class_row).astype(F32).astype(BF)
            part = dot_nn(hot, dtok[0])
            for h in range(2):
                at = base + 1280 * h + 512 * k + 256 * j
                g_ref[at : at + 256] = part[:, 128 * h : 128 * h + 128].astype(BF)
    row = iota((288, steps_all), 0)
    hot_a = (row == action_row.astype(jnp.int32)).astype(F32).astype(BF)
    hot_r = (row == (reward_row + NA).astype(jnp.int32)).astype(F32).astype(BF)
    part = dot_nn(hot_a, dtok[1]) + dot_nn(hot_r, dtok[2])
    for h in range(2):
        at = base + 1280 * h + 1024
        g_ref[at : at + 256] = part[:256, 128 * h : 128 * h + 128].astype(BF)
    e_ref[16:40] = part[256:280]


def compute(codes, seg, pos, small, table, wqkv, wsq, wup, wdown, whead_t):
    seqs = codes.shape[1]
    toks = seqs * TOKS
    f32, bf = jnp.float32, jnp.bfloat16
    vmem = pltpu.VMEM
    return pl.pallas_call(
        compute_kernel,
        out_shape=(
            jax.ShapeDtypeStruct((2560 + 6656 * LAYERS + 2560, 128), bf),
            jax.ShapeDtypeStruct((40, D), f32),
        ),
        in_specs=[pl.BlockSpec(memory_space=vmem)] * 10,
        out_specs=[pl.BlockSpec(memory_space=vmem)] * 2,
        scratch_shapes=[
            vmem((LAYERS + 1, seqs, 3, STEPS, D), f32),
            vmem((LAYERS, toks, 1024), bf),
            vmem((LAYERS, toks, HK), bf),
            vmem((LAYERS, toks, D), f32),
            vmem((LAYERS, toks, D), f32),
            vmem((LAYERS, toks, D), f32),
            vmem((LAYERS, toks, FF), bf),
            vmem((LAYERS, toks, FF), bf),
            vmem((LAYERS, toks, D), bf),
            vmem((LAYERS, toks, D), bf),
            vmem((toks, D), bf),
            vmem((toks, D), bf),
            vmem((seqs, 3, STEPS, D), f32),
            vmem((LAYERS, 3, HK, D), bf),
            vmem((seqs, STEPS, 128), f32),
            vmem((CHUNK * TOKS, D), f32),
            vmem((HCOLS, seqs * STEPS), bf),
        ],
        compiler_params=pltpu.CompilerParams(vmem_limit_bytes=VMEM_LIMIT),
        name="step",
    )(codes, seg, pos, small, table, wqkv, wsq, wup, wdown, whead_t)


def mesh_bits(streams, groups):
    bits = [("stream", 1)]
    step = 2
    rest = []
    while step < streams:
        rest.append(("stream", step))
        step *= 2
    step, others = 1, []
    while step < groups:
        others.append(("seq", step))
        step *= 2
    return bits, [others[:1], rest, others[1:]]


def bit_orders(streams, groups):
    first, parts = mesh_bits(streams, groups)
    orders = []
    for k in range(3):
        turned = parts[k:] + parts[:k]
        orders.append(first + [b for part in turned for b in part])
    return orders


def ring_plan(total, streams, groups):
    devices = streams * groups
    orders = bit_orders(streams, groups)
    unit = 16 * devices
    subs = 2 if total % (2 * 3 * unit) == 0 else 1
    rows = total // (3 * subs)
    assert rows % unit == 0
    lanes, recv = [], 0
    for sub in range(subs):
        for k in range(3):
            steps, size = [], rows
            for _ in orders[k]:
                size //= 2
                steps.append((size, recv))
                recv += size
            lanes.append(
                dict(base=(3 * sub + k) * rows, rows=rows, order=orders[k], steps=steps, sub=sub)
            )
    return lanes, recv


def place_of(bit):
    axis, step = bit
    return (lax.axis_index(axis) // step) % 2


def partner_of(bit):
    axis, step = bit
    me = lax.axis_index(axis)
    other = me + step * (1 - 2 * ((me // step) % 2))
    if axis == "stream":
        return (other, lax.axis_index("seq"))
    return (lax.axis_index("stream"), other)


class Lane:
    def __init__(self, index, spec, g_ref, out_ref, recv_ref, sems):
        self.spec, self.g, self.out = spec, g_ref, out_ref
        self.recv, self.sems, self.index = recv_ref, sems, index
        offset = spec["base"]
        self.keep, self.send = [], []
        for bit, (size, _) in zip(spec["order"], spec["steps"]):
            mine = place_of(bit)
            self.keep.append(pl.multiple_of(offset + mine * size, 16))
            self.send.append(pl.multiple_of(offset + (1 - mine) * size, 16))
            offset = self.keep[-1]

    def scatter(self, i):
        size, slot = self.spec["steps"][i]
        return pltpu.make_async_remote_copy(
            src_ref=self.g.at[pl.ds(self.send[i], size)],
            dst_ref=self.recv.at[pl.ds(slot, size)],
            send_sem=self.sems.at[0, self.index, i],
            recv_sem=self.sems.at[1, self.index, i],
            device_id=partner_of(self.spec["order"][i]),
            device_id_type=pl.DeviceIdType.MESH,
        )

    def gather(self, i):
        size, _ = self.spec["steps"][i]
        rows = pl.ds(self.keep[i], size)
        return pltpu.make_async_remote_copy(
            src_ref=self.out.at[rows],
            dst_ref=self.out.at[rows],
            send_sem=self.sems.at[2, self.index, i],
            recv_sem=self.sems.at[3, self.index, i],
            device_id=partner_of(self.spec["order"][i]),
            device_id_type=pl.DeviceIdType.MESH,
        )

    def add(self, i):
        size, slot = self.spec["steps"][i]
        target = self.out if i + 1 == len(self.keep) else self.g
        block = 96
        while size % block:
            block //= 2

        @pl.loop(0, size // block)
        def _(j):
            at = pl.ds(pl.multiple_of(self.keep[i] + j * block, 16), block)
            got = pl.ds(pl.multiple_of(slot + j * block, 16), block)
            target[at] = (self.g[at].astype(F32) + self.recv[got].astype(F32)).astype(BF)


def reduce_kernel(streams, groups, g_ref, e_ref, go_ref, eo_ref, work_s, recv_s, slot_s, got_s, sems, esems, lsem):
    lanes, _ = ring_plan(g_ref.shape[0], streams, groups)
    order = lanes[0]["order"]
    rounds = len(order)
    load = pltpu.make_async_copy(g_ref, work_s, lsem)
    load.start()
    barrier = pltpu.get_barrier_semaphore()
    for bit in order:
        pl.semaphore_signal(
            barrier, inc=1, device_id=partner_of(bit), device_id_type=pl.DeviceIdType.MESH
        )
    slot_s[0] = e_ref[...]
    pl.semaphore_wait(barrier, rounds)
    load.wait()

    def extra(i):
        return pltpu.make_async_remote_copy(
            src_ref=slot_s.at[i],
            dst_ref=got_s.at[i],
            send_sem=esems.at[0, i],
            recv_sem=esems.at[1, i],
            device_id=partner_of(order[i]),
            device_id_type=pl.DeviceIdType.MESH,
        )

    runs = [Lane(n, spec, work_s, go_ref, recv_s, sems) for n, spec in enumerate(lanes)]
    extra(0).start()
    for run in runs:
        run.scatter(0).start()
    for i in range(rounds):
        extra(i).wait()
        slot_s[i + 1] = slot_s[i] + got_s[i]
        if i + 1 < rounds:
            extra(i + 1).start()
        for run in runs:
            run.scatter(i).wait()
            run.add(i)
            if i + 1 < rounds:
                run.scatter(i + 1).start()
            else:
                run.gather(i).start()
    eo_ref[...] = slot_s[rounds]
    for i in reversed(range(rounds)):
        for run in runs:
            run.gather(i).wait()
            if i:
                run.gather(i - 1).start()


def reduce_all(grads, extra, streams, groups):
    lanes, recv = ring_plan(grads.shape[0], streams, groups)
    rounds = len(lanes[0]["order"])
    vmem = pltpu.VMEM
    return pl.pallas_call(
        lambda *refs: reduce_kernel(streams, groups, *refs),
        out_shape=(
            jax.ShapeDtypeStruct(grads.shape, grads.dtype),
            jax.ShapeDtypeStruct(extra.shape, extra.dtype),
        ),
        in_specs=[pl.BlockSpec(memory_space=pl.ANY), pl.BlockSpec(memory_space=vmem)],
        out_specs=[pl.BlockSpec(memory_space=vmem)] * 2,
        scratch_shapes=[
            vmem(grads.shape, BF),
            vmem((recv, 128), BF),
            vmem((rounds + 1,) + extra.shape, F32),
            vmem((rounds,) + extra.shape, F32),
            pltpu.SemaphoreType.DMA((4, len(lanes), rounds)),
            pltpu.SemaphoreType.DMA((2, rounds)),
            pltpu.SemaphoreType.DMA,
        ],
        compiler_params=pltpu.CompilerParams(
            collective_id=0, has_side_effects=True, vmem_limit_bytes=24 * 1000 * 1000
        ),
        name="reduce",
    )(grads, extra)


def update_pieces():
    pieces = []
    for k in range(LAYERS):
        layer = LAYERS - 1 - k
        base = 2560 + 6656 * k
        for half in range(2):
            r = 512 * half
            pieces.append(
                (4, (layer,), r, 512, [(base + 1024 * j + r, 128 * j) for j in range(2)])
            )
        pieces.append((3, (layer,), 0, 256, [(base + 2048 + 256 * j, 128 * j) for j in range(8)]))
        pieces.append((2, (layer, 0), 0, 256, [(base + 4096 + 256 * j, 128 * j) for j in range(2)]))
        pieces.append((2, (layer, 1), 0, 256, [(base + 4608 + 256 * j, 128 * j) for j in range(2)]))
        pieces.append((1, (layer,), 0, 256, [(base + 5120 + 256 * j, 128 * j) for j in range(6)]))
    pieces.append((6, (), 0, 256, [(256 * j, 128 * j) for j in range(10)]))
    base = 2560 + 6656 * LAYERS
    pieces.append((0, (), 0, 1280, [(base + 1280 * j, 128 * j) for j in range(2)]))
    return pieces


def update_kernel(clip_value, step_rate, *refs):
    g_ref, e_ref = refs[:2]
    ins = refs[2:23]
    stat_ref = refs[23]
    outs = refs[24:45]
    bufs = refs[45:66]
    isem, osem = refs[66:]
    pieces = update_pieces()
    table_rows = ins[0].shape[0]
    tail = table_rows - 1280

    def view(ref, piece):
        array, lead, first, rows, _ = piece
        if lead:
            ref = ref.at[lead]
        if ref.shape[0] == rows:
            return ref
        return ref.at[pl.ds(first, rows)]

    def transfer(kind, n, k, piece):
        src, dst = (ins, bufs) if kind == 0 else (bufs, outs)
        array = piece[0]
        sem = (isem, osem)[kind].at[k, n]
        return pltpu.make_async_copy(
            view(src[7 * k + array], piece), view(dst[7 * k + array], piece), sem
        )

    specials = [(0, (), 1280, tail, None), (5, (), 0, ins[5].shape[0], None)]
    order = specials + pieces
    for n, piece in enumerate(order):
        for k in range(3):
            transfer(0, n, k, piece).start()

    block = 128
    count = g_ref.shape[0] // block

    def gather(j, total):
        v = g_ref[pl.ds(pl.multiple_of(j * block, block), block)].astype(F32)
        return total + jnp.sum((v * v).reshape(block // 8, 8, 128), axis=0)

    total = lax.fori_loop(0, count, gather, jnp.zeros((8, 128), F32))
    rest = jnp.sum(e_ref[0:9] * e_ref[0:9]) + jnp.sum(e_ref[16:40] * e_ref[16:40])
    loss = jnp.max(e_ref[9:10])
    terms = jnp.max(e_ref[10:11])
    inverse = 1.0 / jnp.full((8, 128), terms, F32)
    norm = jnp.sqrt(jnp.full((8, 128), jnp.sum(total) + rest, F32)) * inverse
    factor = inverse * clip_value / jnp.maximum(norm, clip_value)
    stat_ref[0:8] = jnp.full((8, 128), loss, F32)
    stat_ref[8:16] = jnp.full((8, 128), terms, F32)
    stat_ref[16:24] = norm
    factor = factor[:1]

    def advance(views, rows, cols, gradient, scale):
        w, m, e = [v[rows, cols] for v in views]
        clipped = gradient * scale
        moment = MOMENTUM_RATE * m + clipped
        weight = w - step_rate * (clipped + MOMENTUM_RATE * moment)
        views[0][rows, cols] = weight
        views[1][rows, cols] = moment
        views[2][rows, cols] = AVERAGE_RATE * e + (1.0 - AVERAGE_RATE) * weight

    for n, piece in enumerate(order):
        array, lead, first, rows, blocks = piece
        for k in range(3):
            transfer(0, n, k, piece).wait()
        views = [bufs[7 * k + array].at[lead] if lead else bufs[7 * k + array] for k in range(3)]
        if blocks is None:
            at = 16 if array == 0 else 0
            wide = jnp.concatenate([factor, factor], axis=1)
            advance(
                views, slice(first, first + rows), slice(0, D), e_ref[at : at + rows], wide
            )
        else:
            step = 64

            @pl.loop(0, rows // step)
            def _(j):
                for source, column in blocks:
                    g = g_ref[pl.ds(pl.multiple_of(source + j * step, step), step)].astype(F32)
                    at = pl.ds(pl.multiple_of(first + j * step, step), step)
                    advance(views, at, slice(column, column + 128), g, factor)

        for k in range(3):
            transfer(1, n, k, piece).start()
    for n, piece in enumerate(order):
        for k in range(3):
            transfer(1, n, k, piece).wait()


def update_all(grads, extra, arrays, clip_value, step_rate):
    vmem = pltpu.VMEM
    count = len(update_pieces()) + 2
    hbm = pl.BlockSpec(memory_space=pl.ANY)
    results = pl.pallas_call(
        lambda *refs: update_kernel(clip_value, step_rate, *refs),
        out_shape=[jax.ShapeDtypeStruct((24, 128), F32)]
        + [jax.ShapeDtypeStruct(a.shape, F32) for a in arrays],
        in_specs=[pl.BlockSpec(memory_space=vmem)] * 2 + [hbm] * 21,
        out_specs=[pl.BlockSpec(memory_space=vmem)] + [hbm] * 21,
        scratch_shapes=[vmem(a.shape, F32) for a in arrays]
        + [pltpu.SemaphoreType.DMA((3, count)), pltpu.SemaphoreType.DMA((3, count))],
        compiler_params=pltpu.CompilerParams(vmem_limit_bytes=44 * 1000 * 1000),
        name="update",
    )(grads, extra, *arrays)
    return results[0], results[1:]


def on_device(step_codes, segments, *arrays):
    stream_id = lax.axis_index("stream")
    streams = lax.axis_size("stream")
    groups = lax.axis_size("seq")
    group_seqs = step_codes.shape[0]
    own = group_seqs // streams
    codes = lax.all_to_all(
        step_codes.reshape(streams, own, STEPS, -1), "stream", split_axis=0, concat_axis=0
    )
    seg = lax.dynamic_slice_in_dim(segments, stream_id * own, own, 0)
    table, qkv, square, up, down, small, head = arrays[:7]
    table_low = jnp.pad(table.astype(BF), ((0, TROWS - table.shape[0]), (0, 0)))
    pos = jnp.asarray(position_rows()).astype(BF)
    grads, extra = compute(
        codes,
        seg,
        pos,
        small,
        table_low,
        qkv.astype(BF),
        square.astype(BF),
        up.astype(BF),
        down.astype(BF),
        head.astype(BF).T,
    )
    grads, extra = reduce_all(grads, extra, streams, groups)
    params_total = sum(w.size for w in arrays[:7])
    clip_value = CLIP_SCALE * (group_seqs * groups * STEPS) ** (-0.5)
    step_rate = STEP_SCALE * params_total**0.5 / clip_value
    stats, updated = update_all(grads, extra, arrays, clip_value, step_rate)
    return (stats[0, 0], stats[8, 0], stats[16, 0], *updated)


def solution(mesh):
    return jax.shard_map(
        on_device,
        mesh=mesh,
        in_specs=(P("seq", None, "stream"), P("seq", None)) + (P(),) * 21,
        out_specs=(P(),) * 24,
        check_vma=False,
    )
```

```python
import math

import jax
import jax.numpy as jnp
import numpy as np
from jax import lax
from jax.experimental import pallas as pl
from jax.experimental.pallas import tpu as pltpu
from jax.sharding import PartitionSpec as P

D = 256
HEADS = 8
HD = 32
FF = 1024
CATS = 32
CLASSES = 32
NA = 18
STEPS = 16
TOKS = 48
HK = HEADS * TOKS
LAYERS = 2
HCOLS = 1280
TROWS = 1408
CHUNK = 8
EPSILON = 1e-06
MOMENTUM_RATE = 0.9
AVERAGE_RATE = 0.7
CLIP_SCALE = 0.2
STEP_SCALE = 0.03
MASKED = -1e30
POSITION_SCALE = 0.5
SCALE = HD ** (-0.5)
BF = jnp.bfloat16
F32 = jnp.float32
VMEM_LIMIT = 63 * 1000 * 1000


def dot_nn(a, b):
    return lax.dot_general(a, b, (((1,), (0,)), ((), ())), preferred_element_type=F32)


def dot_nt(a, b):
    return lax.dot_general(a, b, (((1,), (1,)), ((), ())), preferred_element_type=F32)


def dot_tn(a, b):
    return lax.dot_general(a, b, (((0,), (0,)), ((), ())), preferred_element_type=F32)


def iota(shape, dim):
    return lax.broadcasted_iota(jnp.int32, shape, dim)


def position_rows():
    distance = np.arange(TOKS, dtype=np.float32)[:, None]
    rates = np.exp(np.arange(D // 2, dtype=np.float32) * np.float32(-2.0 * math.log(10000.0) / D))
    angle = (distance * rates[None, :].astype(np.float32)).astype(np.float32)
    table = np.float32(POSITION_SCALE) * np.concatenate([np.sin(angle), np.cos(angle)], axis=1)
    rows = np.zeros((3, TOKS, D), np.float32)
    for i in range(3):
        for j in range(3):
            for e in range(STEPS):
                d = 3 * (STEPS - 1 - e) + i - j
                if d >= 0:
                    rows[i, j * STEPS + e] = table[d]
    return rows.reshape(3 * TOKS, D)


def rms(values):
    return lax.rsqrt(jnp.mean(values * values, axis=-1, keepdims=True) + EPSILON)


def head_mask(h, rows):
    lane = iota((rows, 128), 1)
    low = (h % 4) * HD
    return ((lane >= low) & (lane < low + HD)).astype(F32).astype(BF)


def expand(rows):
    zero = jnp.zeros((TOKS, 128), BF)
    parts = []
    for h in range(HEADS):
        half = rows[:, 128 * (h // 4) : 128 * (h // 4) + 128] * head_mask(h, TOKS)
        parts.append(jnp.concatenate([half, zero] if h < 4 else [zero, half], axis=1))
    return jnp.concatenate(parts, axis=0)


def fold(values):
    lane = iota((TOKS, 128), 1)
    halves = []
    for g in range(2):
        total = None
        for h in range(4):
            part = values[(4 * g + h) * TOKS : (4 * g + h + 1) * TOKS, 128 * g : 128 * g + 128]
            total = part if total is None else jnp.where(lane >= h * HD, part, total)
        halves.append(total)
    return jnp.concatenate(halves, axis=1)


def spans(tile):
    found = []
    for h in range(HEADS):
        low, high = max(TOKS * h - 128 * tile, 0), min(TOKS * (h + 1) - 128 * tile, 128)
        if low < high:
            found.append((h, low, high))
    return found


def segment_max(scores):
    rows = scores.shape[0]
    lane = iota((rows, 128), 1)
    tiles = [scores[:, 128 * t : 128 * t + 128] for t in range(3)]
    best = {}
    for t in range(3):
        for h, low, high in spans(t):
            part = jnp.where((lane >= low) & (lane < high), tiles[t], -3e38)
            best[h] = part if h not in best else jnp.maximum(best[h], part)
    best = {h: jnp.max(v, axis=1, keepdims=True) for h, v in best.items()}
    outs = []
    for t in range(3):
        total = None
        for h, low, high in spans(t):
            wide = jnp.broadcast_to(best[h], (rows, 128))
            total = wide if total is None else jnp.where(lane >= low, wide, total)
        outs.append(total)
    return jnp.concatenate(outs, axis=1)


def unskew(values):
    row = iota((STEPS, HK), 0)
    values = jnp.concatenate(
        [pltpu.roll(values[:8], 15, 1), pltpu.roll(values[8:], 7, 1)], axis=0
    )
    for bit in (1, 2, 4):
        values = jnp.where((row & bit) > 0, pltpu.roll(values, HK - bit, 1), values)
    return values


SECTIONS = (2560, 4096, 2560, 4096, 5120)


def bit_orders(streams, groups):
    first, rest, others = [("stream", 1)], [], []
    step = 2
    while step < streams:
        rest.append(("stream", step))
        step *= 2
    step = 1
    while step < groups:
        others.append(("seq", step))
        step *= 2
    near, far = others[:1], others[1:]
    return [first + near + rest + far, first + rest + near + far, first + far + near + rest]


def exchange_plan(streams, groups):
    unit = 16 * streams * groups
    sections = SECTIONS
    if any(s % unit or s < 3 * unit for s in sections):
        sections = (sum(SECTIONS),)
    orders = bit_orders(streams, groups)
    plan, base, recv, own = [], 0, 0, 0
    for rows in sections:
        units = rows // unit
        last = max(1, round(0.222 * units))
        parts = [(units - last + 1) // 2, (units - last) // 2, last]
        lanes = []
        for part, order in zip(parts, orders):
            size, steps = part * unit, []
            for _ in order:
                size //= 2
                steps.append((size, recv))
                recv += size
            lanes.append(dict(base=base, order=order, steps=steps, own=own))
            own += size
            base += part * unit
        plan.append(lanes)
    assert base == sum(SECTIONS)
    return plan, recv, own


def place_of(bit):
    axis, step = bit
    return (lax.axis_index(axis) // step) % 2


def partner_of(bit):
    axis, step = bit
    me = lax.axis_index(axis)
    other = me + step * (1 - 2 * ((me // step) % 2))
    if axis == "stream":
        return (other, lax.axis_index("seq"))
    return (lax.axis_index("stream"), other)


class Lane:
    def __init__(self, spec, refs, sems, own_sem):
        self.spec, self.sems, self.own_sem = spec, sems, own_sem
        self.g, self.out, self.recv, self.own = refs
        offset = spec["base"]
        self.keep, self.send = [], []
        for bit, (size, _) in zip(spec["order"], spec["steps"]):
            mine = place_of(bit)
            self.keep.append(pl.multiple_of(offset + mine * size, 16))
            self.send.append(pl.multiple_of(offset + (1 - mine) * size, 16))
            offset = self.keep[-1]

    def remote(self, kind, i, src, dst):
        return pltpu.make_async_remote_copy(
            src_ref=src,
            dst_ref=dst,
            send_sem=self.sems.at[2 * kind, i],
            recv_sem=self.sems.at[2 * kind + 1, i],
            device_id=partner_of(self.spec["order"][i]),
            device_id_type=pl.DeviceIdType.MESH,
        )

    def scatter(self, i):
        size, slot = self.spec["steps"][i]
        return self.remote(
            0, i, self.g.at[pl.ds(self.send[i], size)], self.recv.at[pl.ds(slot, size)]
        )

    def mine(self):
        return self.own.at[pl.ds(self.spec["own"], self.spec["steps"][-1][0])]

    def keep_copy(self):
        rows = pl.ds(self.keep[-1], self.spec["steps"][-1][0])
        return pltpu.make_async_copy(self.mine(), self.out.at[rows], self.own_sem)

    def gather(self, i):
        size, _ = self.spec["steps"][i]
        rows = pl.ds(self.keep[i], size)
        last = i + 1 == len(self.keep)
        return self.remote(1, i, self.mine() if last else self.out.at[rows], self.out.at[rows])

    def add(self, i):
        size, slot = self.spec["steps"][i]
        last = i + 1 == len(self.keep)
        block = 128
        while size % block:
            block //= 2

        @pl.loop(0, size // block)
        def _(j):
            at = pl.ds(pl.multiple_of(self.keep[i] + j * block, 16), block)
            got = pl.ds(pl.multiple_of(slot + j * block, 16), block)
            value = (self.g[at].astype(F32) + self.recv[got].astype(F32)).astype(BF)
            if last:
                own = pl.multiple_of(self.spec["own"] + j * block, 16)
                self.own[pl.ds(own, block)] = value
            else:
                self.g[at] = value


class Exchange:
    def __init__(self, streams, groups, g_ref, out_ref, recv_ref, own_ref, sems, own_sems):
        plan, _, _ = exchange_plan(streams, groups)
        refs = (g_ref, out_ref, recv_ref, own_ref)
        self.sections = [
            [
                Lane(spec, refs, sems.at[n, k], own_sems.at[n, k])
                for k, spec in enumerate(lanes)
            ]
            for n, lanes in enumerate(plan)
        ]
        self.order = plan[0][0]["order"]
        self.rounds = len(self.order)
        self.active = []

    def open(self, n):
        if len(self.sections) > 1:
            for lane in self.sections[n]:
                lane.scatter(0).start()
            self.active.append([n, 0])

    def advance(self, n, stage):
        rounds = self.rounds
        for lane in self.sections[n]:
            if stage < rounds:
                lane.scatter(stage).wait()
                lane.add(stage)
                if stage + 1 < rounds:
                    lane.scatter(stage + 1).start()
                else:
                    lane.keep_copy().start()
                    lane.gather(stage).start()
            else:
                i = 2 * rounds - 1 - stage
                lane.gather(i).wait()
                if i + 1 == rounds:
                    lane.keep_copy().wait()
                if i:
                    lane.gather(i - 1).start()

    def tick(self):
        for item in self.active:
            self.advance(*item)
            item[1] += 1
        self.active = [item for item in self.active if item[1] < 2 * self.rounds]

    def ticks(self, c, count):
        for k in range(count):
            if self.active:
                pl.when(c == k)(self.tick)

    def finish(self, slot_ref, got_ref, sems, total_ref):
        last = len(self.sections) - 1

        def extra(i):
            return pltpu.make_async_remote_copy(
                src_ref=slot_ref.at[i],
                dst_ref=got_ref.at[i],
                send_sem=sems.at[0, i],
                recv_sem=sems.at[1, i],
                device_id=partner_of(self.order[i]),
                device_id_type=pl.DeviceIdType.MESH,
            )

        for lane in self.sections[last]:
            lane.scatter(0).start()
        extra(0).start()
        self.active.append([last, 0])
        i = 0
        while self.active or i < self.rounds:
            if i < self.rounds:
                extra(i).wait()
                slot_ref[i + 1] = slot_ref[i] + got_ref[i]
                if i + 1 < self.rounds:
                    extra(i + 1).start()
            self.tick()
            i += 1
        total_ref[...] = slot_ref[self.rounds]

def step_kernel(
    streams,
    groups,
    codes_hbm,
    seg_ref,
    pos_ref,
    small_ref,
    table_hbm,
    qkv_hbm,
    square_hbm,
    up_hbm,
    down_hbm,
    head_hbm,
    out_hbm,
    total_ref,
    x_s,
    att_s,
    pu_s,
    o_s,
    mid_s,
    hb_s,
    gp_s,
    a_s,
    b_s,
    dyl_s,
    dml_s,
    rk_s,
    start_s,
    l_s,
    slope_s,
    table_s,
    wqkv_s,
    wsq_s,
    wup_s,
    wdown_s,
    whead_s,
    wheadt_s,
    stage_s,
    raw_s,
    send_s,
    codes_s,
    g_s,
    recv_s,
    own_s,
    slot_s,
    got_s,
    load_sems,
    code_sems,
    sems,
    own_sems,
    extra_sems,
):
    toks = x_s.shape[1]
    seqs = toks // TOKS
    steps_all = seqs * STEPS
    chunks = seqs // CHUNK
    rows_c = CHUNK * TOKS
    me = lax.axis_index("stream")
    table_rows = table_hbm.shape[0]

    raw_load = pltpu.make_async_copy(codes_hbm, raw_s, load_sems.at[0])
    raw_load.start()
    loads = [(pltpu.make_async_copy(table_hbm, stage_s, load_sems.at[1]), None, None)]

    def load(src, place, targets):
        copy = pltpu.make_async_copy(src, place, load_sems.at[len(loads) + 1])
        loads.append((copy, place, targets))

    for layer in range(LAYERS):
        places = [o_s.at[layer, pl.ds(256 * j, 256)] for j in range(6)]
        places += [mid_s.at[layer, pl.ds(256 * j, 256)] for j in range(6)]
        places += [x_s.at[1, pl.ds(256 * layer, 256)]]
        places = iter(places)
        for j in range(3):
            cols = pl.ds(256 * j, 256)
            load(qkv_hbm.at[layer, :, cols], next(places), [(wqkv_s.at[layer, :, cols], False)])
        for j in range(2):
            load(square_hbm.at[layer, j], next(places), [(wsq_s.at[layer, j], False)])
        for j in range(4):
            cols = pl.ds(256 * j, 256)
            load(up_hbm.at[layer, :, cols], next(places), [(wup_s.at[layer, :, cols], False)])
        for j in range(4):
            cols = pl.ds(256 * j, 256)
            load(down_hbm.at[layer, cols], next(places), [(wdown_s.at[layer, cols], False)])
    for j in range(HCOLS // 256):
        cols = pl.ds(256 * j, 256)
        load(
            head_hbm.at[:, cols],
            x_s.at[2, cols],
            [(whead_s.at[:, cols], False), (wheadt_s.at[cols], True)],
        )
    for copy, _, _ in loads:
        copy.start()

    comm = Exchange(streams, groups, g_s, out_hbm, recv_s, own_s, sems, own_sems)
    barrier = pltpu.get_barrier_semaphore()
    peers = [((me + j) % streams, lax.axis_index("seq")) for j in range(1, streams)]
    greeted = peers + [partner_of(bit) for bit in comm.order if bit[0] == "seq"]
    for peer in greeted:
        pl.semaphore_signal(
            barrier, inc=1, device_id=peer, device_id_type=pl.DeviceIdType.MESH
        )

    raw_load.wait()
    eye = (iota((STEPS, STEPS), 0) == iota((STEPS, STEPS), 1)).astype(F32).astype(BF)
    for k in range(streams):
        part = raw_s[seqs * k : seqs * k + seqs].reshape(steps_all, STEPS).astype(F32).astype(BF)
        send_s[k] = dot_nt(eye, part).astype(BF)
    pl.semaphore_wait(barrier, len(greeted))
    sends = []
    for j, peer in enumerate(peers):
        sends.append(
            pltpu.make_async_remote_copy(
                src_ref=send_s.at[peer[0]],
                dst_ref=codes_s.at[me],
                send_sem=code_sems.at[0, j],
                recv_sem=code_sems.at[1, j],
                device_id=peer,
                device_id_type=pl.DeviceIdType.MESH,
            )
        )
        sends[-1].start()
    codes_s[me] = send_s[me]

    seg = seg_ref[pl.ds(pl.multiple_of(me * seqs, 8), seqs)].astype(F32)
    seg3 = jnp.broadcast_to(seg[:, None, :], (seqs, STEPS, STEPS))
    i1, i2 = iota((seqs, STEPS, STEPS), 1), iota((seqs, STEPS, STEPS), 2)
    seg_col = jnp.sum(jnp.where(i1 == i2, seg3, 0.0), axis=2, keepdims=True)
    start = jnp.sum(jnp.where(seg3 < seg_col, 1.0, 0.0), axis=2, keepdims=True)
    start_s[...] = jnp.broadcast_to(start, (seqs, STEPS, 128))
    follow = jnp.where((i2 == i1 + 1) & (seg3 == seg_col), 1.0, 0.0).reshape(steps_all, STEPS)
    valid_row = dot_nt(jnp.ones((STEPS, STEPS), BF), follow.astype(BF))[:1]

    loads[0][0].wait()
    whole = table_rows // 16 * 16
    table_s[0:whole] = stage_s[0:whole].astype(BF)
    rest = stage_s[whole:table_rows]
    table_s[whole : whole + 16] = jnp.concatenate(
        [rest, jnp.zeros((16 - (table_rows - whole), D), F32)], axis=0
    ).astype(BF)
    table_s[whole + 16 :] = jnp.zeros((TROWS - whole - 16, D), BF)
    for copy, place, targets in loads[1:]:
        copy.wait()
        for target, turned in targets:
            target[...] = (place[...].T if turned else place[...]).astype(BF)
    for copy in sends:
        copy.wait()
    codes = [codes_s[k] for k in range(4)]

    spread = (iota((STEPS, 512), 1) // CLASSES == iota((STEPS, 512), 0)).astype(F32).astype(BF)
    first = (iota((STEPS, 384), 0) == 0).astype(F32).astype(BF)
    class_lane = (iota((128, 512), 1) % CLASSES).astype(F32)
    lane = iota((128, 384), 1).astype(F32)
    for c in range(steps_all // 128):
        cols = slice(128 * c, 128 * c + 128)
        halves = []
        for k in range(2):
            hot = (dot_tn(codes[k][:, cols], spread) == class_lane).astype(F32).astype(BF)
            piece = dot_nn(hot, table_s[512 * k : 512 * k + 512]).astype(BF).astype(F32)
            halves.append(piece)
        hot = (dot_tn(codes[2][:, cols], first[:, :128]) == lane[:, :128]).astype(F32).astype(BF)
        action = dot_nn(hot, table_s[1024:1152]).astype(BF).astype(F32)
        hot = (dot_tn(codes[3][:, cols], first) + NA == lane).astype(F32).astype(BF)
        reward = dot_nn(hot, table_s[1024:1408]).astype(BF).astype(F32)
        pieces = [p.reshape(8, 1, STEPS, D) for p in (halves[0] + halves[1], action, reward)]
        x_s[0, 384 * c : 384 * c + 384] = jnp.concatenate(pieces, axis=1).reshape(384, D)
    for layer in range(LAYERS):
        rk = dot_nn(pos_ref[...], wsq_s[layer, 1]).astype(BF)
        for k in range(3):
            rk_s[layer, k] = expand(rk[TOKS * k : TOKS * k + TOKS])

    lane_hk = iota((TOKS, HK), 1) % TOKS
    key_step = lane_hk % STEPS
    key_time = 3 * key_step + lane_hk // STEPS
    row_tok = iota((TOKS, HK), 0)
    query_time = 3 * (row_tok % STEPS) + row_tok // STEPS
    causal = key_time <= query_time
    key_step_f = key_step.astype(F32)
    sum_hd = (iota((HK, D), 0) // TOKS == iota((HK, D), 1) // HD).astype(F32).astype(BF)
    sum_hk = (iota((D, HK), 0) // HD == iota((D, HK), 1) // TOKS).astype(F32).astype(BF)

    for layer in range(LAYERS):
        gain_a = small_ref[4 * layer : 4 * layer + 1]
        gain_b = small_ref[4 * layer + 1 : 4 * layer + 2]
        bias_u = small_ref[4 * layer + 2 : 4 * layer + 3]
        bias_v = small_ref[4 * layer + 3 : 4 * layer + 4]

        @pl.loop(0, chunks)
        def _(c):
            rows = pl.ds(pl.multiple_of(c * rows_c, rows_c), rows_c)
            x = x_s[layer, rows]
            low = (x * rms(x) * gain_a).astype(BF)
            a_s[layer, rows] = low
            q = dot_nn(low, wqkv_s[layer, :, :256]).astype(BF).astype(F32)
            qu = (q + bias_u).astype(BF)
            qv = (q + bias_v).astype(BF)
            key = dot_nn(low, wqkv_s[layer, :, 256:512]).astype(BF)
            val = dot_nn(low, wqkv_s[layer, :, 512:]).astype(BF)
            att_s[layer, rows, 0:256] = qu
            att_s[layer, rows, 256:512] = qv
            att_s[layer, rows, 512:768] = key
            att_s[layer, rows, 768:1024] = val
            qv4 = qv.reshape(CHUNK, 3, STEPS, D)
            place = [
                dot_nt(qv4[:, k].reshape(CHUNK * STEPS, D), rk_s[layer, k]) for k in range(3)
            ]
            start_c = start_s[pl.ds(c * CHUNK, CHUNK)]
            for b in range(CHUNK):
                span = slice(TOKS * b, TOKS * b + TOKS)
                score = dot_nt(qu[span], expand(key[span]))
                shifted = [
                    pltpu.roll(
                        place[k][STEPS * b : STEPS * b + STEPS],
                        HK - (STEPS - 1),
                        1,
                        stride=1,
                        stride_axis=0,
                    )
                    for k in range(3)
                ]
                begin = jnp.concatenate([start_c[b]] * 3, axis=0)
                begin = jnp.concatenate([begin] * 3, axis=1)
                score = (score + jnp.concatenate(shifted, axis=0)) * SCALE
                score = jnp.where(causal & (key_step_f >= begin), score, MASKED)
                probs = jnp.exp(score - segment_max(score)).astype(BF)
                pu_s[layer, pl.ds(pl.multiple_of(c * rows_c + TOKS * b, TOKS), TOKS)] = probs
                l_s[span] = dot_nn(probs, expand(val[span]))
            recip = 1.0 / dot_nn(pu_s[layer, rows], sum_hd)
            out = l_s[...] * recip
            o_s[layer, rows] = out
            mid = x + dot_nn(out.astype(BF), wsq_s[layer, 0])
            mid_s[layer, rows] = mid
            low = (mid * rms(mid) * gain_b).astype(BF)
            b_s[layer, rows] = low
            for j in range(FF // 256):
                cols = slice(256 * j, 256 * j + 256)
                inner = dot_nn(low, wup_s[layer, :, cols])
                square = inner * inner
                c0 = math.sqrt(2.0 / math.pi)
                tanh = jnp.tanh(c0 * inner * (1.0 + 0.044715 * square))
                half = 0.5 * (1.0 + tanh)
                hb_s[layer, rows, cols] = (inner * half).astype(BF)
                gp_s[layer, rows, cols] = (
                    half
                    + (0.5 * c0) * inner * (1.0 - tanh * tanh) * (1.0 + (3 * 0.044715) * square)
                ).astype(BF)
            nxt = mid + dot_nn(hb_s[layer, rows], wdown_s[layer])
            x_s[layer + 1, rows] = nxt

    gain_f = small_ref[4 * LAYERS : 4 * LAYERS + 1]
    xf = x_s[LAYERS].reshape(seqs, 3, STEPS, D)[:, 1].reshape(steps_all, D)
    feat = (xf * rms(xf) * gain_f).astype(BF)
    spread_t = (iota((512, STEPS), 0) // CLASSES == iota((512, STEPS), 1)).astype(F32).astype(BF)
    class_row = iota((4, CLASSES, steps_all), 1).astype(F32)
    loss = jnp.zeros((4, steps_all), F32)
    for k in range(2):
        follow_codes = pltpu.roll(codes[k].astype(F32), steps_all - 1, 1).astype(BF)
        for j in range(4):
            base = 512 * k + 128 * j
            logits = dot_nt(wheadt_s[base : base + 128], feat).reshape(4, CLASSES, steps_all)
            target = dot_nn(spread_t[128 * j : 128 * j + 128], follow_codes)
            hot = target.reshape(4, CLASSES, steps_all) == class_row
            top = jnp.max(logits, axis=1, keepdims=True)
            grown = jnp.exp(logits - top)
            total = jnp.sum(grown, axis=1, keepdims=True)
            picked = jnp.sum(jnp.where(hot, logits, 0.0), axis=1)
            loss = loss + valid_row * (jnp.log(total[:, 0]) + top[:, 0] - picked)
            slope = (grown * (1.0 / total) - jnp.where(hot, 1.0, 0.0)) * valid_row[None]
            slope_s[base : base + 128] = slope.reshape(128, steps_all).astype(BF)
    action_row = codes[2][0:1].astype(F32)
    discount_row = codes[2][1:2].astype(F32)
    reward_row = codes[3][0:1].astype(F32)
    logits = dot_nt(wheadt_s[1024:1280], feat)
    row = iota((256, steps_all), 0)
    hot = row == (reward_row + 1.0).astype(jnp.int32)
    disc = logits[:1]
    masked = jnp.where(row == 0, -3e38, logits)
    top = jnp.max(masked, axis=0, keepdims=True)
    grown = jnp.exp(masked - top)
    total = jnp.sum(grown, axis=0, keepdims=True)
    picked = jnp.sum(jnp.where(hot, logits, 0.0), axis=0, keepdims=True)
    fade = jnp.exp(-jnp.abs(disc))
    soft = jnp.maximum(disc, 0.0) + jnp.log(1.0 + fade)
    sigm = jnp.where(disc >= 0.0, 1.0, fade) / (1.0 + fade)
    loss_row = (
        jnp.sum(loss, axis=0, keepdims=True)
        + jnp.log(total)
        + top
        - picked
        + soft
        - discount_row * disc
    )
    slope = grown * (1.0 / total) - jnp.where(hot, 1.0, 0.0)
    slope = jnp.where(row == 0, sigm - discount_row, slope)
    slope_s[1024:1280] = slope.astype(BF)
    loss_sum = jnp.sum(loss_row)
    count = jnp.sum(valid_row) * CATS + 2.0 * steps_all
    slot_s[0, 9:10] = jnp.full((1, D), loss_sum, F32)
    slot_s[0, 10:11] = jnp.full((1, D), count, F32)
    slot_s[0, 11:16] = jnp.zeros((5, D), F32)

    feat_t = feat.astype(F32).T.astype(BF)
    for j in range(5):
        part = dot_nt(feat_t, slope_s[256 * j : 256 * j + 256])
        for k in range(2):
            base = 256 * (2 * j + k)
            g_s[base : base + 256] = part[:, 128 * k : 128 * k + 128].astype(BF)
    comm.open(0)
    dfeat = dot_nn(whead_s[...], slope_s[...]).T
    scale_f = rms(xf)
    hat = xf * scale_f
    slot_s[0, 8:9] = jnp.sum(dfeat * hat, axis=0, keepdims=True)
    inner = dfeat * gain_f
    dxf = scale_f * (inner - hat * jnp.mean(inner * hat, axis=-1, keepdims=True))
    gap = jnp.zeros((seqs, 1, STEPS, D), F32)
    x_s[LAYERS] = jnp.concatenate([gap, dxf.reshape(seqs, 1, STEPS, D), gap], axis=1).reshape(
        toks, D
    )

    for layer in reversed(range(LAYERS)):
        gain_a = small_ref[4 * layer : 4 * layer + 1]
        gain_b = small_ref[4 * layer + 1 : 4 * layer + 2]
        slot_s[0, 4 * layer : 4 * layer + 4] = jnp.zeros((4, D), F32)

        @pl.loop(0, chunks)
        def _(c):
            rows = pl.ds(pl.multiple_of(c * rows_c, rows_c), rows_c)
            comm.ticks(c, chunks)
            dy = x_s[LAYERS, rows]
            dyl = dy.astype(BF)
            dyl_s[rows] = dyl
            for j in range(FF // 256):
                cols = slice(256 * j, 256 * j + 256)
                dact = dot_nt(dyl, wdown_s[layer, cols])
                gp_s[layer, rows, cols] = (dact * gp_s[layer, rows, cols].astype(F32)).astype(BF)
            dlow = dot_nt(gp_s[layer, rows], wup_s[layer])
            mid = mid_s[layer, rows]
            scale = rms(mid)
            hat = mid * scale
            dgain = jnp.sum(dlow * hat, axis=0, keepdims=True)
            inner = dlow * gain_b
            dmid = scale * (inner - hat * jnp.mean(inner * hat, axis=-1, keepdims=True)) + dy
            slot_s[0, 4 * layer + 1 : 4 * layer + 2] += dgain
            mid_s[layer, rows] = dmid
            dml_s[rows] = dmid.astype(BF)

        base = 2560 + 6656 * (LAYERS - 1 - layer)

        def put(offset, value, base=base):
            size = value.shape[0]
            for k in range(2):
                at = base + offset + k * size
                g_s[at : at + size] = value[:, 128 * k : 128 * k + 128].astype(BF)

        for j in range(4):
            part = dot_tn(hb_s[layer, :, 256 * j : 256 * j + 256], dyl_s[...])
            for k in range(2):
                at = base + 1024 * k + 256 * j
                g_s[at : at + 256] = part[:, 128 * k : 128 * k + 128].astype(BF)
        comm.tick()
        for j in range(4):
            put(2048 + 512 * j, dot_tn(b_s[layer], gp_s[layer, :, 256 * j : 256 * j + 256]))
        comm.open(1 + 2 * (LAYERS - 1 - layer))

        @pl.loop(0, chunks)
        def _(c):
            rows = pl.ds(pl.multiple_of(c * rows_c, rows_c), rows_c)
            comm.ticks(c, chunks)
            dmid = mid_s[layer, rows]
            dml = dml_s[rows]
            recip = 1.0 / dot_nn(pu_s[layer, rows], sum_hd)
            do = dot_nt(dml, wsq_s[layer, 0]).astype(BF).astype(F32)
            do = (do * recip).astype(BF)
            mass = do.astype(F32) * o_s[layer, rows]
            mass_hi = mass.astype(BF)
            mass_lo = (mass - mass_hi.astype(F32)).astype(BF)
            delta = dot_nn(mass_hi, sum_hk) + dot_nn(mass_lo, sum_hk)
            qu = att_s[layer, rows, 0:256]
            key = att_s[layer, rows, 512:768]
            val = att_s[layer, rows, 768:1024]
            draws = []
            for b in range(CHUNK):
                span = slice(TOKS * b, TOKS * b + TOKS)
                probs = pu_s[layer, pl.ds(pl.multiple_of(c * rows_c + TOKS * b, TOKS), TOKS)]
                dprob = dot_nt(do[span], expand(val[span]))
                dscore = (probs.astype(F32) * (dprob - delta[span])).astype(BF)
                wide = dscore.astype(F32)
                draws.append(
                    [unskew(wide[STEPS * k : STEPS * k + STEPS]).astype(BF) for k in range(3)]
                )
                dval = fold(dot_tn(probs, do[span])).astype(BF)
                dkey = (fold(dot_tn(dscore, qu[span])) * SCALE).astype(BF)
                l_s[span] = dot_nn(dscore, expand(key[span])) * SCALE
                out_rows = pl.ds(pl.multiple_of(c * rows_c + TOKS * b, TOKS), TOKS)
                pu_s[layer, out_rows] = jnp.concatenate(draws[b], axis=0)
                att_s[layer, out_rows, 512:768] = dkey
                att_s[layer, out_rows, 768:1024] = dval
            dqv = [
                dot_nn(
                    jnp.concatenate([draws[b][k] for b in range(CHUNK)], axis=0), rk_s[layer, k]
                ).reshape(CHUNK, 1, STEPS, D)
                for k in range(3)
            ]
            dqv = jnp.concatenate(dqv, axis=1).reshape(rows_c, D) * SCALE
            dqu = l_s[...]
            slot_s[0, 4 * layer + 2 : 4 * layer + 3] += jnp.sum(dqu, axis=0, keepdims=True)
            slot_s[0, 4 * layer + 3 : 4 * layer + 4] += jnp.sum(dqv, axis=0, keepdims=True)
            dq = (dqu + dqv).astype(BF)
            att_s[layer, rows, 0:256] = dq
            dlow = (
                dot_nt(dq, wqkv_s[layer, :, :256])
                + dot_nt(att_s[layer, rows, 512:768], wqkv_s[layer, :, 256:512])
                + dot_nt(att_s[layer, rows, 768:1024], wqkv_s[layer, :, 512:])
            )
            x = x_s[layer, rows]
            scale = rms(x)
            hat = x * scale
            slot_s[0, 4 * layer : 4 * layer + 1] += jnp.sum(dlow * hat, axis=0, keepdims=True)
            inner = dlow * gain_a
            dx = scale * (inner - hat * jnp.mean(inner * hat, axis=-1, keepdims=True)) + dmid
            x_s[LAYERS, rows] = dx

        comm.tick()
        put(4096, dot_tn(o_s[layer].astype(BF), dml_s[...]))
        drk = []
        draw = pu_s[layer].reshape(seqs, 3, STEPS, HK)
        qv = att_s[layer, :, 256:512].reshape(seqs, 3, STEPS, D)
        for k in range(3):
            wide = dot_tn(
                draw[:, k].reshape(steps_all, HK), qv[:, k].reshape(steps_all, D)
            )
            drk.append(fold(wide) * SCALE)
        put(4608, dot_tn(pos_ref[...], jnp.concatenate(drk, axis=0).astype(BF)))
        put(5120, dot_tn(a_s[layer], att_s[layer, :, 0:256]))
        put(5632, dot_tn(a_s[layer], att_s[layer, :, 512:768]))
        put(6144, dot_tn(a_s[layer], att_s[layer, :, 768:1024]))
        if layer:
            comm.open(2 * (LAYERS - layer))

    dtok = x_s[LAYERS].reshape(seqs, 3, STEPS, D).astype(BF)
    dtok = [dtok[:, k].reshape(steps_all, D) for k in range(3)]
    base = 2560 + 6656 * LAYERS
    class_row = (iota((256, steps_all), 0) % CLASSES).astype(F32)
    for k in range(2):
        for j in range(2):
            wide = dot_nn(spread_t[256 * j : 256 * j + 256], codes[k])
            hot = (wide == class_row).astype(F32).astype(BF)
            part = dot_nn(hot, dtok[0])
            for h in range(2):
                at = base + 1280 * h + 512 * k + 256 * j
                g_s[at : at + 256] = part[:, 128 * h : 128 * h + 128].astype(BF)
    row = iota((288, steps_all), 0)
    hot_a = (row == action_row.astype(jnp.int32)).astype(F32).astype(BF)
    hot_r = (row == (reward_row + NA).astype(jnp.int32)).astype(F32).astype(BF)
    part = dot_nn(hot_a, dtok[1]) + dot_nn(hot_r, dtok[2])
    for h in range(2):
        at = base + 1280 * h + 1024
        g_s[at : at + 256] = part[:256, 128 * h : 128 * h + 128].astype(BF)
    slot_s[0, 16:40] = part[256:280]
    comm.finish(slot_s, got_s, extra_sems, total_ref)


def run_step(codes, seg, pos, small, weights, streams, groups):
    seqs = codes.shape[0] // streams
    toks = seqs * TOKS
    plan, recv, own = exchange_plan(streams, groups)
    rounds = len(plan[0][0]["order"])
    vmem, dma = pltpu.VMEM, pltpu.SemaphoreType.DMA
    hbm = pl.BlockSpec(memory_space=pl.ANY)
    table, qkv, square, up, down, head = weights
    return pl.pallas_call(
        lambda *refs: step_kernel(streams, groups, *refs),
        out_shape=(
            jax.ShapeDtypeStruct((sum(SECTIONS), 128), BF),
            jax.ShapeDtypeStruct((40, D), F32),
        ),
        in_specs=[hbm] + [pl.BlockSpec(memory_space=vmem)] * 3 + [hbm] * 6,
        out_specs=[hbm, pl.BlockSpec(memory_space=vmem)],
        scratch_shapes=[
            vmem((LAYERS + 1, toks, D), F32),
            vmem((LAYERS, toks, 1024), BF),
            vmem((LAYERS, toks, HK), BF),
            vmem((LAYERS, toks, D), F32),
            vmem((LAYERS, toks, D), F32),
            vmem((LAYERS, toks, FF), BF),
            vmem((LAYERS, toks, FF), BF),
            vmem((LAYERS, toks, D), BF),
            vmem((LAYERS, toks, D), BF),
            vmem((toks, D), BF),
            vmem((toks, D), BF),
            vmem((LAYERS, 3, HK, D), BF),
            vmem((seqs, STEPS, 128), F32),
            vmem((CHUNK * TOKS, D), F32),
            vmem((HCOLS, seqs * STEPS), BF),
            vmem((TROWS, D), BF),
            vmem(qkv.shape, BF),
            vmem(square.shape, BF),
            vmem(up.shape, BF),
            vmem(down.shape, BF),
            vmem(head.shape, BF),
            vmem(head.shape[::-1], BF),
            vmem(table.shape, F32),
            vmem(codes.shape, jnp.int32),
            vmem((streams, STEPS, seqs * STEPS), BF),
            vmem((streams, STEPS, seqs * STEPS), BF),
            vmem((sum(SECTIONS), 128), BF),
            vmem((recv, 128), BF),
            vmem((own, 128), BF),
            vmem((rounds + 1, 40, D), F32),
            vmem((rounds, 40, D), F32),
            dma((2 + 13 * LAYERS + 5,)),
            dma((2, streams - 1)),
            dma((len(plan), 3, 4, rounds)),
            dma((len(plan), 3)),
            dma((2, rounds)),
        ],
        compiler_params=pltpu.CompilerParams(
            collective_id=0, has_side_effects=True, vmem_limit_bytes=VMEM_LIMIT
        ),
        name="step",
    )(codes, seg, pos, small, table, qkv, square, up, down, head)


def update_pieces():
    pieces = []
    for k in range(LAYERS):
        layer = LAYERS - 1 - k
        base = 2560 + 6656 * k
        for half in range(2):
            r = 512 * half
            pieces.append(
                (4, (layer,), r, 512, [(base + 1024 * j + r, 128 * j) for j in range(2)])
            )
        pieces.append((3, (layer,), 0, 256, [(base + 2048 + 256 * j, 128 * j) for j in range(8)]))
        pieces.append((2, (layer, 0), 0, 256, [(base + 4096 + 256 * j, 128 * j) for j in range(2)]))
        pieces.append((2, (layer, 1), 0, 256, [(base + 4608 + 256 * j, 128 * j) for j in range(2)]))
        pieces.append((1, (layer,), 0, 256, [(base + 5120 + 256 * j, 128 * j) for j in range(6)]))
    pieces.append((6, (), 0, 256, [(256 * j, 128 * j) for j in range(10)]))
    base = 2560 + 6656 * LAYERS
    pieces.append((0, (), 0, 1280, [(base + 1280 * j, 128 * j) for j in range(2)]))
    return pieces


def update_kernel(clip_value, step_rate, *refs):
    g_ref, e_ref = refs[:2]
    ins = refs[2:23]
    stat_ref = refs[23]
    outs = refs[24:45]
    bufs = refs[45:66]
    isem, osem = refs[66:]
    pieces = update_pieces()
    table_rows = ins[0].shape[0]
    tail = table_rows - 1280

    def view(ref, piece):
        array, lead, first, rows, _ = piece
        if lead:
            ref = ref.at[lead]
        if ref.shape[0] == rows:
            return ref
        return ref.at[pl.ds(first, rows)]

    def transfer(kind, n, k, piece):
        src, dst = (ins, bufs) if kind == 0 else (bufs, outs)
        array = piece[0]
        sem = (isem, osem)[kind].at[k, n]
        return pltpu.make_async_copy(
            view(src[7 * k + array], piece), view(dst[7 * k + array], piece), sem
        )

    specials = [(0, (), 1280, tail, None), (5, (), 0, ins[5].shape[0], None)]
    order = specials + pieces
    for n, piece in enumerate(order):
        for k in range(3):
            transfer(0, n, k, piece).start()

    block = 128
    count = g_ref.shape[0] // block

    def gather(j, total):
        v = g_ref[pl.ds(pl.multiple_of(j * block, block), block)].astype(F32)
        return total + jnp.sum((v * v).reshape(block // 8, 8, 128), axis=0)

    total = lax.fori_loop(0, count, gather, jnp.zeros((8, 128), F32))
    rest = jnp.sum(e_ref[0:9] * e_ref[0:9]) + jnp.sum(e_ref[16:40] * e_ref[16:40])
    loss = jnp.max(e_ref[9:10])
    terms = jnp.max(e_ref[10:11])
    inverse = 1.0 / jnp.full((8, 128), terms, F32)
    norm = jnp.sqrt(jnp.full((8, 128), jnp.sum(total) + rest, F32)) * inverse
    factor = inverse * clip_value / jnp.maximum(norm, clip_value)
    stat_ref[0:8] = jnp.full((8, 128), loss, F32)
    stat_ref[8:16] = jnp.full((8, 128), terms, F32)
    stat_ref[16:24] = norm
    factor = factor[:1]

    def advance(views, rows, cols, gradient, scale):
        w, m, e = [v[rows, cols] for v in views]
        clipped = gradient * scale
        moment = MOMENTUM_RATE * m + clipped
        weight = w - step_rate * (clipped + MOMENTUM_RATE * moment)
        views[0][rows, cols] = weight
        views[1][rows, cols] = moment
        views[2][rows, cols] = AVERAGE_RATE * e + (1.0 - AVERAGE_RATE) * weight

    for n, piece in enumerate(order):
        array, lead, first, rows, blocks = piece
        for k in range(3):
            transfer(0, n, k, piece).wait()
        views = [bufs[7 * k + array].at[lead] if lead else bufs[7 * k + array] for k in range(3)]
        if blocks is None:
            at = 16 if array == 0 else 0
            wide = jnp.concatenate([factor, factor], axis=1)
            advance(
                views, slice(first, first + rows), slice(0, D), e_ref[at : at + rows], wide
            )
        else:
            step = 64

            @pl.loop(0, rows // step)
            def _(j):
                for source, column in blocks:
                    g = g_ref[pl.ds(pl.multiple_of(source + j * step, step), step)].astype(F32)
                    at = pl.ds(pl.multiple_of(first + j * step, step), step)
                    advance(views, at, slice(column, column + 128), g, factor)

        for k in range(3):
            transfer(1, n, k, piece).start()
    for n, piece in enumerate(order):
        for k in range(3):
            transfer(1, n, k, piece).wait()


def update_all(grads, extra, arrays, clip_value, step_rate):
    vmem = pltpu.VMEM
    count = len(update_pieces()) + 2
    hbm = pl.BlockSpec(memory_space=pl.ANY)
    results = pl.pallas_call(
        lambda *refs: update_kernel(clip_value, step_rate, *refs),
        out_shape=[jax.ShapeDtypeStruct((24, 128), F32)]
        + [jax.ShapeDtypeStruct(a.shape, F32) for a in arrays],
        in_specs=[pl.BlockSpec(memory_space=vmem)] * 2 + [hbm] * 21,
        out_specs=[pl.BlockSpec(memory_space=vmem)] + [hbm] * 21,
        scratch_shapes=[vmem(a.shape, F32) for a in arrays]
        + [pltpu.SemaphoreType.DMA((3, count)), pltpu.SemaphoreType.DMA((3, count))],
        compiler_params=pltpu.CompilerParams(vmem_limit_bytes=44 * 1000 * 1000),
        name="update",
    )(grads, extra, *arrays)
    return results[0], results[1:]


def on_device(step_codes, segments, *arrays):
    streams = lax.axis_size("stream")
    groups = lax.axis_size("seq")
    group_seqs = step_codes.shape[0]
    table, qkv, square, up, down, small, head = arrays[:7]
    pos = jnp.asarray(position_rows()).astype(BF)
    grads, extra = run_step(
        step_codes, segments, pos, small, (table, qkv, square, up, down, head), streams, groups
    )
    params_total = sum(w.size for w in arrays[:7])
    clip_value = CLIP_SCALE * (group_seqs * groups * STEPS) ** (-0.5)
    step_rate = STEP_SCALE * params_total**0.5 / clip_value
    stats, updated = update_all(grads, extra, arrays, clip_value, step_rate)
    return (stats[0, 0], stats[8, 0], stats[16, 0], *updated)


def solution(mesh):
    return jax.shard_map(
        on_device,
        mesh=mesh,
        in_specs=(P("seq", None, "stream"), P("seq", None)) + (P(),) * 21,
        out_specs=(P(),) * 24,
        check_vma=False,
    )
```

```python
import math

import jax
import jax.numpy as jnp
import numpy as np
from jax import lax
from jax.experimental import pallas as pl
from jax.experimental.pallas import tpu as pltpu
from jax.sharding import PartitionSpec as P

D = 256
HEADS = 8
HD = 32
FF = 1024
CATS = 32
CLASSES = 32
NA = 18
STEPS = 16
TOKS = 48
HK = HEADS * TOKS
LAYERS = 2
HCOLS = 1280
TROWS = 1408
CHUNK = 16
GROUP = 8
EPSILON = 1e-06
MOMENTUM_RATE = 0.9
AVERAGE_RATE = 0.7
CLIP_SCALE = 0.2
STEP_SCALE = 0.03
MASKED = -1e30
POSITION_SCALE = 0.5
SCALE = HD ** (-0.5)
BF = jnp.bfloat16
F32 = jnp.float32
VMEM_LIMIT = 63 * 1000 * 1000


def dot_nn(a, b):
    return lax.dot_general(a, b, (((1,), (0,)), ((), ())), preferred_element_type=F32)


def dot_nt(a, b):
    return lax.dot_general(a, b, (((1,), (1,)), ((), ())), preferred_element_type=F32)


def dot_tn(a, b):
    return lax.dot_general(a, b, (((0,), (0,)), ((), ())), preferred_element_type=F32)


def iota(shape, dim):
    return lax.broadcasted_iota(jnp.int32, shape, dim)


def position_rows():
    distance = np.arange(TOKS, dtype=np.float32)[:, None]
    rates = np.exp(np.arange(D // 2, dtype=np.float32) * np.float32(-2.0 * math.log(10000.0) / D))
    angle = (distance * rates[None, :].astype(np.float32)).astype(np.float32)
    table = np.float32(POSITION_SCALE) * np.concatenate([np.sin(angle), np.cos(angle)], axis=1)
    rows = np.zeros((3, TOKS, D), np.float32)
    for i in range(3):
        for j in range(3):
            for e in range(STEPS):
                d = 3 * (STEPS - 1 - e) + i - j
                if d >= 0:
                    rows[i, j * STEPS + e] = table[d]
    return rows.reshape(3 * TOKS, D)


def rms(values):
    return lax.rsqrt(jnp.mean(values * values, axis=-1, keepdims=True) + EPSILON)


def head_mask(h, rows):
    lane = iota((rows, 128), 1)
    low = (h % 4) * HD
    return ((lane >= low) & (lane < low + HD)).astype(F32).astype(BF)


def expand(rows):
    zero = jnp.zeros((TOKS, 128), BF)
    parts = []
    for h in range(HEADS):
        half = rows[:, 128 * (h // 4) : 128 * (h // 4) + 128] * head_mask(h, TOKS)
        parts.append(jnp.concatenate([half, zero] if h < 4 else [zero, half], axis=1))
    return jnp.concatenate(parts, axis=0)


def fold(values):
    lane = iota((TOKS, 128), 1)
    halves = []
    for g in range(2):
        total = None
        for h in range(4):
            part = values[(4 * g + h) * TOKS : (4 * g + h + 1) * TOKS, 128 * g : 128 * g + 128]
            total = part if total is None else jnp.where(lane >= h * HD, part, total)
        halves.append(total)
    return jnp.concatenate(halves, axis=1)


def spans(tile):
    found = []
    for h in range(HEADS):
        low, high = max(TOKS * h - 128 * tile, 0), min(TOKS * (h + 1) - 128 * tile, 128)
        if low < high:
            found.append((h, low, high))
    return found


def segment_max(scores):
    rows = scores.shape[0]
    lane = iota((rows, 128), 1)
    tiles = [scores[:, 128 * t : 128 * t + 128] for t in range(3)]
    best = {}
    for t in range(3):
        for h, low, high in spans(t):
            part = jnp.where((lane >= low) & (lane < high), tiles[t], -3e38)
            best[h] = part if h not in best else jnp.maximum(best[h], part)
    best = {h: jnp.max(v, axis=1, keepdims=True) for h, v in best.items()}
    outs = []
    for t in range(3):
        total = None
        for h, low, high in spans(t):
            wide = jnp.broadcast_to(best[h], (rows, 128))
            total = wide if total is None else jnp.where(lane >= low, wide, total)
        outs.append(total)
    return jnp.concatenate(outs, axis=1)


def unskew(values):
    row = iota((STEPS, HK), 0)
    values = jnp.concatenate(
        [pltpu.roll(values[:8], 15, 1), pltpu.roll(values[8:], 7, 1)], axis=0
    )
    for bit in (1, 2, 4):
        values = jnp.where((row & bit) > 0, pltpu.roll(values, HK - bit, 1), values)
    return values


SECTIONS = (2560, 4608, 2048, 4608, 4608)
DUE = ((1, 3, 5, 7, 9, 10), (3, 6, 8, 10), (7, 9, 11), (9, 12), ())


def stage_orders(streams, groups):
    rest, others = [], []
    step = 2
    while step < streams:
        rest.append(("stream", step))
        step *= 2
    step = 1
    while step < groups:
        others.append(("seq", step))
        step *= 2
    near = [tuple(others[:1] + rest)]
    far = [tuple(others[k : k + 2]) for k in range(1, len(others), 2)]
    core = [(("stream", 1),)]
    return [core + near + far, core + far + near]


def exchange_plan(streams, groups):
    unit = 16 * streams * groups
    sections = SECTIONS
    if any(s % unit or s < 2 * unit for s in sections):
        sections = (sum(SECTIONS),)
    orders = stage_orders(streams, groups)
    plan, base, recv, own = [], 0, 0, 0
    for rows in sections:
        units = rows // unit
        last = max(1, round(0.222 * units))
        lanes = []
        for part, order in zip((units - last, last), orders):
            size, sizes, slots = part * unit, [], []
            for bits in order:
                size //= 2 ** len(bits)
                sizes.append(size)
                slots.append(recv)
                recv += size * (2 ** len(bits) - 1)
            lanes.append(dict(base=base, order=order, sizes=sizes, slots=slots, own=own))
            own += size
            base += part * unit
        plan.append(lanes)
    assert base == sum(SECTIONS)
    return plan, recv, own


def place_of(bit):
    axis, step = bit
    return (lax.axis_index(axis) // step) % 2


def flips_of(bits):
    count = len(bits)
    return [tuple((n >> k) % 2 for k in range(count)) for n in range(1, 2**count)]


def partner_of(bits, flips):
    place = {"stream": lax.axis_index("stream"), "seq": lax.axis_index("seq")}
    for bit, flip in zip(bits, flips):
        if flip:
            axis, step = bit
            place[axis] = place[axis] + step * (1 - 2 * place_of(bit))
    return (place["stream"], place["seq"])


def share_of(bits, flips):
    total = 0
    for bit, flip in zip(bits, flips):
        mine = place_of(bit)
        total = 2 * total + ((1 - mine) if flip else mine)
    return total


class Lane:
    def __init__(self, spec, refs, sems, own_sem):
        self.spec, self.sems, self.own_sem = spec, sems, own_sem
        self.g, self.out, self.recv, self.own = refs
        offset = spec["base"]
        self.keep, self.send = [], []
        for bits, size in zip(spec["order"], spec["sizes"]):
            self.send.append(
                [
                    pl.multiple_of(offset + share_of(bits, flips) * size, 16)
                    for flips in flips_of(bits)
                ]
            )
            offset = pl.multiple_of(offset + share_of(bits, (0,) * len(bits)) * size, 16)
            self.keep.append(offset)

    def remote(self, kind, i, n, src, dst):
        bits = self.spec["order"][i]
        return pltpu.make_async_remote_copy(
            src_ref=src,
            dst_ref=dst,
            send_sem=self.sems.at[2 * kind, i, n],
            recv_sem=self.sems.at[2 * kind + 1, i, n],
            device_id=partner_of(bits, flips_of(bits)[n]),
            device_id_type=pl.DeviceIdType.MESH,
        )

    def scatter(self, i):
        size, slot = self.spec["sizes"][i], self.spec["slots"][i]
        return [
            self.remote(
                0, i, n, self.g.at[pl.ds(at, size)], self.recv.at[pl.ds(slot + n * size, size)]
            )
            for n, at in enumerate(self.send[i])
        ]

    def mine(self):
        return self.own.at[pl.ds(self.spec["own"], self.spec["sizes"][-1])]

    def keep_copy(self):
        rows = pl.ds(self.keep[-1], self.spec["sizes"][-1])
        return pltpu.make_async_copy(self.mine(), self.out.at[rows], self.own_sem)

    def gather(self, i):
        rows = pl.ds(self.keep[i], self.spec["sizes"][i])
        last = i + 1 == len(self.keep)
        return [
            self.remote(1, i, n, self.mine() if last else self.out.at[rows], self.out.at[rows])
            for n in range(len(self.send[i]))
        ]

    def add(self, i):
        size, slot = self.spec["sizes"][i], self.spec["slots"][i]
        last = i + 1 == len(self.keep)
        block = 256
        while size % block:
            block //= 2

        @pl.loop(0, size // block)
        def _(j):
            at = pl.ds(pl.multiple_of(self.keep[i] + j * block, 16), block)
            value = self.g[at].astype(F32)
            for n in range(len(self.send[i])):
                got = pl.ds(pl.multiple_of(slot + n * size + j * block, 16), block)
                value = value + self.recv[got].astype(F32)
            if last:
                own = pl.multiple_of(self.spec["own"] + j * block, 16)
                self.own[pl.ds(own, block)] = value.astype(BF)
            else:
                self.g[at] = value.astype(BF)


def start_all(copies):
    for copy in copies:
        copy.start()


def wait_all(copies):
    for copy in copies:
        copy.wait()


class Exchange:
    def __init__(self, streams, groups, g_ref, out_ref, recv_ref, own_ref, sems, own_sems):
        plan, _, _ = exchange_plan(streams, groups)
        refs = (g_ref, out_ref, recv_ref, own_ref)
        self.sections = [
            [
                Lane(spec, refs, sems.at[n, k], own_sems.at[n, k])
                for k, spec in enumerate(lanes)
            ]
            for n, lanes in enumerate(plan)
        ]
        self.order = plan[0][0]["order"]
        self.stages = len(self.order)
        self.active = []
        self.moment = 0

    def open(self, n):
        if len(self.sections) > 1:
            for lane in self.sections[n]:
                start_all(lane.scatter(0))
            self.active.append([n, 0])

    def advance(self, n, stage):
        stages = self.stages
        for lane in self.sections[n]:
            if stage < stages:
                wait_all(lane.scatter(stage))
                lane.add(stage)
                if stage + 1 < stages:
                    start_all(lane.scatter(stage + 1))
                else:
                    start_all(lane.gather(stage))
                    lane.keep_copy().start()
            else:
                i = 2 * stages - 1 - stage
                wait_all(lane.gather(i))
                if i + 1 == stages:
                    lane.keep_copy().wait()
                if i:
                    start_all(lane.gather(i - 1))

    def plan(self, count):
        moments = []
        for _ in range(count):
            self.moment += 1
            ready = [
                item
                for item in self.active
                if item[1] < len(DUE[item[0]]) and DUE[item[0]][item[1]] <= self.moment
            ]
            moments.append(self.step(ready))
        return moments

    def step(self, items):
        taken = [tuple(item) for item in items]
        for item in items:
            item[1] += 1
        self.active = [item for item in self.active if item[1] < 2 * self.stages]
        return taken

    def emit(self, moment):
        for n, stage in moment:
            self.advance(n, stage)

    def tick(self):
        self.emit(self.plan(1)[0])

    def when(self, condition, moment):
        if moment:
            pl.when(condition)(lambda: self.emit(moment))

    def finish(self, slot_ref, got_ref, sems, total_ref):
        last = len(self.sections) - 1

        def extra(i):
            bits = self.order[i]
            return [
                pltpu.make_async_remote_copy(
                    src_ref=slot_ref.at[i],
                    dst_ref=got_ref.at[i, n],
                    send_sem=sems.at[0, i, n],
                    recv_sem=sems.at[1, i, n],
                    device_id=partner_of(bits, flips),
                    device_id_type=pl.DeviceIdType.MESH,
                )
                for n, flips in enumerate(flips_of(bits))
            ]

        for lane in self.sections[last]:
            start_all(lane.scatter(0))
        start_all(extra(0))
        self.active.append([last, 0])
        i = 0
        while self.active:
            self.emit(self.step(list(self.active)))
            if i < self.stages:
                wait_all(extra(i))
                slot_ref[i + 1] = self.total(slot_ref[i], got_ref, i)
                if i + 1 < self.stages:
                    start_all(extra(i + 1))
            i += 1
        total_ref[...] = slot_ref[self.stages]

    def total(self, mine, got_ref, i):
        bits = self.order[i]
        if len(bits) == 1:
            return mine + got_ref[i, 0]
        return (mine + got_ref[i, 0]) + (got_ref[i, 1] + got_ref[i, 2])

def step_kernel(
    streams,
    groups,
    codes_hbm,
    seg_ref,
    pos_ref,
    small_ref,
    table_hbm,
    qkv_hbm,
    square_hbm,
    up_hbm,
    down_hbm,
    head_hbm,
    out_hbm,
    total_ref,
    x_s,
    att_s,
    pu_s,
    o_s,
    mid_s,
    hb_s,
    gp_s,
    b_s,
    dyl_s,
    dml_s,
    rk_s,
    start_s,
    l_s,
    slope_s,
    table_s,
    tail_s,
    wqkv_s,
    wsq_s,
    wup_s,
    wdown_s,
    whead_s,
    wheadt_s,
    raw_s,
    send_s,
    got_codes_s,
    g_s,
    recv_s,
    own_s,
    slot_s,
    got_s,
    load_sems,
    code_sems,
    sems,
    own_sems,
    extra_sems,
):
    toks = x_s.shape[1]
    seqs = toks // TOKS
    steps_all = seqs * STEPS
    chunks = seqs // CHUNK
    rows_c = CHUNK * TOKS
    me = lax.axis_index("stream")
    table_rows = table_hbm.shape[0]

    raw_load = pltpu.make_async_copy(codes_hbm, raw_s, load_sems.at[0])
    raw_load.start()
    whole = table_rows // 128 * 128
    rest = table_rows - whole
    loads = []

    def load(src, place, targets):
        copy = pltpu.make_async_copy(src, place, load_sems.at[len(loads) + 1])
        loads.append((copy, place, targets))

    table_rows_main = pl.ds(0, whole)
    load(
        table_hbm.at[table_rows_main],
        x_s.at[2, table_rows_main],
        [(table_s.at[table_rows_main], False)],
    )
    load(table_hbm.at[pl.ds(whole, rest)], tail_s, None)
    for layer in range(LAYERS):
        places = [o_s.at[layer, pl.ds(256 * j, 256)] for j in range(6)]
        places += [mid_s.at[layer, pl.ds(256 * j, 256)] for j in range(6)]
        places += [x_s.at[1, pl.ds(256 * layer, 256)]]
        places = iter(places)
        for j in range(3):
            cols = pl.ds(256 * j, 256)
            load(qkv_hbm.at[layer, :, cols], next(places), [(wqkv_s.at[layer, :, cols], False)])
        for j in range(2):
            load(square_hbm.at[layer, j], next(places), [(wsq_s.at[layer, j], False)])
        for j in range(4):
            cols = pl.ds(256 * j, 256)
            load(up_hbm.at[layer, :, cols], next(places), [(wup_s.at[layer, :, cols], False)])
        for j in range(4):
            cols = pl.ds(256 * j, 256)
            load(down_hbm.at[layer, cols], next(places), [(wdown_s.at[layer, cols], False)])
    for j in range(HCOLS // 256):
        cols = pl.ds(256 * j, 256)
        load(
            head_hbm.at[:, cols],
            x_s.at[1, pl.ds(512 + 256 * j, 256)] if j < 4 else l_s.at[pl.ds(0, 256)],
            [(whead_s.at[:, cols], False), (wheadt_s.at[cols], True)],
        )
    for copy, _, _ in loads:
        copy.start()

    comm = Exchange(streams, groups, g_s, out_hbm, recv_s, own_s, sems, own_sems)
    barrier = pltpu.get_barrier_semaphore()
    greeted = [((me + j) % streams, lax.axis_index("seq")) for j in range(1, streams)]
    peers = list(greeted)
    for bits in comm.order:
        for flips in flips_of(bits):
            if any(flip and bit[0] == "seq" for bit, flip in zip(bits, flips)):
                greeted.append(partner_of(bits, flips))
    for peer in greeted:
        pl.semaphore_signal(
            barrier, inc=1, device_id=peer, device_id_type=pl.DeviceIdType.MESH
        )

    raw_load.wait()
    send_s[...] = raw_s[...].astype(F32).astype(BF)
    pl.semaphore_wait(barrier, len(greeted))
    sends = []
    for j, peer in enumerate(peers):
        sends.append(
            pltpu.make_async_remote_copy(
                src_ref=send_s,
                dst_ref=got_codes_s.at[me],
                send_sem=code_sems.at[0, j],
                recv_sem=code_sems.at[1, j],
                device_id=peer,
                device_id_type=pl.DeviceIdType.MESH,
            )
        )
        sends[-1].start()
    got_codes_s[me] = send_s[...]

    group = seg_ref.shape[1]
    step_lane = iota((STEPS, steps_all), 1) % STEPS
    step_row = iota((STEPS, steps_all), 0)
    own_lane = iota((group, steps_all), 1) // STEPS + me * seqs
    pick = (iota((group, steps_all), 0) == own_lane).astype(F32).astype(BF)
    seg = dot_nn(seg_ref[...].astype(F32).astype(BF), pick)
    seg_own = jnp.sum(jnp.where(step_row == step_lane, seg, 0.0), axis=0, keepdims=True)
    start = jnp.sum(jnp.where(seg < seg_own, 1.0, 0.0), axis=0, keepdims=True)
    valid_row = jnp.sum(
        jnp.where((step_row == step_lane + 1) & (seg == seg_own), 1.0, 0.0), axis=0, keepdims=True
    )
    start_low = jnp.broadcast_to(start, (STEPS, steps_all)).astype(BF)
    one_row = (iota((STEPS, 128), 0) == 0).astype(F32).astype(BF)
    start_s[...] = dot_tn(start_low, one_row).reshape(seqs, STEPS, 128)

    table_s[whole:] = jnp.zeros((TROWS - whole, D), BF)
    for copy, place, targets in loads:
        copy.wait()
        if targets is None:
            pad = -rest % 16
            table_s[whole : whole + rest + pad] = jnp.concatenate(
                [place[...], jnp.zeros((pad, D), F32)], axis=0
            ).astype(BF)
            continue
        for target, turned in targets:
            target[...] = (place[...].T if turned else place[...]).astype(BF)
    for copy in sends:
        copy.wait()
    codes = []
    for k in range(4):
        wide = dot_nn(got_codes_s[k].reshape(STEPS * STEPS, group), pick)
        wide = wide.reshape(STEPS, STEPS, steps_all)
        at_step = iota((STEPS, STEPS, steps_all), 0) == iota((STEPS, STEPS, steps_all), 2) % STEPS
        codes.append(jnp.sum(jnp.where(at_step, wide, 0.0), axis=0).astype(BF))

    spread = (iota((STEPS, 512), 1) // CLASSES == iota((STEPS, 512), 0)).astype(F32).astype(BF)
    first = (iota((STEPS, 384), 0) == 0).astype(F32).astype(BF)
    class_lane = (iota((128, 512), 1) % CLASSES).astype(F32)
    lane = iota((128, 384), 1).astype(F32)
    for c in range(steps_all // 128):
        cols = slice(128 * c, 128 * c + 128)
        halves = []
        for k in range(2):
            hot = (dot_tn(codes[k][:, cols], spread) == class_lane).astype(F32).astype(BF)
            piece = dot_nn(hot, table_s[512 * k : 512 * k + 512]).astype(BF).astype(F32)
            halves.append(piece)
        hot = (dot_tn(codes[2][:, cols], first[:, :128]) == lane[:, :128]).astype(F32).astype(BF)
        action = dot_nn(hot, table_s[1024:1152]).astype(BF).astype(F32)
        hot = (dot_tn(codes[3][:, cols], first) + NA == lane).astype(F32).astype(BF)
        reward = dot_nn(hot, table_s[1024:1408]).astype(BF).astype(F32)
        pieces = [p.reshape(8, 1, STEPS, D) for p in (halves[0] + halves[1], action, reward)]
        x_s[0, 384 * c : 384 * c + 384] = jnp.concatenate(pieces, axis=1).reshape(384, D)
    for layer in range(LAYERS):
        rk = dot_nn(pos_ref[...], wsq_s[layer, 1]).astype(BF)
        for k in range(3):
            rk_s[layer, k] = expand(rk[TOKS * k : TOKS * k + TOKS])

    lane_hk = iota((TOKS, HK), 1) % TOKS
    key_step = lane_hk % STEPS
    key_time = 3 * key_step + lane_hk // STEPS
    row_tok = iota((TOKS, HK), 0)
    query_time = 3 * (row_tok % STEPS) + row_tok // STEPS
    causal = key_time <= query_time
    key_step_f = key_step.astype(F32)
    sum_hd = (iota((HK, D), 0) // TOKS == iota((HK, D), 1) // HD).astype(F32).astype(BF)
    sum_hk = (iota((D, HK), 0) // HD == iota((D, HK), 1) // TOKS).astype(F32).astype(BF)

    for layer in range(LAYERS):
        gain_a = small_ref[4 * layer : 4 * layer + 1]
        gain_b = small_ref[4 * layer + 1 : 4 * layer + 2]
        bias_u = small_ref[4 * layer + 2 : 4 * layer + 3]
        bias_v = small_ref[4 * layer + 3 : 4 * layer + 4]

        @pl.loop(0, chunks)
        def _(c):
            rows = pl.ds(pl.multiple_of(c * rows_c, rows_c), rows_c)
            x = x_s[layer, rows]
            low = (x * rms(x) * gain_a).astype(BF)
            q = dot_nn(low, wqkv_s[layer, :, :256]).astype(BF).astype(F32)
            qu = (q + bias_u).astype(BF)
            qv = (q + bias_v).astype(BF)
            key = dot_nn(low, wqkv_s[layer, :, 256:512]).astype(BF)
            val = dot_nn(low, wqkv_s[layer, :, 512:]).astype(BF)
            att_s[layer, rows, 0:256] = qu
            att_s[layer, rows, 256:512] = qv
            att_s[layer, rows, 512:768] = key
            att_s[layer, rows, 768:1024] = val
            qv4 = qv.reshape(CHUNK, 3, STEPS, D)
            place = [
                dot_nt(qv4[:, k].reshape(CHUNK * STEPS, D), rk_s[layer, k]) for k in range(3)
            ]
            start_c = start_s[pl.ds(c * CHUNK, CHUNK)]
            for g in range(0, CHUNK, GROUP):
                members = range(g, g + GROUP)
                spans = {b: slice(TOKS * b, TOKS * b + TOKS) for b in members}
                scores = {b: dot_nt(qu[spans[b]], expand(key[spans[b]])) for b in members}
                for b in members:
                    shifted = [
                        pltpu.roll(
                            place[k][STEPS * b : STEPS * b + STEPS],
                            HK - (STEPS - 1),
                            1,
                            stride=1,
                            stride_axis=0,
                        )
                        for k in range(3)
                    ]
                    begin = jnp.concatenate([start_c[b]] * 3, axis=0)
                    begin = jnp.concatenate([begin] * 3, axis=1)
                    score = (scores[b] + jnp.concatenate(shifted, axis=0)) * SCALE
                    scores[b] = jnp.where(causal & (key_step_f >= begin), score, MASKED)
                tops = {b: segment_max(scores[b]) for b in members}
                probs = {b: jnp.exp(scores[b] - tops[b]).astype(BF) for b in members}
                for b in members:
                    l_s[spans[b]] = dot_nn(probs[b], expand(val[spans[b]]))
                for b in members:
                    pu_s[layer, pl.ds(pl.multiple_of(c * rows_c + TOKS * b, TOKS), TOKS)] = probs[b]
            recip = 1.0 / dot_nn(pu_s[layer, rows], sum_hd)
            out = l_s[...] * recip
            o_s[layer, rows] = out
            mid = x + dot_nn(out.astype(BF), wsq_s[layer, 0])
            mid_s[layer, rows] = mid
            low = (mid * rms(mid) * gain_b).astype(BF)
            for j in range(FF // 256):
                cols = slice(256 * j, 256 * j + 256)
                inner = dot_nn(low, wup_s[layer, :, cols])
                square = inner * inner
                c0 = math.sqrt(2.0 / math.pi)
                tanh = jnp.tanh(c0 * inner * (1.0 + 0.044715 * square))
                half = 0.5 * (1.0 + tanh)
                hb_s[layer, rows, cols] = (inner * half).astype(BF)
                gp_s[layer, rows, cols] = (
                    half
                    + (0.5 * c0) * inner * (1.0 - tanh * tanh) * (1.0 + (3 * 0.044715) * square)
                ).astype(BF)
            nxt = mid + dot_nn(hb_s[layer, rows], wdown_s[layer])
            x_s[layer + 1, rows] = nxt

    gain_f = small_ref[4 * LAYERS : 4 * LAYERS + 1]
    xf = x_s[LAYERS].reshape(seqs, 3, STEPS, D)[:, 1].reshape(steps_all, D)
    feat = (xf * rms(xf) * gain_f).astype(BF)
    spread_t = (iota((512, STEPS), 0) // CLASSES == iota((512, STEPS), 1)).astype(F32).astype(BF)
    class_row = iota((4, CLASSES, steps_all), 1).astype(F32)
    loss = jnp.zeros((4, steps_all), F32)
    for k in range(2):
        follow_codes = pltpu.roll(codes[k].astype(F32), steps_all - 1, 1).astype(BF)
        for j in range(4):
            base = 512 * k + 128 * j
            logits = dot_nt(wheadt_s[base : base + 128], feat).reshape(4, CLASSES, steps_all)
            target = dot_nn(spread_t[128 * j : 128 * j + 128], follow_codes)
            hot = target.reshape(4, CLASSES, steps_all) == class_row
            top = jnp.max(logits, axis=1, keepdims=True)
            grown = jnp.exp(logits - top)
            total = jnp.sum(grown, axis=1, keepdims=True)
            picked = jnp.sum(jnp.where(hot, logits, 0.0), axis=1)
            loss = loss + valid_row * (jnp.log(total[:, 0]) + top[:, 0] - picked)
            slope = (grown * (1.0 / total) - jnp.where(hot, 1.0, 0.0)) * valid_row[None]
            slope_s[base : base + 128] = slope.reshape(128, steps_all).astype(BF)
    action_row = codes[2][0:1].astype(F32)
    discount_row = codes[2][1:2].astype(F32)
    reward_row = codes[3][0:1].astype(F32)
    logits = dot_nt(wheadt_s[1024:1280], feat)
    row = iota((256, steps_all), 0)
    hot = row == (reward_row + 1.0).astype(jnp.int32)
    disc = logits[:1]
    masked = jnp.where(row == 0, -3e38, logits)
    top = jnp.max(masked, axis=0, keepdims=True)
    grown = jnp.exp(masked - top)
    total = jnp.sum(grown, axis=0, keepdims=True)
    picked = jnp.sum(jnp.where(hot, logits, 0.0), axis=0, keepdims=True)
    fade = jnp.exp(-jnp.abs(disc))
    soft = jnp.maximum(disc, 0.0) + jnp.log(1.0 + fade)
    sigm = jnp.where(disc >= 0.0, 1.0, fade) / (1.0 + fade)
    loss_row = (
        jnp.sum(loss, axis=0, keepdims=True)
        + jnp.log(total)
        + top
        - picked
        + soft
        - discount_row * disc
    )
    slope = grown * (1.0 / total) - jnp.where(hot, 1.0, 0.0)
    slope = jnp.where(row == 0, sigm - discount_row, slope)
    slope_s[1024:1280] = slope.astype(BF)
    loss_sum = jnp.sum(loss_row)
    count = jnp.sum(valid_row) * CATS + 2.0 * steps_all
    slot_s[0, 9:10] = jnp.full((1, D), loss_sum, F32)
    slot_s[0, 10:11] = jnp.full((1, D), count, F32)
    slot_s[0, 11:16] = jnp.zeros((5, D), F32)

    feat_t = feat.astype(F32).T.astype(BF)
    for j in range(5):
        part = dot_nt(feat_t, slope_s[256 * j : 256 * j + 256])
        for k in range(2):
            base = 256 * (2 * j + k)
            g_s[base : base + 256] = part[:, 128 * k : 128 * k + 128].astype(BF)
    comm.open(0)
    dfeat = dot_nn(whead_s[...], slope_s[...]).T
    scale_f = rms(xf)
    hat = xf * scale_f
    slot_s[0, 8:9] = jnp.sum(dfeat * hat, axis=0, keepdims=True)
    inner = dfeat * gain_f
    dxf = scale_f * (inner - hat * jnp.mean(inner * hat, axis=-1, keepdims=True))
    gap = jnp.zeros((seqs, 1, STEPS, D), F32)
    x_s[LAYERS] = jnp.concatenate([gap, dxf.reshape(seqs, 1, STEPS, D), gap], axis=1).reshape(
        toks, D
    )

    for layer in reversed(range(LAYERS)):
        gain_a = small_ref[4 * layer : 4 * layer + 1]
        gain_b = small_ref[4 * layer + 1 : 4 * layer + 2]
        slot_s[0, 4 * layer : 4 * layer + 4] = jnp.zeros((4, D), F32)

        moments = comm.plan(chunks - 1)

        @pl.loop(0, chunks)
        def _(c):
            rows = pl.ds(pl.multiple_of(c * rows_c, rows_c), rows_c)
            for k in range(1, chunks):
                comm.when(c == k, moments[k - 1])
            dy = x_s[LAYERS, rows]
            dyl = dy.astype(BF)
            dyl_s[rows] = dyl
            for j in range(FF // 256):
                cols = slice(256 * j, 256 * j + 256)
                dact = dot_nt(dyl, wdown_s[layer, cols])
                gp_s[layer, rows, cols] = (dact * gp_s[layer, rows, cols].astype(F32)).astype(BF)
            dlow = dot_nt(gp_s[layer, rows], wup_s[layer])
            mid = mid_s[layer, rows]
            scale = rms(mid)
            hat = mid * scale
            b_s[rows] = (hat * gain_b).astype(BF)
            dgain = jnp.sum(dlow * hat, axis=0, keepdims=True)
            inner = dlow * gain_b
            dmid = scale * (inner - hat * jnp.mean(inner * hat, axis=-1, keepdims=True)) + dy
            slot_s[0, 4 * layer + 1 : 4 * layer + 2] += dgain
            mid_s[layer, rows] = dmid
            dml_s[rows] = dmid.astype(BF)

        base = 2560 + 6656 * (LAYERS - 1 - layer)

        def put(offset, value, base=base):
            size = value.shape[0]
            for k in range(2):
                at = base + offset + k * size
                g_s[at : at + size] = value[:, 128 * k : 128 * k + 128].astype(BF)

        comm.tick()
        for j in range(4):
            part = dot_tn(hb_s[layer, :, 256 * j : 256 * j + 256], dyl_s[...])
            for k in range(2):
                at = base + 1024 * k + 256 * j
                g_s[at : at + 256] = part[:, 128 * k : 128 * k + 128].astype(BF)
        for j in range(4):
            put(2048 + 512 * j, dot_tn(b_s[...], gp_s[layer, :, 256 * j : 256 * j + 256]))
        put(4096, dot_tn(o_s[layer].astype(BF), dml_s[...]))
        comm.open(1 + 2 * (LAYERS - 1 - layer))
        moments_a = comm.plan(2 * chunks - 1)

        @pl.loop(0, chunks)
        def _(c):
            rows = pl.ds(pl.multiple_of(c * rows_c, rows_c), rows_c)
            for k in range(1, chunks):
                comm.when(c == k, moments_a[2 * k - 1])
            dmid = mid_s[layer, rows]
            dml = dml_s[rows]
            recip = 1.0 / dot_nn(pu_s[layer, rows], sum_hd)
            do = dot_nt(dml, wsq_s[layer, 0]).astype(BF).astype(F32)
            do = (do * recip).astype(BF)
            mass = do.astype(F32) * o_s[layer, rows]
            mass_hi = mass.astype(BF)
            mass_lo = (mass - mass_hi.astype(F32)).astype(BF)
            delta = dot_nn(mass_hi, sum_hk) + dot_nn(mass_lo, sum_hk)
            qu = att_s[layer, rows, 0:256]
            key = att_s[layer, rows, 512:768]
            val = att_s[layer, rows, 768:1024]
            probs_all = pu_s[layer, rows]
            draws = {}
            for g in range(0, CHUNK, GROUP):
                members = range(g, g + GROUP)
                spans = {b: slice(TOKS * b, TOKS * b + TOKS) for b in members}
                dprob = {b: dot_nt(do[spans[b]], expand(val[spans[b]])) for b in members}
                dval = {b: dot_tn(probs_all[spans[b]], do[spans[b]]) for b in members}
                dscore = {
                    b: (probs_all[spans[b]].astype(F32) * (dprob[b] - delta[spans[b]])).astype(BF)
                    for b in members
                }
                dkey = {b: dot_tn(dscore[b], qu[spans[b]]) for b in members}
                dque = {b: dot_nn(dscore[b], expand(key[spans[b]])) for b in members}
                for b in members:
                    wide = dscore[b].astype(F32)
                    draws[b] = [
                        unskew(wide[STEPS * k : STEPS * k + STEPS]).astype(BF) for k in range(3)
                    ]
                for b in members:
                    l_s[spans[b]] = dque[b] * SCALE
                for b in members:
                    out_rows = pl.ds(pl.multiple_of(c * rows_c + TOKS * b, TOKS), TOKS)
                    att_s[layer, out_rows, 512:768] = (fold(dkey[b]) * SCALE).astype(BF)
                    att_s[layer, out_rows, 768:1024] = fold(dval[b]).astype(BF)
                    pu_s[layer, out_rows] = jnp.concatenate(draws[b], axis=0)
            for k in range(chunks):
                comm.when(c == k, moments_a[2 * k])
            dqv = [
                dot_nn(
                    jnp.concatenate([draws[b][k] for b in range(CHUNK)], axis=0), rk_s[layer, k]
                ).reshape(CHUNK, 1, STEPS, D)
                for k in range(3)
            ]
            dqv = jnp.concatenate(dqv, axis=1).reshape(rows_c, D) * SCALE
            dqu = l_s[...]
            slot_s[0, 4 * layer + 2 : 4 * layer + 3] += jnp.sum(dqu, axis=0, keepdims=True)
            slot_s[0, 4 * layer + 3 : 4 * layer + 4] += jnp.sum(dqv, axis=0, keepdims=True)
            dq = (dqu + dqv).astype(BF)
            att_s[layer, rows, 0:256] = dq
            dlow = (
                dot_nt(dq, wqkv_s[layer, :, :256])
                + dot_nt(att_s[layer, rows, 512:768], wqkv_s[layer, :, 256:512])
                + dot_nt(att_s[layer, rows, 768:1024], wqkv_s[layer, :, 512:])
            )
            x = x_s[layer, rows]
            scale = rms(x)
            hat = x * scale
            dyl_s[rows] = (hat * gain_a).astype(BF)
            slot_s[0, 4 * layer : 4 * layer + 1] += jnp.sum(dlow * hat, axis=0, keepdims=True)
            inner = dlow * gain_a
            dx = scale * (inner - hat * jnp.mean(inner * hat, axis=-1, keepdims=True)) + dmid
            x_s[LAYERS, rows] = dx

        comm.tick()
        drk = []
        draw = pu_s[layer].reshape(seqs, 3, STEPS, HK)
        qv = att_s[layer, :, 256:512].reshape(seqs, 3, STEPS, D)
        for k in range(3):
            wide = dot_tn(
                draw[:, k].reshape(steps_all, HK), qv[:, k].reshape(steps_all, D)
            )
            drk.append(fold(wide) * SCALE)
        put(4608, dot_tn(pos_ref[...], jnp.concatenate(drk, axis=0).astype(BF)))
        put(5120, dot_tn(dyl_s[...], att_s[layer, :, 0:256]))
        put(5632, dot_tn(dyl_s[...], att_s[layer, :, 512:768]))
        put(6144, dot_tn(dyl_s[...], att_s[layer, :, 768:1024]))
        if layer:
            comm.open(2 * (LAYERS - layer))

    dtok = x_s[LAYERS].reshape(seqs, 3, STEPS, D).astype(BF)
    dtok = [dtok[:, k].reshape(steps_all, D) for k in range(3)]
    base = 2560 + 6656 * LAYERS
    class_row = (iota((256, steps_all), 0) % CLASSES).astype(F32)
    for k in range(2):
        for j in range(2):
            wide = dot_nn(spread_t[256 * j : 256 * j + 256], codes[k])
            hot = (wide == class_row).astype(F32).astype(BF)
            part = dot_nn(hot, dtok[0])
            for h in range(2):
                at = base + 1280 * h + 512 * k + 256 * j
                g_s[at : at + 256] = part[:, 128 * h : 128 * h + 128].astype(BF)
    row = iota((288, steps_all), 0)
    hot_a = (row == action_row.astype(jnp.int32)).astype(F32).astype(BF)
    hot_r = (row == (reward_row + NA).astype(jnp.int32)).astype(F32).astype(BF)
    part = dot_nn(hot_a, dtok[1]) + dot_nn(hot_r, dtok[2])
    for h in range(2):
        at = base + 1280 * h + 1024
        g_s[at : at + 256] = part[:256, 128 * h : 128 * h + 128].astype(BF)
    slot_s[0, 16:40] = part[256:280]
    comm.finish(slot_s, got_s, extra_sems, total_ref)


def run_step(codes, seg, pos, small, weights, streams, groups):
    seqs = codes.shape[2] // streams
    toks = seqs * TOKS
    plan, recv, own = exchange_plan(streams, groups)
    stages = len(plan[0][0]["order"])
    vmem, dma = pltpu.VMEM, pltpu.SemaphoreType.DMA
    hbm = pl.BlockSpec(memory_space=pl.ANY)
    table, qkv, square, up, down, head = weights
    return pl.pallas_call(
        lambda *refs: step_kernel(streams, groups, *refs),
        out_shape=(
            jax.ShapeDtypeStruct((sum(SECTIONS), 128), BF),
            jax.ShapeDtypeStruct((40, D), F32),
        ),
        in_specs=[hbm] + [pl.BlockSpec(memory_space=vmem)] * 3 + [hbm] * 6,
        out_specs=[hbm, pl.BlockSpec(memory_space=vmem)],
        scratch_shapes=[
            vmem((LAYERS + 1, toks, D), F32),
            vmem((LAYERS, toks, 1024), BF),
            vmem((LAYERS, toks, HK), BF),
            vmem((LAYERS, toks, D), F32),
            vmem((LAYERS, toks, D), F32),
            vmem((LAYERS, toks, FF), BF),
            vmem((LAYERS, toks, FF), BF),
            vmem((toks, D), BF),
            vmem((toks, D), BF),
            vmem((toks, D), BF),
            vmem((LAYERS, 3, HK, D), BF),
            vmem((seqs, STEPS, 128), F32),
            vmem((CHUNK * TOKS, D), F32),
            vmem((HCOLS, seqs * STEPS), BF),
            vmem((TROWS, D), BF),
            vmem((table.shape[0] % 128, D), F32),
            vmem(qkv.shape, BF),
            vmem(square.shape, BF),
            vmem(up.shape, BF),
            vmem(down.shape, BF),
            vmem(head.shape, BF),
            vmem(head.shape[::-1], BF),
            vmem(codes.shape, jnp.int32),
            vmem(codes.shape, BF),
            vmem((streams,) + codes.shape, BF),
            vmem((sum(SECTIONS), 128), BF),
            vmem((recv, 128), BF),
            vmem((own, 128), BF),
            vmem((stages + 1, 40, D), F32),
            vmem((stages, 3, 40, D), F32),
            dma((3 + 13 * LAYERS + 5,)),
            dma((2, streams - 1)),
            dma((len(plan), 2, 4, stages, 3)),
            dma((len(plan), 2)),
            dma((2, stages, 3)),
        ],
        compiler_params=pltpu.CompilerParams(
            collective_id=0, has_side_effects=True, vmem_limit_bytes=VMEM_LIMIT
        ),
        name="step",
    )(codes, seg, pos, small, table, qkv, square, up, down, head)


def update_pieces():
    pieces = []
    for k in range(LAYERS):
        layer = LAYERS - 1 - k
        base = 2560 + 6656 * k
        for half in range(2):
            r = 512 * half
            pieces.append(
                (4, (layer,), r, 512, [(base + 1024 * j + r, 128 * j) for j in range(2)])
            )
        pieces.append((3, (layer,), 0, 256, [(base + 2048 + 256 * j, 128 * j) for j in range(8)]))
        pieces.append((2, (layer, 0), 0, 256, [(base + 4096 + 256 * j, 128 * j) for j in range(2)]))
        pieces.append((2, (layer, 1), 0, 256, [(base + 4608 + 256 * j, 128 * j) for j in range(2)]))
        pieces.append((1, (layer,), 0, 256, [(base + 5120 + 256 * j, 128 * j) for j in range(6)]))
    pieces.append((6, (), 0, 256, [(256 * j, 128 * j) for j in range(10)]))
    base = 2560 + 6656 * LAYERS
    pieces.append((0, (), 0, 1280, [(base + 1280 * j, 128 * j) for j in range(2)]))
    return pieces


def update_kernel(clip_value, step_rate, *refs):
    g_ref, e_ref = refs[:2]
    ins = refs[2:23]
    stat_ref = refs[23]
    outs = refs[24:45]
    bufs = refs[45:66]
    isem, osem = refs[66:]
    pieces = update_pieces()
    table_rows = ins[0].shape[0]
    tail = table_rows - 1280

    def view(ref, piece):
        array, lead, first, rows, _ = piece
        if lead:
            ref = ref.at[lead]
        if ref.shape[0] == rows:
            return ref
        return ref.at[pl.ds(first, rows)]

    def transfer(kind, n, k, piece):
        src, dst = (ins, bufs) if kind == 0 else (bufs, outs)
        array = piece[0]
        sem = (isem, osem)[kind].at[k, n]
        return pltpu.make_async_copy(
            view(src[7 * k + array], piece), view(dst[7 * k + array], piece), sem
        )

    specials = [(0, (), 1280, tail, None), (5, (), 0, ins[5].shape[0], None)]
    order = specials + pieces
    for n, piece in enumerate(order):
        for k in range(3):
            transfer(0, n, k, piece).start()

    block = 128
    count = g_ref.shape[0] // block

    def gather(j, total):
        v = g_ref[pl.ds(pl.multiple_of(j * block, block), block)].astype(F32)
        return total + jnp.sum((v * v).reshape(block // 8, 8, 128), axis=0)

    total = lax.fori_loop(0, count, gather, jnp.zeros((8, 128), F32))
    rest = jnp.sum(e_ref[0:9] * e_ref[0:9]) + jnp.sum(e_ref[16:40] * e_ref[16:40])
    loss = jnp.max(e_ref[9:10])
    terms = jnp.max(e_ref[10:11])
    inverse = 1.0 / jnp.full((8, 128), terms, F32)
    norm = jnp.sqrt(jnp.full((8, 128), jnp.sum(total) + rest, F32)) * inverse
    factor = inverse * clip_value / jnp.maximum(norm, clip_value)
    stat_ref[0:8] = jnp.full((8, 128), loss, F32)
    stat_ref[8:16] = jnp.full((8, 128), terms, F32)
    stat_ref[16:24] = norm
    factor = factor[:1]

    def advance(views, rows, cols, gradient, scale):
        w, m, e = [v[rows, cols] for v in views]
        clipped = gradient * scale
        moment = MOMENTUM_RATE * m + clipped
        weight = w - step_rate * (clipped + MOMENTUM_RATE * moment)
        views[0][rows, cols] = weight
        views[1][rows, cols] = moment
        views[2][rows, cols] = AVERAGE_RATE * e + (1.0 - AVERAGE_RATE) * weight

    for n, piece in enumerate(order):
        array, lead, first, rows, blocks = piece
        for k in range(3):
            transfer(0, n, k, piece).wait()
        views = [bufs[7 * k + array].at[lead] if lead else bufs[7 * k + array] for k in range(3)]
        if blocks is None:
            at = 16 if array == 0 else 0
            wide = jnp.concatenate([factor, factor], axis=1)
            advance(
                views, slice(first, first + rows), slice(0, D), e_ref[at : at + rows], wide
            )
        else:
            step = 64

            @pl.loop(0, rows // step)
            def _(j):
                for source, column in blocks:
                    g = g_ref[pl.ds(pl.multiple_of(source + j * step, step), step)].astype(F32)
                    at = pl.ds(pl.multiple_of(first + j * step, step), step)
                    advance(views, at, slice(column, column + 128), g, factor)

        for k in range(3):
            transfer(1, n, k, piece).start()
    for n, piece in enumerate(order):
        for k in range(3):
            transfer(1, n, k, piece).wait()


def update_all(grads, extra, arrays, clip_value, step_rate):
    vmem = pltpu.VMEM
    count = len(update_pieces()) + 2
    hbm = pl.BlockSpec(memory_space=pl.ANY)
    results = pl.pallas_call(
        lambda *refs: update_kernel(clip_value, step_rate, *refs),
        out_shape=[jax.ShapeDtypeStruct((24, 128), F32)]
        + [jax.ShapeDtypeStruct(a.shape, F32) for a in arrays],
        in_specs=[pl.BlockSpec(memory_space=vmem)] * 2 + [hbm] * 21,
        out_specs=[pl.BlockSpec(memory_space=vmem)] + [hbm] * 21,
        scratch_shapes=[vmem(a.shape, F32) for a in arrays]
        + [pltpu.SemaphoreType.DMA((3, count)), pltpu.SemaphoreType.DMA((3, count))],
        compiler_params=pltpu.CompilerParams(vmem_limit_bytes=VMEM_LIMIT),
        name="update",
    )(grads, extra, *arrays)
    return results[0], results[1:]


def on_device(step_codes, segments, *arrays):
    streams = lax.axis_size("stream")
    groups = lax.axis_size("seq")
    group_seqs = step_codes.shape[0]
    table, qkv, square, up, down, small, head = arrays[:7]
    pos = jnp.asarray(position_rows()).astype(BF)
    grads, extra = run_step(
        step_codes.transpose(1, 2, 0),
        segments.T,
        pos,
        small,
        (table, qkv, square, up, down, head),
        streams,
        groups,
    )
    params_total = sum(w.size for w in arrays[:7])
    clip_value = CLIP_SCALE * (group_seqs * groups * STEPS) ** (-0.5)
    step_rate = STEP_SCALE * params_total**0.5 / clip_value
    stats, updated = update_all(grads, extra, arrays, clip_value, step_rate)
    return (stats[0, 0], stats[8, 0], stats[16, 0], *updated)


def solution(mesh):
    return jax.shard_map(
        on_device,
        mesh=mesh,
        in_specs=(P("seq", None, "stream"), P("seq", None)) + (P(),) * 21,
        out_specs=(P(),) * 24,
        check_vma=False,
    )
```

```python
import math

import jax
import jax.numpy as jnp
import numpy as np
from jax import lax
from jax.experimental import pallas as pl
from jax.experimental.pallas import tpu as pltpu
from jax.sharding import PartitionSpec as P

D = 256
HEADS = 8
HD = 32
FF = 1024
CATS = 32
CLASSES = 32
NA = 18
STEPS = 16
TOKS = 48
HK = HEADS * TOKS
LAYERS = 2
HCOLS = 1280
TROWS = 1408
CHUNK = 16
GROUP = 8
EPSILON = 1e-06
MOMENTUM_RATE = 0.9
AVERAGE_RATE = 0.7
CLIP_SCALE = 0.2
STEP_SCALE = 0.03
MASKED = -1e30
POSITION_SCALE = 0.5
SCALE = HD ** (-0.5)
BF = jnp.bfloat16
F32 = jnp.float32
VMEM_LIMIT = 63 * 1000 * 1000


def dot_nn(a, b):
    return lax.dot_general(a, b, (((1,), (0,)), ((), ())), preferred_element_type=F32)


def dot_nt(a, b):
    return lax.dot_general(a, b, (((1,), (1,)), ((), ())), preferred_element_type=F32)


def dot_tn(a, b):
    return lax.dot_general(a, b, (((0,), (0,)), ((), ())), preferred_element_type=F32)


def iota(shape, dim):
    return lax.broadcasted_iota(jnp.int32, shape, dim)


def position_rows():
    distance = np.arange(TOKS, dtype=np.float32)[:, None]
    rates = np.exp(np.arange(D // 2, dtype=np.float32) * np.float32(-2.0 * math.log(10000.0) / D))
    angle = (distance * rates[None, :].astype(np.float32)).astype(np.float32)
    table = np.float32(POSITION_SCALE) * np.concatenate([np.sin(angle), np.cos(angle)], axis=1)
    rows = np.zeros((3, TOKS, D), np.float32)
    for i in range(3):
        for j in range(3):
            for e in range(STEPS):
                d = 3 * (STEPS - 1 - e) + i - j
                if d >= 0:
                    rows[i, j * STEPS + e] = table[d]
    return rows.reshape(3 * TOKS, D)


def rms(values):
    return lax.rsqrt(jnp.mean(values * values, axis=-1, keepdims=True) + EPSILON)


def head_mask(h, rows):
    lane = iota((rows, 128), 1)
    low = (h % 4) * HD
    return ((lane >= low) & (lane < low + HD)).astype(F32).astype(BF)


def expand(rows):
    zero = jnp.zeros((TOKS, 128), BF)
    parts = []
    for h in range(HEADS):
        half = rows[:, 128 * (h // 4) : 128 * (h // 4) + 128] * head_mask(h, TOKS)
        parts.append(jnp.concatenate([half, zero] if h < 4 else [zero, half], axis=1))
    return jnp.concatenate(parts, axis=0)


def fold(values):
    lane = iota((TOKS, 128), 1)
    halves = []
    for g in range(2):
        total = None
        for h in range(4):
            part = values[(4 * g + h) * TOKS : (4 * g + h + 1) * TOKS, 128 * g : 128 * g + 128]
            total = part if total is None else jnp.where(lane >= h * HD, part, total)
        halves.append(total)
    return jnp.concatenate(halves, axis=1)


def spans(tile):
    found = []
    for h in range(HEADS):
        low, high = max(TOKS * h - 128 * tile, 0), min(TOKS * (h + 1) - 128 * tile, 128)
        if low < high:
            found.append((h, low, high))
    return found


def segment_max(scores):
    rows = scores.shape[0]
    lane = iota((rows, 128), 1)
    tiles = [scores[:, 128 * t : 128 * t + 128] for t in range(3)]
    best = {}
    for t in range(3):
        for h, low, high in spans(t):
            part = jnp.where((lane >= low) & (lane < high), tiles[t], -3e38)
            best[h] = part if h not in best else jnp.maximum(best[h], part)
    best = {h: jnp.max(v, axis=1, keepdims=True) for h, v in best.items()}
    outs = []
    for t in range(3):
        total = None
        for h, low, high in spans(t):
            wide = jnp.broadcast_to(best[h], (rows, 128))
            total = wide if total is None else jnp.where(lane >= low, wide, total)
        outs.append(total)
    return jnp.concatenate(outs, axis=1)


def unskew(values):
    row = iota((STEPS, HK), 0)
    values = jnp.concatenate(
        [pltpu.roll(values[:8], 15, 1), pltpu.roll(values[8:], 7, 1)], axis=0
    )
    for bit in (1, 2, 4):
        values = jnp.where((row & bit) > 0, pltpu.roll(values, HK - bit, 1), values)
    return values


SECTIONS = (2560, 4608, 2048, 4608, 4608)
DUE = ((1, 3, 5, 7, 9, 10), (3, 6, 8, 10), (7, 9, 11), (9, 12), ())


def stage_orders(streams, groups):
    rest, others = [], []
    step = 2
    while step < streams:
        rest.append(("stream", step))
        step *= 2
    step = 1
    while step < groups:
        others.append(("seq", step))
        step *= 2
    near = [tuple(others[:1] + rest)]
    far = [tuple(others[k : k + 2]) for k in range(1, len(others), 2)]
    core = [(("stream", 1),)]
    return [core + near + far, core + far + near]


def exchange_plan(streams, groups):
    unit = 16 * streams * groups
    sections = SECTIONS
    if any(s % unit or s < 2 * unit for s in sections):
        sections = (sum(SECTIONS),)
    orders = stage_orders(streams, groups)
    plan, base, recv, own = [], 0, 0, 0
    for rows in sections:
        units = rows // unit
        last = max(1, round(0.222 * units))
        lanes = []
        for part, order in zip((units - last, last), orders):
            size, sizes, slots = part * unit, [], []
            for bits in order:
                size //= 2 ** len(bits)
                sizes.append(size)
                slots.append(recv)
                recv += size * (2 ** len(bits) - 1)
            lanes.append(dict(base=base, order=order, sizes=sizes, slots=slots, own=own))
            own += size
            base += part * unit
        plan.append(lanes)
    assert base == sum(SECTIONS)
    return plan, recv, own


def place_of(bit):
    axis, step = bit
    return (lax.axis_index(axis) // step) % 2


def flips_of(bits):
    count = len(bits)
    return [tuple((n >> k) % 2 for k in range(count)) for n in range(1, 2**count)]


def partner_of(bits, flips):
    place = {"stream": lax.axis_index("stream"), "seq": lax.axis_index("seq")}
    for bit, flip in zip(bits, flips):
        if flip:
            axis, step = bit
            place[axis] = place[axis] + step * (1 - 2 * place_of(bit))
    return (place["stream"], place["seq"])


def share_of(bits, flips):
    total = 0
    for bit, flip in zip(bits, flips):
        mine = place_of(bit)
        total = 2 * total + ((1 - mine) if flip else mine)
    return total


class Lane:
    def __init__(self, spec, refs, sems, own_sem):
        self.spec, self.sems, self.own_sem = spec, sems, own_sem
        self.g, self.out, self.recv, self.own = refs
        offset = spec["base"]
        self.keep, self.send = [], []
        for bits, size in zip(spec["order"], spec["sizes"]):
            self.send.append(
                [
                    pl.multiple_of(offset + share_of(bits, flips) * size, 16)
                    for flips in flips_of(bits)
                ]
            )
            offset = pl.multiple_of(offset + share_of(bits, (0,) * len(bits)) * size, 16)
            self.keep.append(offset)

    def remote(self, kind, i, n, src, dst):
        bits = self.spec["order"][i]
        return pltpu.make_async_remote_copy(
            src_ref=src,
            dst_ref=dst,
            send_sem=self.sems.at[2 * kind, i, n],
            recv_sem=self.sems.at[2 * kind + 1, i, n],
            device_id=partner_of(bits, flips_of(bits)[n]),
            device_id_type=pl.DeviceIdType.MESH,
        )

    def scatter(self, i):
        size, slot = self.spec["sizes"][i], self.spec["slots"][i]
        return [
            self.remote(
                0, i, n, self.g.at[pl.ds(at, size)], self.recv.at[pl.ds(slot + n * size, size)]
            )
            for n, at in enumerate(self.send[i])
        ]

    def mine(self):
        return self.own.at[pl.ds(self.spec["own"], self.spec["sizes"][-1])]

    def keep_copy(self):
        rows = pl.ds(self.keep[-1], self.spec["sizes"][-1])
        return pltpu.make_async_copy(self.mine(), self.out.at[rows], self.own_sem)

    def gather(self, i):
        rows = pl.ds(self.keep[i], self.spec["sizes"][i])
        last = i + 1 == len(self.keep)
        return [
            self.remote(1, i, n, self.mine() if last else self.out.at[rows], self.out.at[rows])
            for n in range(len(self.send[i]))
        ]

    def add(self, i):
        size, slot = self.spec["sizes"][i], self.spec["slots"][i]
        last = i + 1 == len(self.keep)
        block = 256
        while size % block:
            block //= 2

        @pl.loop(0, size // block)
        def _(j):
            at = pl.ds(pl.multiple_of(self.keep[i] + j * block, 16), block)
            value = self.g[at].astype(F32)
            for n in range(len(self.send[i])):
                got = pl.ds(pl.multiple_of(slot + n * size + j * block, 16), block)
                value = value + self.recv[got].astype(F32)
            if last:
                own = pl.multiple_of(self.spec["own"] + j * block, 16)
                self.own[pl.ds(own, block)] = value.astype(BF)
            else:
                self.g[at] = value.astype(BF)


def start_all(copies):
    for copy in copies:
        copy.start()


def wait_all(copies):
    for copy in copies:
        copy.wait()


class Exchange:
    def __init__(self, streams, groups, g_ref, out_ref, recv_ref, own_ref, sems, own_sems):
        plan, _, _ = exchange_plan(streams, groups)
        refs = (g_ref, out_ref, recv_ref, own_ref)
        self.sections = [
            [
                Lane(spec, refs, sems.at[n, k], own_sems.at[n, k])
                for k, spec in enumerate(lanes)
            ]
            for n, lanes in enumerate(plan)
        ]
        self.order = plan[0][0]["order"]
        self.stages = len(self.order)
        self.active = []
        self.moment = 0

    def open(self, n):
        if len(self.sections) > 1:
            for lane in self.sections[n]:
                start_all(lane.scatter(0))
            self.active.append([n, 0])

    def advance(self, n, stage):
        stages = self.stages
        for lane in self.sections[n]:
            if stage < stages:
                wait_all(lane.scatter(stage))
                lane.add(stage)
                if stage + 1 < stages:
                    start_all(lane.scatter(stage + 1))
                else:
                    start_all(lane.gather(stage))
                    lane.keep_copy().start()
            else:
                i = 2 * stages - 1 - stage
                wait_all(lane.gather(i))
                if i + 1 == stages:
                    lane.keep_copy().wait()
                if i:
                    start_all(lane.gather(i - 1))

    def plan(self, count):
        moments = []
        for _ in range(count):
            self.moment += 1
            ready = [
                item
                for item in self.active
                if item[1] < len(DUE[item[0]]) and DUE[item[0]][item[1]] <= self.moment
            ]
            moments.append(self.step(ready))
        return moments

    def step(self, items):
        taken = [tuple(item) for item in items]
        for item in items:
            item[1] += 1
        self.active = [item for item in self.active if item[1] < 2 * self.stages]
        return taken

    def emit(self, moment):
        for n, stage in moment:
            self.advance(n, stage)

    def tick(self):
        self.emit(self.plan(1)[0])

    def when(self, condition, moment):
        if moment:
            pl.when(condition)(lambda: self.emit(moment))

    def finish(self, slot_ref, got_ref, sems, total_ref):
        last = len(self.sections) - 1

        def extra(i):
            bits = self.order[i]
            return [
                pltpu.make_async_remote_copy(
                    src_ref=slot_ref.at[i],
                    dst_ref=got_ref.at[i, n],
                    send_sem=sems.at[0, i, n],
                    recv_sem=sems.at[1, i, n],
                    device_id=partner_of(bits, flips),
                    device_id_type=pl.DeviceIdType.MESH,
                )
                for n, flips in enumerate(flips_of(bits))
            ]

        for lane in self.sections[last]:
            start_all(lane.scatter(0))
        start_all(extra(0))
        self.active.append([last, 0])
        i = 0
        while self.active:
            self.emit(self.step(list(self.active)))
            if i < self.stages:
                wait_all(extra(i))
                slot_ref[i + 1] = self.total(slot_ref[i], got_ref, i)
                if i + 1 < self.stages:
                    start_all(extra(i + 1))
            i += 1
        total_ref[...] = slot_ref[self.stages]

    def total(self, mine, got_ref, i):
        bits = self.order[i]
        if len(bits) == 1:
            return mine + got_ref[i, 0]
        return (mine + got_ref[i, 0]) + (got_ref[i, 1] + got_ref[i, 2])

def step_kernel(
    streams,
    groups,
    codes_hbm,
    seg_ref,
    pos_ref,
    small_ref,
    table_hbm,
    qkv_hbm,
    square_hbm,
    up_hbm,
    down_hbm,
    head_hbm,
    out_hbm,
    total_ref,
    x_s,
    att_s,
    pu_s,
    o_s,
    mid_s,
    hb_s,
    gp_s,
    b_s,
    dyl_s,
    dml_s,
    rk_s,
    start_s,
    l_s,
    slope_s,
    table_s,
    tail_s,
    wqkv_s,
    wsq_s,
    wup_s,
    wdown_s,
    whead_s,
    wheadt_s,
    raw_s,
    send_s,
    got_codes_s,
    g_s,
    recv_s,
    own_s,
    slot_s,
    got_s,
    load_sems,
    code_sems,
    sems,
    own_sems,
    extra_sems,
):
    toks = x_s.shape[1]
    seqs = toks // TOKS
    steps_all = seqs * STEPS
    chunks = seqs // CHUNK
    rows_c = CHUNK * TOKS
    me = lax.axis_index("stream")
    table_rows = table_hbm.shape[0]

    raw_load = pltpu.make_async_copy(codes_hbm, raw_s, load_sems.at[0])
    raw_load.start()
    whole = table_rows // 128 * 128
    rest = table_rows - whole
    loads = []

    def load(src, place, targets):
        copy = pltpu.make_async_copy(src, place, load_sems.at[len(loads) + 1])
        loads.append((copy, place, targets))

    table_rows_main = pl.ds(0, whole)
    load(
        table_hbm.at[table_rows_main],
        x_s.at[2, table_rows_main],
        [(table_s.at[table_rows_main], False)],
    )
    load(table_hbm.at[pl.ds(whole, rest)], tail_s, None)
    for layer in range(LAYERS):
        places = [o_s.at[layer, pl.ds(256 * j, 256)] for j in range(6)]
        places += [mid_s.at[layer, pl.ds(256 * j, 256)] for j in range(6)]
        places += [x_s.at[1, pl.ds(256 * layer, 256)]]
        places = iter(places)
        for j in range(3):
            cols = pl.ds(256 * j, 256)
            load(qkv_hbm.at[layer, :, cols], next(places), [(wqkv_s.at[layer, :, cols], False)])
        for j in range(2):
            load(square_hbm.at[layer, j], next(places), [(wsq_s.at[layer, j], False)])
        for j in range(4):
            cols = pl.ds(256 * j, 256)
            load(up_hbm.at[layer, :, cols], next(places), [(wup_s.at[layer, :, cols], False)])
        for j in range(4):
            cols = pl.ds(256 * j, 256)
            load(down_hbm.at[layer, cols], next(places), [(wdown_s.at[layer, cols], False)])
    for j in range(HCOLS // 256):
        cols = pl.ds(256 * j, 256)
        load(
            head_hbm.at[:, cols],
            x_s.at[1, pl.ds(512 + 256 * j, 256)] if j < 4 else l_s.at[pl.ds(0, 256)],
            [(whead_s.at[:, cols], False), (wheadt_s.at[cols], True)],
        )
    for copy, _, _ in loads:
        copy.start()

    comm = Exchange(streams, groups, g_s, out_hbm, recv_s, own_s, sems, own_sems)
    barrier = pltpu.get_barrier_semaphore()
    greeted = [((me + j) % streams, lax.axis_index("seq")) for j in range(1, streams)]
    peers = list(greeted)
    for bits in comm.order:
        for flips in flips_of(bits):
            if any(flip and bit[0] == "seq" for bit, flip in zip(bits, flips)):
                greeted.append(partner_of(bits, flips))
    for peer in greeted:
        pl.semaphore_signal(
            barrier, inc=1, device_id=peer, device_id_type=pl.DeviceIdType.MESH
        )

    raw_load.wait()
    send_s[...] = raw_s[...].astype(F32).astype(BF)
    pl.semaphore_wait(barrier, len(greeted))
    sends = []
    for j, peer in enumerate(peers):
        sends.append(
            pltpu.make_async_remote_copy(
                src_ref=send_s,
                dst_ref=got_codes_s.at[me],
                send_sem=code_sems.at[0, j],
                recv_sem=code_sems.at[1, j],
                device_id=peer,
                device_id_type=pl.DeviceIdType.MESH,
            )
        )
        sends[-1].start()
    got_codes_s[me] = send_s[...]

    group = seg_ref.shape[1]
    step_lane = iota((STEPS, steps_all), 1) % STEPS
    step_row = iota((STEPS, steps_all), 0)
    own_lane = iota((group, steps_all), 1) // STEPS + me * seqs
    pick = (iota((group, steps_all), 0) == own_lane).astype(F32).astype(BF)
    seg = dot_nn(seg_ref[...].astype(F32).astype(BF), pick)
    seg_own = jnp.sum(jnp.where(step_row == step_lane, seg, 0.0), axis=0, keepdims=True)
    start = jnp.sum(jnp.where(seg < seg_own, 1.0, 0.0), axis=0, keepdims=True)
    valid_row = jnp.sum(
        jnp.where((step_row == step_lane + 1) & (seg == seg_own), 1.0, 0.0), axis=0, keepdims=True
    )
    start_low = jnp.broadcast_to(start, (STEPS, steps_all)).astype(BF)
    one_row = (iota((STEPS, 128), 0) == 0).astype(F32).astype(BF)
    start_s[...] = dot_tn(start_low, one_row).reshape(seqs, STEPS, 128)

    table_s[whole:] = jnp.zeros((TROWS - whole, D), BF)
    for copy, place, targets in loads:
        copy.wait()
        if targets is None:
            pad = -rest % 16
            table_s[whole : whole + rest + pad] = jnp.concatenate(
                [place[...], jnp.zeros((pad, D), F32)], axis=0
            ).astype(BF)
            continue
        for target, turned in targets:
            target[...] = (place[...].T if turned else place[...]).astype(BF)
    for copy in sends:
        copy.wait()
    codes = []
    for k in range(4):
        wide = dot_nn(got_codes_s[k].reshape(STEPS * STEPS, group), pick)
        wide = wide.reshape(STEPS, STEPS, steps_all)
        at_step = iota((STEPS, STEPS, steps_all), 0) == iota((STEPS, STEPS, steps_all), 2) % STEPS
        codes.append(jnp.sum(jnp.where(at_step, wide, 0.0), axis=0).astype(BF))

    spread = (iota((STEPS, 512), 1) // CLASSES == iota((STEPS, 512), 0)).astype(F32).astype(BF)
    first = (iota((STEPS, 384), 0) == 0).astype(F32).astype(BF)
    class_lane = (iota((128, 512), 1) % CLASSES).astype(F32)
    lane = iota((128, 384), 1).astype(F32)
    for c in range(steps_all // 128):
        cols = slice(128 * c, 128 * c + 128)
        halves = []
        for k in range(2):
            hot = (dot_tn(codes[k][:, cols], spread) == class_lane).astype(F32).astype(BF)
            piece = dot_nn(hot, table_s[512 * k : 512 * k + 512]).astype(BF).astype(F32)
            halves.append(piece)
        hot = (dot_tn(codes[2][:, cols], first[:, :128]) == lane[:, :128]).astype(F32).astype(BF)
        action = dot_nn(hot, table_s[1024:1152]).astype(BF).astype(F32)
        hot = (dot_tn(codes[3][:, cols], first) + NA == lane).astype(F32).astype(BF)
        reward = dot_nn(hot, table_s[1024:1408]).astype(BF).astype(F32)
        pieces = [p.reshape(8, 1, STEPS, D) for p in (halves[0] + halves[1], action, reward)]
        x_s[0, 384 * c : 384 * c + 384] = jnp.concatenate(pieces, axis=1).reshape(384, D)
    for layer in range(LAYERS):
        rk = dot_nn(pos_ref[...], wsq_s[layer, 1]).astype(BF)
        for k in range(3):
            rk_s[layer, k] = expand(rk[TOKS * k : TOKS * k + TOKS])

    lane_hk = iota((TOKS, HK), 1) % TOKS
    key_step = lane_hk % STEPS
    key_time = 3 * key_step + lane_hk // STEPS
    row_tok = iota((TOKS, HK), 0)
    query_time = 3 * (row_tok % STEPS) + row_tok // STEPS
    causal = key_time <= query_time
    key_step_f = key_step.astype(F32)
    sum_hd = (iota((HK, D), 0) // TOKS == iota((HK, D), 1) // HD).astype(F32).astype(BF)
    sum_hk = (iota((D, HK), 0) // HD == iota((D, HK), 1) // TOKS).astype(F32).astype(BF)

    for layer in range(LAYERS):
        gain_a = small_ref[4 * layer : 4 * layer + 1]
        gain_b = small_ref[4 * layer + 1 : 4 * layer + 2]
        bias_u = small_ref[4 * layer + 2 : 4 * layer + 3]
        bias_v = small_ref[4 * layer + 3 : 4 * layer + 4]

        @pl.loop(0, chunks)
        def _(c):
            rows = pl.ds(pl.multiple_of(c * rows_c, rows_c), rows_c)
            x = x_s[layer, rows]
            low = (x * rms(x) * gain_a).astype(BF)
            q = dot_nn(low, wqkv_s[layer, :, :256]).astype(BF).astype(F32)
            qu = (q + bias_u).astype(BF)
            qv = (q + bias_v).astype(BF)
            key = dot_nn(low, wqkv_s[layer, :, 256:512]).astype(BF)
            val = dot_nn(low, wqkv_s[layer, :, 512:]).astype(BF)
            att_s[layer, rows, 0:256] = qu
            att_s[layer, rows, 256:512] = qv
            att_s[layer, rows, 512:768] = key
            att_s[layer, rows, 768:1024] = val
            qv4 = qv.reshape(CHUNK, 3, STEPS, D)
            place = [
                dot_nt(qv4[:, k].reshape(CHUNK * STEPS, D), rk_s[layer, k]) for k in range(3)
            ]
            start_c = start_s[pl.ds(c * CHUNK, CHUNK)]
            for g in range(0, CHUNK, GROUP):
                members = range(g, g + GROUP)
                spans = {b: slice(TOKS * b, TOKS * b + TOKS) for b in members}
                scores = {b: dot_nt(qu[spans[b]], expand(key[spans[b]])) for b in members}
                for b in members:
                    shifted = [
                        pltpu.roll(
                            place[k][STEPS * b : STEPS * b + STEPS],
                            HK - (STEPS - 1),
                            1,
                            stride=1,
                            stride_axis=0,
                        )
                        for k in range(3)
                    ]
                    begin = jnp.concatenate([start_c[b]] * 3, axis=0)
                    begin = jnp.concatenate([begin] * 3, axis=1)
                    score = (scores[b] + jnp.concatenate(shifted, axis=0)) * SCALE
                    scores[b] = jnp.where(causal & (key_step_f >= begin), score, MASKED)
                tops = {b: segment_max(scores[b]) for b in members}
                probs = {b: jnp.exp(scores[b] - tops[b]).astype(BF) for b in members}
                for b in members:
                    l_s[spans[b]] = dot_nn(probs[b], expand(val[spans[b]]))
                for b in members:
                    pu_s[layer, pl.ds(pl.multiple_of(c * rows_c + TOKS * b, TOKS), TOKS)] = probs[b]
            recip = 1.0 / dot_nn(pu_s[layer, rows], sum_hd)
            out = l_s[...] * recip
            o_s[layer, rows] = out
            mid = x + dot_nn(out.astype(BF), wsq_s[layer, 0])
            mid_s[layer, rows] = mid
            low = (mid * rms(mid) * gain_b).astype(BF)
            for j in range(FF // 256):
                cols = slice(256 * j, 256 * j + 256)
                inner = dot_nn(low, wup_s[layer, :, cols])
                square = inner * inner
                c0 = math.sqrt(2.0 / math.pi)
                tanh = jnp.tanh(c0 * inner * (1.0 + 0.044715 * square))
                half = 0.5 * (1.0 + tanh)
                hb_s[layer, rows, cols] = (inner * half).astype(BF)
                gp_s[layer, rows, cols] = (
                    half
                    + (0.5 * c0) * inner * (1.0 - tanh * tanh) * (1.0 + (3 * 0.044715) * square)
                ).astype(BF)
            nxt = mid + dot_nn(hb_s[layer, rows], wdown_s[layer])
            x_s[layer + 1, rows] = nxt

    gain_f = small_ref[4 * LAYERS : 4 * LAYERS + 1]
    xf = x_s[LAYERS].reshape(seqs, 3, STEPS, D)[:, 1].reshape(steps_all, D)
    feat = (xf * rms(xf) * gain_f).astype(BF)
    spread_t = (iota((512, STEPS), 0) // CLASSES == iota((512, STEPS), 1)).astype(F32).astype(BF)
    class_row = iota((4, CLASSES, steps_all), 1).astype(F32)
    loss = jnp.zeros((4, steps_all), F32)
    for k in range(2):
        follow_codes = pltpu.roll(codes[k].astype(F32), steps_all - 1, 1).astype(BF)
        for j in range(4):
            base = 512 * k + 128 * j
            logits = dot_nt(wheadt_s[base : base + 128], feat).reshape(4, CLASSES, steps_all)
            target = dot_nn(spread_t[128 * j : 128 * j + 128], follow_codes)
            hot = target.reshape(4, CLASSES, steps_all) == class_row
            top = jnp.max(logits, axis=1, keepdims=True)
            grown = jnp.exp(logits - top)
            total = jnp.sum(grown, axis=1, keepdims=True)
            picked = jnp.sum(jnp.where(hot, logits, 0.0), axis=1)
            loss = loss + valid_row * (jnp.log(total[:, 0]) + top[:, 0] - picked)
            slope = (grown * (1.0 / total) - jnp.where(hot, 1.0, 0.0)) * valid_row[None]
            slope_s[base : base + 128] = slope.reshape(128, steps_all).astype(BF)
    action_row = codes[2][0:1].astype(F32)
    discount_row = codes[2][1:2].astype(F32)
    reward_row = codes[3][0:1].astype(F32)
    logits = dot_nt(wheadt_s[1024:1280], feat)
    row = iota((256, steps_all), 0)
    hot = row == (reward_row + 1.0).astype(jnp.int32)
    disc = logits[:1]
    masked = jnp.where(row == 0, -3e38, logits)
    top = jnp.max(masked, axis=0, keepdims=True)
    grown = jnp.exp(masked - top)
    total = jnp.sum(grown, axis=0, keepdims=True)
    picked = jnp.sum(jnp.where(hot, logits, 0.0), axis=0, keepdims=True)
    fade = jnp.exp(-jnp.abs(disc))
    soft = jnp.maximum(disc, 0.0) + jnp.log(1.0 + fade)
    sigm = jnp.where(disc >= 0.0, 1.0, fade) / (1.0 + fade)
    loss_row = (
        jnp.sum(loss, axis=0, keepdims=True)
        + jnp.log(total)
        + top
        - picked
        + soft
        - discount_row * disc
    )
    slope = grown * (1.0 / total) - jnp.where(hot, 1.0, 0.0)
    slope = jnp.where(row == 0, sigm - discount_row, slope)
    slope_s[1024:1280] = slope.astype(BF)
    loss_sum = jnp.sum(loss_row)
    count = jnp.sum(valid_row) * CATS + 2.0 * steps_all
    slot_s[0, 9:10] = jnp.full((1, D), loss_sum, F32)
    slot_s[0, 10:11] = jnp.full((1, D), count, F32)
    slot_s[0, 11:16] = jnp.zeros((5, D), F32)

    feat_t = feat.astype(F32).T.astype(BF)
    for j in range(5):
        part = dot_nt(feat_t, slope_s[256 * j : 256 * j + 256])
        for k in range(2):
            base = 256 * (2 * j + k)
            g_s[base : base + 256] = part[:, 128 * k : 128 * k + 128].astype(BF)
    comm.open(0)
    dfeat = dot_nn(whead_s[...], slope_s[...]).T
    scale_f = rms(xf)
    hat = xf * scale_f
    slot_s[0, 8:9] = jnp.sum(dfeat * hat, axis=0, keepdims=True)
    inner = dfeat * gain_f
    dxf = scale_f * (inner - hat * jnp.mean(inner * hat, axis=-1, keepdims=True))
    gap = jnp.zeros((seqs, 1, STEPS, D), F32)
    x_s[LAYERS] = jnp.concatenate([gap, dxf.reshape(seqs, 1, STEPS, D), gap], axis=1).reshape(
        toks, D
    )

    for layer in reversed(range(LAYERS)):
        gain_a = small_ref[4 * layer : 4 * layer + 1]
        gain_b = small_ref[4 * layer + 1 : 4 * layer + 2]
        slot_s[0, 4 * layer : 4 * layer + 4] = jnp.zeros((4, D), F32)

        moments = comm.plan(chunks - 1)

        @pl.loop(0, chunks)
        def _(c):
            rows = pl.ds(pl.multiple_of(c * rows_c, rows_c), rows_c)
            for k in range(1, chunks):
                comm.when(c == k, moments[k - 1])
            dy = x_s[LAYERS, rows]
            dyl = dy.astype(BF)
            dyl_s[rows] = dyl
            for j in range(FF // 256):
                cols = slice(256 * j, 256 * j + 256)
                dact = dot_nt(dyl, wdown_s[layer, cols])
                gp_s[layer, rows, cols] = (dact * gp_s[layer, rows, cols].astype(F32)).astype(BF)
            dlow = dot_nt(gp_s[layer, rows], wup_s[layer])
            mid = mid_s[layer, rows]
            scale = rms(mid)
            hat = mid * scale
            b_s[rows] = (hat * gain_b).astype(BF)
            dgain = jnp.sum(dlow * hat, axis=0, keepdims=True)
            inner = dlow * gain_b
            dmid = scale * (inner - hat * jnp.mean(inner * hat, axis=-1, keepdims=True)) + dy
            slot_s[0, 4 * layer + 1 : 4 * layer + 2] += dgain
            mid_s[layer, rows] = dmid
            dml_s[rows] = dmid.astype(BF)

        base = 2560 + 6656 * (LAYERS - 1 - layer)

        def put(offset, value, base=base):
            size = value.shape[0]
            for k in range(2):
                at = base + offset + k * size
                g_s[at : at + size] = value[:, 128 * k : 128 * k + 128].astype(BF)

        comm.tick()
        for j in range(4):
            part = dot_tn(hb_s[layer, :, 256 * j : 256 * j + 256], dyl_s[...])
            for k in range(2):
                at = base + 1024 * k + 256 * j
                g_s[at : at + 256] = part[:, 128 * k : 128 * k + 128].astype(BF)
        for j in range(4):
            put(2048 + 512 * j, dot_tn(b_s[...], gp_s[layer, :, 256 * j : 256 * j + 256]))
        put(4096, dot_tn(o_s[layer].astype(BF), dml_s[...]))
        comm.open(1 + 2 * (LAYERS - 1 - layer))
        moments = comm.plan(seqs // GROUP - 1)
        rows_a = GROUP * TOKS

        @pl.loop(0, seqs // GROUP)
        def _(c):
            rows = pl.ds(pl.multiple_of(c * rows_a, rows_a), rows_a)
            for k in range(1, seqs // GROUP):
                comm.when(c == k, moments[k - 1])
            dmid = mid_s[layer, rows]
            dml = dml_s[rows]
            recip = 1.0 / dot_nn(pu_s[layer, rows], sum_hd)
            do = dot_nt(dml, wsq_s[layer, 0]).astype(BF).astype(F32)
            do = (do * recip).astype(BF)
            mass = do.astype(F32) * o_s[layer, rows]
            mass_hi = mass.astype(BF)
            mass_lo = (mass - mass_hi.astype(F32)).astype(BF)
            delta = dot_nn(mass_hi, sum_hk) + dot_nn(mass_lo, sum_hk)
            qu = att_s[layer, rows, 0:256]
            key = att_s[layer, rows, 512:768]
            val = att_s[layer, rows, 768:1024]
            probs_all = pu_s[layer, rows]
            draws = {}
            for g in range(1):
                members = range(g, g + GROUP)
                spans = {b: slice(TOKS * b, TOKS * b + TOKS) for b in members}
                dprob = {b: dot_nt(do[spans[b]], expand(val[spans[b]])) for b in members}
                dval = {b: dot_tn(probs_all[spans[b]], do[spans[b]]) for b in members}
                dscore = {
                    b: (probs_all[spans[b]].astype(F32) * (dprob[b] - delta[spans[b]])).astype(BF)
                    for b in members
                }
                dkey = {b: dot_tn(dscore[b], qu[spans[b]]) for b in members}
                dque = {b: dot_nn(dscore[b], expand(key[spans[b]])) for b in members}
                for b in members:
                    wide = dscore[b].astype(F32)
                    draws[b] = [
                        unskew(wide[STEPS * k : STEPS * k + STEPS]).astype(BF) for k in range(3)
                    ]
                for b in members:
                    l_s[spans[b]] = dque[b] * SCALE
                for b in members:
                    out_rows = pl.ds(pl.multiple_of(c * rows_a + TOKS * b, TOKS), TOKS)
                    att_s[layer, out_rows, 512:768] = (fold(dkey[b]) * SCALE).astype(BF)
                    att_s[layer, out_rows, 768:1024] = fold(dval[b]).astype(BF)
                    pu_s[layer, out_rows] = jnp.concatenate(draws[b], axis=0)
            dqv = [
                dot_nn(
                    jnp.concatenate([draws[b][k] for b in range(GROUP)], axis=0), rk_s[layer, k]
                ).reshape(GROUP, 1, STEPS, D)
                for k in range(3)
            ]
            dqv = jnp.concatenate(dqv, axis=1).reshape(rows_a, D) * SCALE
            dqu = l_s[0:rows_a]
            slot_s[0, 4 * layer + 2 : 4 * layer + 3] += jnp.sum(dqu, axis=0, keepdims=True)
            slot_s[0, 4 * layer + 3 : 4 * layer + 4] += jnp.sum(dqv, axis=0, keepdims=True)
            dq = (dqu + dqv).astype(BF)
            att_s[layer, rows, 0:256] = dq
            dlow = (
                dot_nt(dq, wqkv_s[layer, :, :256])
                + dot_nt(att_s[layer, rows, 512:768], wqkv_s[layer, :, 256:512])
                + dot_nt(att_s[layer, rows, 768:1024], wqkv_s[layer, :, 512:])
            )
            x = x_s[layer, rows]
            scale = rms(x)
            hat = x * scale
            dyl_s[rows] = (hat * gain_a).astype(BF)
            slot_s[0, 4 * layer : 4 * layer + 1] += jnp.sum(dlow * hat, axis=0, keepdims=True)
            inner = dlow * gain_a
            dx = scale * (inner - hat * jnp.mean(inner * hat, axis=-1, keepdims=True)) + dmid
            x_s[LAYERS, rows] = dx

        comm.tick()
        drk = []
        draw = pu_s[layer].reshape(seqs, 3, STEPS, HK)
        qv = att_s[layer, :, 256:512].reshape(seqs, 3, STEPS, D)
        for k in range(3):
            wide = dot_tn(
                draw[:, k].reshape(steps_all, HK), qv[:, k].reshape(steps_all, D)
            )
            drk.append(fold(wide) * SCALE)
        put(4608, dot_tn(pos_ref[...], jnp.concatenate(drk, axis=0).astype(BF)))
        put(5120, dot_tn(dyl_s[...], att_s[layer, :, 0:256]))
        put(5632, dot_tn(dyl_s[...], att_s[layer, :, 512:768]))
        put(6144, dot_tn(dyl_s[...], att_s[layer, :, 768:1024]))
        if layer:
            comm.open(2 * (LAYERS - layer))

    dtok = x_s[LAYERS].reshape(seqs, 3, STEPS, D).astype(BF)
    dtok = [dtok[:, k].reshape(steps_all, D) for k in range(3)]
    base = 2560 + 6656 * LAYERS
    class_row = (iota((256, steps_all), 0) % CLASSES).astype(F32)
    for k in range(2):
        for j in range(2):
            wide = dot_nn(spread_t[256 * j : 256 * j + 256], codes[k])
            hot = (wide == class_row).astype(F32).astype(BF)
            part = dot_nn(hot, dtok[0])
            for h in range(2):
                at = base + 1280 * h + 512 * k + 256 * j
                g_s[at : at + 256] = part[:, 128 * h : 128 * h + 128].astype(BF)
    row = iota((288, steps_all), 0)
    hot_a = (row == action_row.astype(jnp.int32)).astype(F32).astype(BF)
    hot_r = (row == (reward_row + NA).astype(jnp.int32)).astype(F32).astype(BF)
    part = dot_nn(hot_a, dtok[1]) + dot_nn(hot_r, dtok[2])
    for h in range(2):
        at = base + 1280 * h + 1024
        g_s[at : at + 256] = part[:256, 128 * h : 128 * h + 128].astype(BF)
    slot_s[0, 16:40] = part[256:280]
    comm.finish(slot_s, got_s, extra_sems, total_ref)


def run_step(codes, seg, pos, small, weights, streams, groups):
    seqs = codes.shape[2] // streams
    toks = seqs * TOKS
    plan, recv, own = exchange_plan(streams, groups)
    stages = len(plan[0][0]["order"])
    vmem, dma = pltpu.VMEM, pltpu.SemaphoreType.DMA
    hbm = pl.BlockSpec(memory_space=pl.ANY)
    table, qkv, square, up, down, head = weights
    return pl.pallas_call(
        lambda *refs: step_kernel(streams, groups, *refs),
        out_shape=(
            jax.ShapeDtypeStruct((sum(SECTIONS), 128), BF),
            jax.ShapeDtypeStruct((40, D), F32),
        ),
        in_specs=[hbm] + [pl.BlockSpec(memory_space=vmem)] * 3 + [hbm] * 6,
        out_specs=[hbm, pl.BlockSpec(memory_space=vmem)],
        scratch_shapes=[
            vmem((LAYERS + 1, toks, D), F32),
            vmem((LAYERS, toks, 1024), BF),
            vmem((LAYERS, toks, HK), BF),
            vmem((LAYERS, toks, D), F32),
            vmem((LAYERS, toks, D), F32),
            vmem((LAYERS, toks, FF), BF),
            vmem((LAYERS, toks, FF), BF),
            vmem((toks, D), BF),
            vmem((toks, D), BF),
            vmem((toks, D), BF),
            vmem((LAYERS, 3, HK, D), BF),
            vmem((seqs, STEPS, 128), F32),
            vmem((CHUNK * TOKS, D), F32),
            vmem((HCOLS, seqs * STEPS), BF),
            vmem((TROWS, D), BF),
            vmem((table.shape[0] % 128, D), F32),
            vmem(qkv.shape, BF),
            vmem(square.shape, BF),
            vmem(up.shape, BF),
            vmem(down.shape, BF),
            vmem(head.shape, BF),
            vmem(head.shape[::-1], BF),
            vmem(codes.shape, jnp.int32),
            vmem(codes.shape, BF),
            vmem((streams,) + codes.shape, BF),
            vmem((sum(SECTIONS), 128), BF),
            vmem((recv, 128), BF),
            vmem((own, 128), BF),
            vmem((stages + 1, 40, D), F32),
            vmem((stages, 3, 40, D), F32),
            dma((3 + 13 * LAYERS + 5,)),
            dma((2, streams - 1)),
            dma((len(plan), 2, 4, stages, 3)),
            dma((len(plan), 2)),
            dma((2, stages, 3)),
        ],
        compiler_params=pltpu.CompilerParams(
            collective_id=0, has_side_effects=True, vmem_limit_bytes=VMEM_LIMIT
        ),
        name="step",
    )(codes, seg, pos, small, table, qkv, square, up, down, head)


def update_pieces():
    pieces = []
    for k in range(LAYERS):
        layer = LAYERS - 1 - k
        base = 2560 + 6656 * k
        for half in range(2):
            r = 512 * half
            pieces.append(
                (4, (layer,), r, 512, [(base + 1024 * j + r, 128 * j) for j in range(2)])
            )
        pieces.append((3, (layer,), 0, 256, [(base + 2048 + 256 * j, 128 * j) for j in range(8)]))
        pieces.append((2, (layer, 0), 0, 256, [(base + 4096 + 256 * j, 128 * j) for j in range(2)]))
        pieces.append((2, (layer, 1), 0, 256, [(base + 4608 + 256 * j, 128 * j) for j in range(2)]))
        pieces.append((1, (layer,), 0, 256, [(base + 5120 + 256 * j, 128 * j) for j in range(6)]))
    pieces.append((6, (), 0, 256, [(256 * j, 128 * j) for j in range(10)]))
    base = 2560 + 6656 * LAYERS
    pieces.append((0, (), 0, 1280, [(base + 1280 * j, 128 * j) for j in range(2)]))
    return pieces


def update_kernel(clip_value, step_rate, *refs):
    g_ref, e_ref = refs[:2]
    ins = refs[2:23]
    stat_ref = refs[23]
    outs = refs[24:45]
    bufs = refs[45:66]
    isem, osem = refs[66:]
    pieces = update_pieces()
    table_rows = ins[0].shape[0]
    tail = table_rows - 1280

    def view(ref, piece):
        array, lead, first, rows, _ = piece
        if lead:
            ref = ref.at[lead]
        if ref.shape[0] == rows:
            return ref
        return ref.at[pl.ds(first, rows)]

    def transfer(kind, n, k, piece):
        src, dst = (ins, bufs) if kind == 0 else (bufs, outs)
        array = piece[0]
        sem = (isem, osem)[kind].at[k, n]
        return pltpu.make_async_copy(
            view(src[7 * k + array], piece), view(dst[7 * k + array], piece), sem
        )

    specials = [(0, (), 1280, tail, None), (5, (), 0, ins[5].shape[0], None)]
    order = specials + pieces
    for n, piece in enumerate(order):
        for k in range(3):
            transfer(0, n, k, piece).start()

    block = 128
    count = g_ref.shape[0] // block

    def gather(j, total):
        v = g_ref[pl.ds(pl.multiple_of(j * block, block), block)].astype(F32)
        return total + jnp.sum((v * v).reshape(block // 8, 8, 128), axis=0)

    total = lax.fori_loop(0, count, gather, jnp.zeros((8, 128), F32))
    rest = jnp.sum(e_ref[0:9] * e_ref[0:9]) + jnp.sum(e_ref[16:40] * e_ref[16:40])
    loss = jnp.max(e_ref[9:10])
    terms = jnp.max(e_ref[10:11])
    inverse = 1.0 / jnp.full((8, 128), terms, F32)
    norm = jnp.sqrt(jnp.full((8, 128), jnp.sum(total) + rest, F32)) * inverse
    factor = inverse * clip_value / jnp.maximum(norm, clip_value)
    stat_ref[0:8] = jnp.full((8, 128), loss, F32)
    stat_ref[8:16] = jnp.full((8, 128), terms, F32)
    stat_ref[16:24] = norm
    factor = factor[:1]

    def advance(views, rows, cols, gradient, scale):
        w, m, e = [v[rows, cols] for v in views]
        clipped = gradient * scale
        moment = MOMENTUM_RATE * m + clipped
        weight = w - step_rate * (clipped + MOMENTUM_RATE * moment)
        views[0][rows, cols] = weight
        views[1][rows, cols] = moment
        views[2][rows, cols] = AVERAGE_RATE * e + (1.0 - AVERAGE_RATE) * weight

    for n, piece in enumerate(order):
        array, lead, first, rows, blocks = piece
        for k in range(3):
            transfer(0, n, k, piece).wait()
        views = [bufs[7 * k + array].at[lead] if lead else bufs[7 * k + array] for k in range(3)]
        if blocks is None:
            at = 16 if array == 0 else 0
            wide = jnp.concatenate([factor, factor], axis=1)
            advance(
                views, slice(first, first + rows), slice(0, D), e_ref[at : at + rows], wide
            )
        else:
            step = 64

            @pl.loop(0, rows // step)
            def _(j):
                for source, column in blocks:
                    g = g_ref[pl.ds(pl.multiple_of(source + j * step, step), step)].astype(F32)
                    at = pl.ds(pl.multiple_of(first + j * step, step), step)
                    advance(views, at, slice(column, column + 128), g, factor)

        for k in range(3):
            transfer(1, n, k, piece).start()
    for n, piece in enumerate(order):
        for k in range(3):
            transfer(1, n, k, piece).wait()


def update_all(grads, extra, arrays, clip_value, step_rate):
    vmem = pltpu.VMEM
    count = len(update_pieces()) + 2
    hbm = pl.BlockSpec(memory_space=pl.ANY)
    results = pl.pallas_call(
        lambda *refs: update_kernel(clip_value, step_rate, *refs),
        out_shape=[jax.ShapeDtypeStruct((24, 128), F32)]
        + [jax.ShapeDtypeStruct(a.shape, F32) for a in arrays],
        in_specs=[pl.BlockSpec(memory_space=vmem)] * 2 + [hbm] * 21,
        out_specs=[pl.BlockSpec(memory_space=vmem)] + [hbm] * 21,
        scratch_shapes=[vmem(a.shape, F32) for a in arrays]
        + [pltpu.SemaphoreType.DMA((3, count)), pltpu.SemaphoreType.DMA((3, count))],
        compiler_params=pltpu.CompilerParams(vmem_limit_bytes=VMEM_LIMIT),
        name="update",
    )(grads, extra, *arrays)
    return results[0], results[1:]


def on_device(step_codes, segments, *arrays):
    streams = lax.axis_size("stream")
    groups = lax.axis_size("seq")
    group_seqs = step_codes.shape[0]
    table, qkv, square, up, down, small, head = arrays[:7]
    pos = jnp.asarray(position_rows()).astype(BF)
    grads, extra = run_step(
        step_codes.transpose(1, 2, 0),
        segments.T,
        pos,
        small,
        (table, qkv, square, up, down, head),
        streams,
        groups,
    )
    params_total = sum(w.size for w in arrays[:7])
    clip_value = CLIP_SCALE * (group_seqs * groups * STEPS) ** (-0.5)
    step_rate = STEP_SCALE * params_total**0.5 / clip_value
    stats, updated = update_all(grads, extra, arrays, clip_value, step_rate)
    return (stats[0, 0], stats[8, 0], stats[16, 0], *updated)


def solution(mesh):
    return jax.shard_map(
        on_device,
        mesh=mesh,
        in_specs=(P("seq", None, "stream"), P("seq", None)) + (P(),) * 21,
        out_specs=(P(),) * 24,
        check_vma=False,
    )
```

```python
import math

import jax
import jax.numpy as jnp
import numpy as np
from jax import lax
from jax.experimental import pallas as pl
from jax.experimental.pallas import tpu as pltpu
from jax.sharding import PartitionSpec as P

D = 256
HEADS = 8
HD = 32
FF = 1024
CATS = 32
CLASSES = 32
NA = 18
STEPS = 16
TOKS = 48
HK = HEADS * TOKS
LAYERS = 2
HCOLS = 1280
TROWS = 1408
CHUNK = 16
GROUP = 8
EPSILON = 1e-06
MOMENTUM_RATE = 0.9
AVERAGE_RATE = 0.7
CLIP_SCALE = 0.2
STEP_SCALE = 0.03
MASKED = -1e30
POSITION_SCALE = 0.5
SCALE = HD ** (-0.5)
BF = jnp.bfloat16
F32 = jnp.float32
VMEM_LIMIT = 63 * 1000 * 1000


def dot_nn(a, b):
    return lax.dot_general(a, b, (((1,), (0,)), ((), ())), preferred_element_type=F32)


def dot_nt(a, b):
    return lax.dot_general(a, b, (((1,), (1,)), ((), ())), preferred_element_type=F32)


def dot_tn(a, b):
    return lax.dot_general(a, b, (((0,), (0,)), ((), ())), preferred_element_type=F32)


def iota(shape, dim):
    return lax.broadcasted_iota(jnp.int32, shape, dim)


def position_rows():
    distance = np.arange(TOKS, dtype=np.float32)[:, None]
    rates = np.exp(np.arange(D // 2, dtype=np.float32) * np.float32(-2.0 * math.log(10000.0) / D))
    angle = (distance * rates[None, :].astype(np.float32)).astype(np.float32)
    table = np.float32(POSITION_SCALE) * np.concatenate([np.sin(angle), np.cos(angle)], axis=1)
    rows = np.zeros((3, TOKS, D), np.float32)
    for i in range(3):
        for j in range(3):
            for e in range(STEPS):
                d = 3 * (STEPS - 1 - e) + i - j
                if d >= 0:
                    rows[i, j * STEPS + e] = table[d]
    return rows.reshape(3 * TOKS, D)


def rms(values):
    return lax.rsqrt(jnp.mean(values * values, axis=-1, keepdims=True) + EPSILON)


def head_mask(h, rows):
    lane = iota((rows, 128), 1)
    low = (h % 4) * HD
    return ((lane >= low) & (lane < low + HD)).astype(F32).astype(BF)


def expand(rows):
    zero = jnp.zeros((TOKS, 128), BF)
    parts = []
    for h in range(HEADS):
        half = rows[:, 128 * (h // 4) : 128 * (h // 4) + 128] * head_mask(h, TOKS)
        parts.append(jnp.concatenate([half, zero] if h < 4 else [zero, half], axis=1))
    return jnp.concatenate(parts, axis=0)


def fold(values):
    lane = iota((TOKS, 128), 1)
    halves = []
    for g in range(2):
        total = None
        for h in range(4):
            part = values[(4 * g + h) * TOKS : (4 * g + h + 1) * TOKS, 128 * g : 128 * g + 128]
            total = part if total is None else jnp.where(lane >= h * HD, part, total)
        halves.append(total)
    return jnp.concatenate(halves, axis=1)


def spans(tile):
    found = []
    for h in range(HEADS):
        low, high = max(TOKS * h - 128 * tile, 0), min(TOKS * (h + 1) - 128 * tile, 128)
        if low < high:
            found.append((h, low, high))
    return found


def segment_max(scores):
    rows = scores.shape[0]
    lane = iota((rows, 128), 1)
    tiles = [scores[:, 128 * t : 128 * t + 128] for t in range(3)]
    best = {}
    for t in range(3):
        for h, low, high in spans(t):
            part = jnp.where((lane >= low) & (lane < high), tiles[t], -3e38)
            best[h] = part if h not in best else jnp.maximum(best[h], part)
    best = {h: jnp.max(v, axis=1, keepdims=True) for h, v in best.items()}
    outs = []
    for t in range(3):
        total = None
        for h, low, high in spans(t):
            wide = jnp.broadcast_to(best[h], (rows, 128))
            total = wide if total is None else jnp.where(lane >= low, wide, total)
        outs.append(total)
    return jnp.concatenate(outs, axis=1)


def unskew(values):
    row = iota((STEPS, HK), 0)
    values = jnp.concatenate(
        [pltpu.roll(values[:8], 15, 1), pltpu.roll(values[8:], 7, 1)], axis=0
    )
    for bit in (1, 2, 4):
        values = jnp.where((row & bit) > 0, pltpu.roll(values, HK - bit, 1), values)
    return values


SECTIONS = (2560, 4608, 2048, 4608, 2048, 2560)
DUE = ((1, 3, 5, 7, 9, 10), (3, 6, 8, 10), (7, 9, 11), (9, 12), (), ())


def stage_orders(streams, groups):
    rest, others = [], []
    step = 2
    while step < streams:
        rest.append(("stream", step))
        step *= 2
    step = 1
    while step < groups:
        others.append(("seq", step))
        step *= 2
    near = [tuple(others[:1] + rest)]
    far = [tuple(others[k : k + 2]) for k in range(1, len(others), 2)]
    core = [(("stream", 1),)]
    return [core + near + far, core + far + near]


def exchange_plan(streams, groups):
    unit = 16 * streams * groups
    sections = SECTIONS
    if any(s % unit or s < 2 * unit for s in sections):
        sections = (sum(SECTIONS),)
    orders = stage_orders(streams, groups)
    plan, base, recv, own = [], 0, 0, 0
    for rows in sections:
        units = rows // unit
        last = max(1, round(0.222 * units))
        lanes = []
        for part, order in zip((units - last, last), orders):
            size, sizes, slots = part * unit, [], []
            for bits in order:
                size //= 2 ** len(bits)
                sizes.append(size)
                slots.append(recv)
                recv += size * (2 ** len(bits) - 1)
            lanes.append(dict(base=base, order=order, sizes=sizes, slots=slots, own=own))
            own += size
            base += part * unit
        plan.append(lanes)
    assert base == sum(SECTIONS)
    return plan, recv, own


def place_of(bit):
    axis, step = bit
    return (lax.axis_index(axis) // step) % 2


def flips_of(bits):
    count = len(bits)
    return [tuple((n >> k) % 2 for k in range(count)) for n in range(1, 2**count)]


def partner_of(bits, flips):
    place = {"stream": lax.axis_index("stream"), "seq": lax.axis_index("seq")}
    for bit, flip in zip(bits, flips):
        if flip:
            axis, step = bit
            place[axis] = place[axis] + step * (1 - 2 * place_of(bit))
    return (place["stream"], place["seq"])


def share_of(bits, flips):
    total = 0
    for bit, flip in zip(bits, flips):
        mine = place_of(bit)
        total = 2 * total + ((1 - mine) if flip else mine)
    return total


class Lane:
    def __init__(self, spec, refs, sems, own_sem):
        self.spec, self.sems, self.own_sem = spec, sems, own_sem
        self.g, self.out, self.recv, self.own = refs
        offset = spec["base"]
        self.keep, self.send = [], []
        for bits, size in zip(spec["order"], spec["sizes"]):
            self.send.append(
                [
                    pl.multiple_of(offset + share_of(bits, flips) * size, 16)
                    for flips in flips_of(bits)
                ]
            )
            offset = pl.multiple_of(offset + share_of(bits, (0,) * len(bits)) * size, 16)
            self.keep.append(offset)

    def remote(self, kind, i, n, src, dst):
        bits = self.spec["order"][i]
        return pltpu.make_async_remote_copy(
            src_ref=src,
            dst_ref=dst,
            send_sem=self.sems.at[2 * kind, i, n],
            recv_sem=self.sems.at[2 * kind + 1, i, n],
            device_id=partner_of(bits, flips_of(bits)[n]),
            device_id_type=pl.DeviceIdType.MESH,
        )

    def scatter(self, i):
        size, slot = self.spec["sizes"][i], self.spec["slots"][i]
        return [
            self.remote(
                0, i, n, self.g.at[pl.ds(at, size)], self.recv.at[pl.ds(slot + n * size, size)]
            )
            for n, at in enumerate(self.send[i])
        ]

    def mine(self):
        return self.own.at[pl.ds(self.spec["own"], self.spec["sizes"][-1])]

    def keep_copy(self):
        rows = pl.ds(self.keep[-1], self.spec["sizes"][-1])
        return pltpu.make_async_copy(self.mine(), self.out.at[rows], self.own_sem)

    def gather(self, i):
        rows = pl.ds(self.keep[i], self.spec["sizes"][i])
        last = i + 1 == len(self.keep)
        return [
            self.remote(1, i, n, self.mine() if last else self.out.at[rows], self.out.at[rows])
            for n in range(len(self.send[i]))
        ]

    def add(self, i):
        size, slot = self.spec["sizes"][i], self.spec["slots"][i]
        last = i + 1 == len(self.keep)
        block = 256
        while size % block:
            block //= 2

        @pl.loop(0, size // block)
        def _(j):
            at = pl.ds(pl.multiple_of(self.keep[i] + j * block, 16), block)
            value = self.g[at].astype(F32)
            for n in range(len(self.send[i])):
                got = pl.ds(pl.multiple_of(slot + n * size + j * block, 16), block)
                value = value + self.recv[got].astype(F32)
            if last:
                own = pl.multiple_of(self.spec["own"] + j * block, 16)
                self.own[pl.ds(own, block)] = value.astype(BF)
            else:
                self.g[at] = value.astype(BF)


def start_all(copies):
    for copy in copies:
        copy.start()


def wait_all(copies):
    for copy in copies:
        copy.wait()


class Exchange:
    def __init__(self, streams, groups, g_ref, out_ref, recv_ref, own_ref, sems, own_sems):
        plan, _, _ = exchange_plan(streams, groups)
        refs = (g_ref, out_ref, recv_ref, own_ref)
        self.sections = [
            [
                Lane(spec, refs, sems.at[n, k], own_sems.at[n, k])
                for k, spec in enumerate(lanes)
            ]
            for n, lanes in enumerate(plan)
        ]
        self.order = plan[0][0]["order"]
        self.stages = len(self.order)
        self.active = []
        self.moment = 0

    def open(self, n):
        if len(self.sections) > 1:
            for lane in self.sections[n]:
                start_all(lane.scatter(0))
            self.active.append([n, 0])

    def advance(self, n, stage):
        stages = self.stages
        for lane in self.sections[n]:
            if stage < stages:
                wait_all(lane.scatter(stage))
                lane.add(stage)
                if stage + 1 < stages:
                    start_all(lane.scatter(stage + 1))
                else:
                    start_all(lane.gather(stage))
                    lane.keep_copy().start()
            else:
                i = 2 * stages - 1 - stage
                wait_all(lane.gather(i))
                if i + 1 == stages:
                    lane.keep_copy().wait()
                if i:
                    start_all(lane.gather(i - 1))

    def plan(self, count):
        moments = []
        for _ in range(count):
            self.moment += 1
            ready = [
                item
                for item in self.active
                if item[1] < len(DUE[item[0]]) and DUE[item[0]][item[1]] <= self.moment
            ]
            moments.append(self.step(ready))
        return moments

    def step(self, items):
        taken = [tuple(item) for item in items]
        for item in items:
            item[1] += 1
        self.active = [item for item in self.active if item[1] < 2 * self.stages]
        return taken

    def emit(self, moment):
        for n, stage in moment:
            self.advance(n, stage)

    def tick(self):
        self.emit(self.plan(1)[0])

    def when(self, condition, moment):
        if moment:
            pl.when(condition)(lambda: self.emit(moment))

    def finish(self, slot_ref, got_ref, sems, total_ref):
        last = len(self.sections) - 1

        def extra(i):
            bits = self.order[i]
            return [
                pltpu.make_async_remote_copy(
                    src_ref=slot_ref.at[i],
                    dst_ref=got_ref.at[i, n],
                    send_sem=sems.at[0, i, n],
                    recv_sem=sems.at[1, i, n],
                    device_id=partner_of(bits, flips),
                    device_id_type=pl.DeviceIdType.MESH,
                )
                for n, flips in enumerate(flips_of(bits))
            ]

        for lane in self.sections[last]:
            start_all(lane.scatter(0))
        start_all(extra(0))
        self.active.append([last, 0])
        i = 0
        while self.active:
            self.emit(self.step(list(reversed(self.active))))
            if i < self.stages:
                wait_all(extra(i))
                slot_ref[i + 1] = self.total(slot_ref[i], got_ref, i)
                if i + 1 < self.stages:
                    start_all(extra(i + 1))
            i += 1
        total_ref[...] = slot_ref[self.stages]

    def total(self, mine, got_ref, i):
        bits = self.order[i]
        if len(bits) == 1:
            return mine + got_ref[i, 0]
        return (mine + got_ref[i, 0]) + (got_ref[i, 1] + got_ref[i, 2])

def step_kernel(
    streams,
    groups,
    codes_hbm,
    seg_ref,
    pos_ref,
    small_ref,
    table_hbm,
    qkv_hbm,
    square_hbm,
    up_hbm,
    down_hbm,
    head_hbm,
    out_hbm,
    total_ref,
    x_s,
    att_s,
    pu_s,
    o_s,
    mid_s,
    hb_s,
    gp_s,
    b_s,
    dyl_s,
    dml_s,
    rk_s,
    start_s,
    l_s,
    slope_s,
    table_s,
    tail_s,
    wqkv_s,
    wsq_s,
    wup_s,
    wdown_s,
    whead_s,
    wheadt_s,
    raw_s,
    send_s,
    got_codes_s,
    g_s,
    recv_s,
    own_s,
    slot_s,
    got_s,
    load_sems,
    code_sems,
    sems,
    own_sems,
    extra_sems,
):
    toks = x_s.shape[1]
    seqs = toks // TOKS
    steps_all = seqs * STEPS
    chunks = seqs // CHUNK
    rows_c = CHUNK * TOKS
    me = lax.axis_index("stream")
    table_rows = table_hbm.shape[0]

    raw_load = pltpu.make_async_copy(codes_hbm, raw_s, load_sems.at[0])
    raw_load.start()
    whole = table_rows // 128 * 128
    rest = table_rows - whole
    loads = []

    def load(src, place, targets):
        copy = pltpu.make_async_copy(src, place, load_sems.at[len(loads) + 1])
        loads.append((copy, place, targets))

    table_rows_main = pl.ds(0, whole)
    load(
        table_hbm.at[table_rows_main],
        x_s.at[2, table_rows_main],
        [(table_s.at[table_rows_main], False)],
    )
    load(table_hbm.at[pl.ds(whole, rest)], tail_s, None)
    for layer in range(LAYERS):
        places = [o_s.at[layer, pl.ds(256 * j, 256)] for j in range(6)]
        places += [mid_s.at[layer, pl.ds(256 * j, 256)] for j in range(6)]
        places += [x_s.at[1, pl.ds(256 * layer, 256)]]
        places = iter(places)
        for j in range(3):
            cols = pl.ds(256 * j, 256)
            load(qkv_hbm.at[layer, :, cols], next(places), [(wqkv_s.at[layer, :, cols], False)])
        for j in range(2):
            load(square_hbm.at[layer, j], next(places), [(wsq_s.at[layer, j], False)])
        for j in range(4):
            cols = pl.ds(256 * j, 256)
            load(up_hbm.at[layer, :, cols], next(places), [(wup_s.at[layer, :, cols], False)])
        for j in range(4):
            cols = pl.ds(256 * j, 256)
            load(down_hbm.at[layer, cols], next(places), [(wdown_s.at[layer, cols], False)])
    for j in range(HCOLS // 256):
        cols = pl.ds(256 * j, 256)
        load(
            head_hbm.at[:, cols],
            x_s.at[1, pl.ds(512 + 256 * j, 256)] if j < 4 else l_s.at[pl.ds(0, 256)],
            [(whead_s.at[:, cols], False), (wheadt_s.at[cols], True)],
        )
    for copy, _, _ in loads:
        copy.start()

    comm = Exchange(streams, groups, g_s, out_hbm, recv_s, own_s, sems, own_sems)
    barrier = pltpu.get_barrier_semaphore()
    greeted = [((me + j) % streams, lax.axis_index("seq")) for j in range(1, streams)]
    peers = list(greeted)
    for bits in comm.order:
        for flips in flips_of(bits):
            if any(flip and bit[0] == "seq" for bit, flip in zip(bits, flips)):
                greeted.append(partner_of(bits, flips))
    for peer in greeted:
        pl.semaphore_signal(
            barrier, inc=1, device_id=peer, device_id_type=pl.DeviceIdType.MESH
        )

    raw_load.wait()
    send_s[...] = raw_s[...].astype(F32).astype(BF)
    pl.semaphore_wait(barrier, len(greeted))
    sends = []
    for j, peer in enumerate(peers):
        sends.append(
            pltpu.make_async_remote_copy(
                src_ref=send_s,
                dst_ref=got_codes_s.at[me],
                send_sem=code_sems.at[0, j],
                recv_sem=code_sems.at[1, j],
                device_id=peer,
                device_id_type=pl.DeviceIdType.MESH,
            )
        )
        sends[-1].start()
    got_codes_s[me] = send_s[...]

    group = seg_ref.shape[1]
    step_lane = iota((STEPS, steps_all), 1) % STEPS
    step_row = iota((STEPS, steps_all), 0)
    own_lane = iota((group, steps_all), 1) // STEPS + me * seqs
    pick = (iota((group, steps_all), 0) == own_lane).astype(F32).astype(BF)
    seg = dot_nn(seg_ref[...].astype(F32).astype(BF), pick)
    seg_own = jnp.sum(jnp.where(step_row == step_lane, seg, 0.0), axis=0, keepdims=True)
    start = jnp.sum(jnp.where(seg < seg_own, 1.0, 0.0), axis=0, keepdims=True)
    valid_row = jnp.sum(
        jnp.where((step_row == step_lane + 1) & (seg == seg_own), 1.0, 0.0), axis=0, keepdims=True
    )
    start_low = jnp.broadcast_to(start, (STEPS, steps_all)).astype(BF)
    one_row = (iota((STEPS, 128), 0) == 0).astype(F32).astype(BF)
    start_s[...] = dot_tn(start_low, one_row).reshape(seqs, STEPS, 128)

    table_s[whole:] = jnp.zeros((TROWS - whole, D), BF)
    for copy, place, targets in loads:
        copy.wait()
        if targets is None:
            pad = -rest % 16
            table_s[whole : whole + rest + pad] = jnp.concatenate(
                [place[...], jnp.zeros((pad, D), F32)], axis=0
            ).astype(BF)
            continue
        for target, turned in targets:
            target[...] = (place[...].T if turned else place[...]).astype(BF)
    for copy in sends:
        copy.wait()
    codes = []
    for k in range(4):
        wide = dot_nn(got_codes_s[k].reshape(STEPS * STEPS, group), pick)
        wide = wide.reshape(STEPS, STEPS, steps_all)
        at_step = iota((STEPS, STEPS, steps_all), 0) == iota((STEPS, STEPS, steps_all), 2) % STEPS
        codes.append(jnp.sum(jnp.where(at_step, wide, 0.0), axis=0).astype(BF))

    spread = (iota((STEPS, 512), 1) // CLASSES == iota((STEPS, 512), 0)).astype(F32).astype(BF)
    first = (iota((STEPS, 384), 0) == 0).astype(F32).astype(BF)
    class_lane = (iota((128, 512), 1) % CLASSES).astype(F32)
    lane = iota((128, 384), 1).astype(F32)
    for c in range(steps_all // 128):
        cols = slice(128 * c, 128 * c + 128)
        halves = []
        for k in range(2):
            hot = (dot_tn(codes[k][:, cols], spread) == class_lane).astype(F32).astype(BF)
            piece = dot_nn(hot, table_s[512 * k : 512 * k + 512]).astype(BF).astype(F32)
            halves.append(piece)
        hot = (dot_tn(codes[2][:, cols], first[:, :128]) == lane[:, :128]).astype(F32).astype(BF)
        action = dot_nn(hot, table_s[1024:1152]).astype(BF).astype(F32)
        hot = (dot_tn(codes[3][:, cols], first) + NA == lane).astype(F32).astype(BF)
        reward = dot_nn(hot, table_s[1024:1408]).astype(BF).astype(F32)
        pieces = [p.reshape(8, 1, STEPS, D) for p in (halves[0] + halves[1], action, reward)]
        x_s[0, 384 * c : 384 * c + 384] = jnp.concatenate(pieces, axis=1).reshape(384, D)
    for layer in range(LAYERS):
        rk = dot_nn(pos_ref[...], wsq_s[layer, 1]).astype(BF)
        for k in range(3):
            rk_s[layer, k] = expand(rk[TOKS * k : TOKS * k + TOKS])

    lane_hk = iota((TOKS, HK), 1) % TOKS
    key_step = lane_hk % STEPS
    key_time = 3 * key_step + lane_hk // STEPS
    row_tok = iota((TOKS, HK), 0)
    query_time = 3 * (row_tok % STEPS) + row_tok // STEPS
    causal = key_time <= query_time
    key_step_f = key_step.astype(F32)
    sum_hd = (iota((HK, D), 0) // TOKS == iota((HK, D), 1) // HD).astype(F32).astype(BF)
    sum_hk = (iota((D, HK), 0) // HD == iota((D, HK), 1) // TOKS).astype(F32).astype(BF)

    for layer in range(LAYERS):
        gain_a = small_ref[4 * layer : 4 * layer + 1]
        gain_b = small_ref[4 * layer + 1 : 4 * layer + 2]
        bias_u = small_ref[4 * layer + 2 : 4 * layer + 3]
        bias_v = small_ref[4 * layer + 3 : 4 * layer + 4]

        @pl.loop(0, chunks)
        def _(c):
            rows = pl.ds(pl.multiple_of(c * rows_c, rows_c), rows_c)
            x = x_s[layer, rows]
            low = (x * rms(x) * gain_a).astype(BF)
            q = dot_nn(low, wqkv_s[layer, :, :256]).astype(BF).astype(F32)
            qu = (q + bias_u).astype(BF)
            qv = (q + bias_v).astype(BF)
            key = dot_nn(low, wqkv_s[layer, :, 256:512]).astype(BF)
            val = dot_nn(low, wqkv_s[layer, :, 512:]).astype(BF)
            att_s[layer, rows, 0:256] = qu
            att_s[layer, rows, 256:512] = qv
            att_s[layer, rows, 512:768] = key
            att_s[layer, rows, 768:1024] = val
            qv4 = qv.reshape(CHUNK, 3, STEPS, D)
            place = [
                dot_nt(qv4[:, k].reshape(CHUNK * STEPS, D), rk_s[layer, k]) for k in range(3)
            ]
            start_c = start_s[pl.ds(c * CHUNK, CHUNK)]
            for g in range(0, CHUNK, GROUP):
                members = range(g, g + GROUP)
                spans = {b: slice(TOKS * b, TOKS * b + TOKS) for b in members}
                scores = {b: dot_nt(qu[spans[b]], expand(key[spans[b]])) for b in members}
                for b in members:
                    shifted = [
                        pltpu.roll(
                            place[k][STEPS * b : STEPS * b + STEPS],
                            HK - (STEPS - 1),
                            1,
                            stride=1,
                            stride_axis=0,
                        )
                        for k in range(3)
                    ]
                    begin = jnp.concatenate([start_c[b]] * 3, axis=0)
                    begin = jnp.concatenate([begin] * 3, axis=1)
                    score = (scores[b] + jnp.concatenate(shifted, axis=0)) * SCALE
                    scores[b] = jnp.where(causal & (key_step_f >= begin), score, MASKED)
                tops = {b: segment_max(scores[b]) for b in members}
                probs = {b: jnp.exp(scores[b] - tops[b]).astype(BF) for b in members}
                for b in members:
                    l_s[spans[b]] = dot_nn(probs[b], expand(val[spans[b]]))
                for b in members:
                    pu_s[layer, pl.ds(pl.multiple_of(c * rows_c + TOKS * b, TOKS), TOKS)] = probs[b]
            recip = 1.0 / dot_nn(pu_s[layer, rows], sum_hd)
            out = l_s[...] * recip
            o_s[layer, rows] = out
            mid = x + dot_nn(out.astype(BF), wsq_s[layer, 0])
            mid_s[layer, rows] = mid
            low = (mid * rms(mid) * gain_b).astype(BF)
            for j in range(FF // 256):
                cols = slice(256 * j, 256 * j + 256)
                inner = dot_nn(low, wup_s[layer, :, cols])
                square = inner * inner
                c0 = math.sqrt(2.0 / math.pi)
                tanh = jnp.tanh(c0 * inner * (1.0 + 0.044715 * square))
                half = 0.5 * (1.0 + tanh)
                hb_s[layer, rows, cols] = (inner * half).astype(BF)
                gp_s[layer, rows, cols] = (
                    half
                    + (0.5 * c0) * inner * (1.0 - tanh * tanh) * (1.0 + (3 * 0.044715) * square)
                ).astype(BF)
            nxt = mid + dot_nn(hb_s[layer, rows], wdown_s[layer])
            x_s[layer + 1, rows] = nxt

    gain_f = small_ref[4 * LAYERS : 4 * LAYERS + 1]
    xf = x_s[LAYERS].reshape(seqs, 3, STEPS, D)[:, 1].reshape(steps_all, D)
    feat = (xf * rms(xf) * gain_f).astype(BF)
    spread_t = (iota((512, STEPS), 0) // CLASSES == iota((512, STEPS), 1)).astype(F32).astype(BF)
    class_row = iota((4, CLASSES, steps_all), 1).astype(F32)
    loss = jnp.zeros((4, steps_all), F32)
    for k in range(2):
        follow_codes = pltpu.roll(codes[k].astype(F32), steps_all - 1, 1).astype(BF)
        for j in range(4):
            base = 512 * k + 128 * j
            logits = dot_nt(wheadt_s[base : base + 128], feat).reshape(4, CLASSES, steps_all)
            target = dot_nn(spread_t[128 * j : 128 * j + 128], follow_codes)
            hot = target.reshape(4, CLASSES, steps_all) == class_row
            top = jnp.max(logits, axis=1, keepdims=True)
            grown = jnp.exp(logits - top)
            total = jnp.sum(grown, axis=1, keepdims=True)
            picked = jnp.sum(jnp.where(hot, logits, 0.0), axis=1)
            loss = loss + valid_row * (jnp.log(total[:, 0]) + top[:, 0] - picked)
            slope = (grown * (1.0 / total) - jnp.where(hot, 1.0, 0.0)) * valid_row[None]
            slope_s[base : base + 128] = slope.reshape(128, steps_all).astype(BF)
    action_row = codes[2][0:1].astype(F32)
    discount_row = codes[2][1:2].astype(F32)
    reward_row = codes[3][0:1].astype(F32)
    logits = dot_nt(wheadt_s[1024:1280], feat)
    row = iota((256, steps_all), 0)
    hot = row == (reward_row + 1.0).astype(jnp.int32)
    disc = logits[:1]
    masked = jnp.where(row == 0, -3e38, logits)
    top = jnp.max(masked, axis=0, keepdims=True)
    grown = jnp.exp(masked - top)
    total = jnp.sum(grown, axis=0, keepdims=True)
    picked = jnp.sum(jnp.where(hot, logits, 0.0), axis=0, keepdims=True)
    fade = jnp.exp(-jnp.abs(disc))
    soft = jnp.maximum(disc, 0.0) + jnp.log(1.0 + fade)
    sigm = jnp.where(disc >= 0.0, 1.0, fade) / (1.0 + fade)
    loss_row = (
        jnp.sum(loss, axis=0, keepdims=True)
        + jnp.log(total)
        + top
        - picked
        + soft
        - discount_row * disc
    )
    slope = grown * (1.0 / total) - jnp.where(hot, 1.0, 0.0)
    slope = jnp.where(row == 0, sigm - discount_row, slope)
    slope_s[1024:1280] = slope.astype(BF)
    loss_sum = jnp.sum(loss_row)
    count = jnp.sum(valid_row) * CATS + 2.0 * steps_all
    slot_s[0, 9:10] = jnp.full((1, D), loss_sum, F32)
    slot_s[0, 10:11] = jnp.full((1, D), count, F32)
    slot_s[0, 11:16] = jnp.zeros((5, D), F32)

    feat_t = feat.astype(F32).T.astype(BF)
    for j in range(5):
        part = dot_nt(feat_t, slope_s[256 * j : 256 * j + 256])
        for k in range(2):
            base = 256 * (2 * j + k)
            g_s[base : base + 256] = part[:, 128 * k : 128 * k + 128].astype(BF)
    comm.open(0)
    dfeat = dot_nn(whead_s[...], slope_s[...]).T
    scale_f = rms(xf)
    hat = xf * scale_f
    slot_s[0, 8:9] = jnp.sum(dfeat * hat, axis=0, keepdims=True)
    inner = dfeat * gain_f
    dxf = scale_f * (inner - hat * jnp.mean(inner * hat, axis=-1, keepdims=True))
    gap = jnp.zeros((seqs, 1, STEPS, D), F32)
    x_s[LAYERS] = jnp.concatenate([gap, dxf.reshape(seqs, 1, STEPS, D), gap], axis=1).reshape(
        toks, D
    )

    for layer in reversed(range(LAYERS)):
        gain_a = small_ref[4 * layer : 4 * layer + 1]
        gain_b = small_ref[4 * layer + 1 : 4 * layer + 2]
        slot_s[0, 4 * layer : 4 * layer + 4] = jnp.zeros((4, D), F32)

        moments = comm.plan(chunks - 1)

        @pl.loop(0, chunks)
        def _(c):
            rows = pl.ds(pl.multiple_of(c * rows_c, rows_c), rows_c)
            for k in range(1, chunks):
                comm.when(c == k, moments[k - 1])
            dy = x_s[LAYERS, rows]
            dyl = dy.astype(BF)
            dyl_s[rows] = dyl
            for j in range(FF // 256):
                cols = slice(256 * j, 256 * j + 256)
                dact = dot_nt(dyl, wdown_s[layer, cols])
                gp_s[layer, rows, cols] = (dact * gp_s[layer, rows, cols].astype(F32)).astype(BF)
            dlow = dot_nt(gp_s[layer, rows], wup_s[layer])
            mid = mid_s[layer, rows]
            scale = rms(mid)
            hat = mid * scale
            b_s[rows] = (hat * gain_b).astype(BF)
            dgain = jnp.sum(dlow * hat, axis=0, keepdims=True)
            inner = dlow * gain_b
            dmid = scale * (inner - hat * jnp.mean(inner * hat, axis=-1, keepdims=True)) + dy
            slot_s[0, 4 * layer + 1 : 4 * layer + 2] += dgain
            mid_s[layer, rows] = dmid
            dml_s[rows] = dmid.astype(BF)

        base = 2560 + 6656 * (LAYERS - 1 - layer)

        def put(offset, value, base=base):
            size = value.shape[0]
            for k in range(2):
                at = base + offset + k * size
                g_s[at : at + size] = value[:, 128 * k : 128 * k + 128].astype(BF)

        comm.tick()
        for j in range(4):
            part = dot_tn(hb_s[layer, :, 256 * j : 256 * j + 256], dyl_s[...])
            for k in range(2):
                at = base + 1024 * k + 256 * j
                g_s[at : at + 256] = part[:, 128 * k : 128 * k + 128].astype(BF)
        for j in range(4):
            put(2048 + 512 * j, dot_tn(b_s[...], gp_s[layer, :, 256 * j : 256 * j + 256]))
        put(4096, dot_tn(o_s[layer].astype(BF), dml_s[...]))
        comm.open(1 + 2 * (LAYERS - 1 - layer))
        moments = comm.plan(seqs // GROUP - 1)
        rows_a = GROUP * TOKS

        @pl.loop(0, seqs // GROUP)
        def _(c):
            rows = pl.ds(pl.multiple_of(c * rows_a, rows_a), rows_a)
            for k in range(1, seqs // GROUP):
                comm.when(c == k, moments[k - 1])
            dmid = mid_s[layer, rows]
            dml = dml_s[rows]
            recip = 1.0 / dot_nn(pu_s[layer, rows], sum_hd)
            do = dot_nt(dml, wsq_s[layer, 0]).astype(BF).astype(F32)
            do = (do * recip).astype(BF)
            mass = do.astype(F32) * o_s[layer, rows]
            mass_hi = mass.astype(BF)
            mass_lo = (mass - mass_hi.astype(F32)).astype(BF)
            delta = dot_nn(mass_hi, sum_hk) + dot_nn(mass_lo, sum_hk)
            qu = att_s[layer, rows, 0:256]
            key = att_s[layer, rows, 512:768]
            val = att_s[layer, rows, 768:1024]
            probs_all = pu_s[layer, rows]
            draws = {}
            for g in range(1):
                members = range(g, g + GROUP)
                spans = {b: slice(TOKS * b, TOKS * b + TOKS) for b in members}
                dprob = {b: dot_nt(do[spans[b]], expand(val[spans[b]])) for b in members}
                dval = {b: dot_tn(probs_all[spans[b]], do[spans[b]]) for b in members}
                dscore = {
                    b: (probs_all[spans[b]].astype(F32) * (dprob[b] - delta[spans[b]])).astype(BF)
                    for b in members
                }
                dkey = {b: dot_tn(dscore[b], qu[spans[b]]) for b in members}
                dque = {b: dot_nn(dscore[b], expand(key[spans[b]])) for b in members}
                for b in members:
                    wide = dscore[b].astype(F32)
                    draws[b] = [
                        unskew(wide[STEPS * k : STEPS * k + STEPS]).astype(BF) for k in range(3)
                    ]
                for b in members:
                    l_s[spans[b]] = dque[b] * SCALE
                for b in members:
                    out_rows = pl.ds(pl.multiple_of(c * rows_a + TOKS * b, TOKS), TOKS)
                    att_s[layer, out_rows, 512:768] = (fold(dkey[b]) * SCALE).astype(BF)
                    att_s[layer, out_rows, 768:1024] = fold(dval[b]).astype(BF)
                    pu_s[layer, out_rows] = jnp.concatenate(draws[b], axis=0)
            dqv = [
                dot_nn(
                    jnp.concatenate([draws[b][k] for b in range(GROUP)], axis=0), rk_s[layer, k]
                ).reshape(GROUP, 1, STEPS, D)
                for k in range(3)
            ]
            dqv = jnp.concatenate(dqv, axis=1).reshape(rows_a, D) * SCALE
            dqu = l_s[0:rows_a]
            slot_s[0, 4 * layer + 2 : 4 * layer + 3] += jnp.sum(dqu, axis=0, keepdims=True)
            slot_s[0, 4 * layer + 3 : 4 * layer + 4] += jnp.sum(dqv, axis=0, keepdims=True)
            dq = (dqu + dqv).astype(BF)
            att_s[layer, rows, 0:256] = dq
            dlow = (
                dot_nt(dq, wqkv_s[layer, :, :256])
                + dot_nt(att_s[layer, rows, 512:768], wqkv_s[layer, :, 256:512])
                + dot_nt(att_s[layer, rows, 768:1024], wqkv_s[layer, :, 512:])
            )
            x = x_s[layer, rows]
            scale = rms(x)
            hat = x * scale
            dyl_s[rows] = (hat * gain_a).astype(BF)
            slot_s[0, 4 * layer : 4 * layer + 1] += jnp.sum(dlow * hat, axis=0, keepdims=True)
            inner = dlow * gain_a
            dx = scale * (inner - hat * jnp.mean(inner * hat, axis=-1, keepdims=True)) + dmid
            x_s[LAYERS, rows] = dx

        comm.tick()
        drk = []
        draw = pu_s[layer].reshape(seqs, 3, STEPS, HK)
        qv = att_s[layer, :, 256:512].reshape(seqs, 3, STEPS, D)
        for k in range(3):
            wide = dot_tn(
                draw[:, k].reshape(steps_all, HK), qv[:, k].reshape(steps_all, D)
            )
            drk.append(fold(wide) * SCALE)
        put(4608, dot_tn(pos_ref[...], jnp.concatenate(drk, axis=0).astype(BF)))
        put(5120, dot_tn(dyl_s[...], att_s[layer, :, 0:256]))
        put(5632, dot_tn(dyl_s[...], att_s[layer, :, 512:768]))
        put(6144, dot_tn(dyl_s[...], att_s[layer, :, 768:1024]))
        comm.open(2 * (LAYERS - layer))

    dtok = x_s[LAYERS].reshape(seqs, 3, STEPS, D).astype(BF)
    dtok = [dtok[:, k].reshape(steps_all, D) for k in range(3)]
    base = 2560 + 6656 * LAYERS
    class_row = (iota((256, steps_all), 0) % CLASSES).astype(F32)
    for k in range(2):
        for j in range(2):
            wide = dot_nn(spread_t[256 * j : 256 * j + 256], codes[k])
            hot = (wide == class_row).astype(F32).astype(BF)
            part = dot_nn(hot, dtok[0])
            for h in range(2):
                at = base + 1280 * h + 512 * k + 256 * j
                g_s[at : at + 256] = part[:, 128 * h : 128 * h + 128].astype(BF)
    row = iota((288, steps_all), 0)
    hot_a = (row == action_row.astype(jnp.int32)).astype(F32).astype(BF)
    hot_r = (row == (reward_row + NA).astype(jnp.int32)).astype(F32).astype(BF)
    part = dot_nn(hot_a, dtok[1]) + dot_nn(hot_r, dtok[2])
    for h in range(2):
        at = base + 1280 * h + 1024
        g_s[at : at + 256] = part[:256, 128 * h : 128 * h + 128].astype(BF)
    slot_s[0, 16:40] = part[256:280]
    comm.finish(slot_s, got_s, extra_sems, total_ref)


def run_step(codes, seg, pos, small, weights, streams, groups):
    seqs = codes.shape[2] // streams
    toks = seqs * TOKS
    plan, recv, own = exchange_plan(streams, groups)
    stages = len(plan[0][0]["order"])
    vmem, dma = pltpu.VMEM, pltpu.SemaphoreType.DMA
    hbm = pl.BlockSpec(memory_space=pl.ANY)
    table, qkv, square, up, down, head = weights
    return pl.pallas_call(
        lambda *refs: step_kernel(streams, groups, *refs),
        out_shape=(
            jax.ShapeDtypeStruct((sum(SECTIONS), 128), BF),
            jax.ShapeDtypeStruct((40, D), F32),
        ),
        in_specs=[hbm] + [pl.BlockSpec(memory_space=vmem)] * 3 + [hbm] * 6,
        out_specs=[hbm, pl.BlockSpec(memory_space=vmem)],
        scratch_shapes=[
            vmem((LAYERS + 1, toks, D), F32),
            vmem((LAYERS, toks, 1024), BF),
            vmem((LAYERS, toks, HK), BF),
            vmem((LAYERS, toks, D), F32),
            vmem((LAYERS, toks, D), F32),
            vmem((LAYERS, toks, FF), BF),
            vmem((LAYERS, toks, FF), BF),
            vmem((toks, D), BF),
            vmem((toks, D), BF),
            vmem((toks, D), BF),
            vmem((LAYERS, 3, HK, D), BF),
            vmem((seqs, STEPS, 128), F32),
            vmem((CHUNK * TOKS, D), F32),
            vmem((HCOLS, seqs * STEPS), BF),
            vmem((TROWS, D), BF),
            vmem((table.shape[0] % 128, D), F32),
            vmem(qkv.shape, BF),
            vmem(square.shape, BF),
            vmem(up.shape, BF),
            vmem(down.shape, BF),
            vmem(head.shape, BF),
            vmem(head.shape[::-1], BF),
            vmem(codes.shape, jnp.int32),
            vmem(codes.shape, BF),
            vmem((streams,) + codes.shape, BF),
            vmem((sum(SECTIONS), 128), BF),
            vmem((recv, 128), BF),
            vmem((own, 128), BF),
            vmem((stages + 1, 40, D), F32),
            vmem((stages, 3, 40, D), F32),
            dma((3 + 13 * LAYERS + 5,)),
            dma((2, streams - 1)),
            dma((len(plan), 2, 4, stages, 3)),
            dma((len(plan), 2)),
            dma((2, stages, 3)),
        ],
        compiler_params=pltpu.CompilerParams(
            collective_id=0, has_side_effects=True, vmem_limit_bytes=VMEM_LIMIT
        ),
        name="step",
    )(codes, seg, pos, small, table, qkv, square, up, down, head)


def update_pieces():
    pieces = []
    for k in range(LAYERS):
        layer = LAYERS - 1 - k
        base = 2560 + 6656 * k
        for half in range(2):
            r = 512 * half
            pieces.append(
                (4, (layer,), r, 512, [(base + 1024 * j + r, 128 * j) for j in range(2)])
            )
        pieces.append((3, (layer,), 0, 256, [(base + 2048 + 256 * j, 128 * j) for j in range(8)]))
        pieces.append((2, (layer, 0), 0, 256, [(base + 4096 + 256 * j, 128 * j) for j in range(2)]))
        pieces.append((2, (layer, 1), 0, 256, [(base + 4608 + 256 * j, 128 * j) for j in range(2)]))
        pieces.append((1, (layer,), 0, 256, [(base + 5120 + 256 * j, 128 * j) for j in range(6)]))
    base = 2560 + 6656 * LAYERS
    first = [(6, (), 0, 256, [(256 * j, 128 * j) for j in range(10)])]
    for r in range(0, 1280, 640):
        first.append((0, (), r, 640, [(base + 1280 * j + r, 128 * j) for j in range(2)]))
    return first + sorted(pieces, key=lambda p: -p[3] * len(p[4]))


def update_kernel(clip_value, step_rate, *refs):
    g_ref, e_ref = refs[:2]
    ins = refs[2:23]
    loss_ref, terms_ref, norm_ref = refs[23:26]
    outs = refs[26:47]
    bufs = refs[47:68]
    isem, osem = refs[68:]
    pieces = update_pieces()
    table_rows = ins[0].shape[0]
    tail = table_rows - 1280

    def view(ref, piece):
        array, lead, first, rows, _ = piece
        if lead:
            ref = ref.at[lead]
        if ref.shape[0] == rows:
            return ref
        return ref.at[pl.ds(first, rows)]

    def transfer(kind, n, k, piece):
        src, dst = (ins, bufs) if kind == 0 else (bufs, outs)
        array = piece[0]
        sem = (isem, osem)[kind].at[k, n]
        return pltpu.make_async_copy(
            view(src[7 * k + array], piece), view(dst[7 * k + array], piece), sem
        )

    specials = [(0, (), 1280, tail, None), (5, (), 0, ins[5].shape[0], None)]
    order = pieces + specials
    for n, piece in enumerate(order):
        for k in range(3):
            transfer(0, n, k, piece).start()

    block = 512
    count = g_ref.shape[0] // block

    def gather(j, total):
        v = g_ref[pl.ds(pl.multiple_of(j * block, block), block)].astype(F32)
        return total + jnp.sum((v * v).reshape(block // 64, 64, 128), axis=0)

    total = lax.fori_loop(0, count, gather, jnp.zeros((64, 128), F32))
    rest = jnp.sum(e_ref[0:9] * e_ref[0:9]) + jnp.sum(e_ref[16:40] * e_ref[16:40])
    loss = jnp.max(e_ref[9:10])
    terms = jnp.max(e_ref[10:11])
    inverse = 1.0 / jnp.full((8, 128), terms, F32)
    norm = jnp.sqrt(jnp.full((8, 128), jnp.sum(total) + rest, F32)) * inverse
    factor = inverse * clip_value / jnp.maximum(norm, clip_value)
    loss_ref[0, 0] = loss
    terms_ref[0, 0] = terms
    norm_ref[0, 0] = jnp.max(norm)
    factor = factor[:1]

    def advance(views, rows, cols, gradient, scale):
        w, m, e = [v[rows, cols] for v in views]
        clipped = gradient * scale
        moment = MOMENTUM_RATE * m + clipped
        weight = w - step_rate * (clipped + MOMENTUM_RATE * moment)
        views[0][rows, cols] = weight
        views[1][rows, cols] = moment
        views[2][rows, cols] = AVERAGE_RATE * e + (1.0 - AVERAGE_RATE) * weight

    for n, piece in enumerate(order):
        array, lead, first, rows, blocks = piece
        for k in range(3):
            transfer(0, n, k, piece).wait()
        views = [bufs[7 * k + array].at[lead] if lead else bufs[7 * k + array] for k in range(3)]
        if blocks is None:
            at = 16 if array == 0 else 0
            wide = jnp.concatenate([factor, factor], axis=1)
            advance(
                views, slice(first, first + rows), slice(0, D), e_ref[at : at + rows], wide
            )
        else:
            step = 64

            @pl.loop(0, rows // step)
            def _(j):
                for source, column in blocks:
                    g = g_ref[pl.ds(pl.multiple_of(source + j * step, step), step)].astype(F32)
                    at = pl.ds(pl.multiple_of(first + j * step, step), step)
                    advance(views, at, slice(column, column + 128), g, factor)

        for k in range(3):
            transfer(1, n, k, piece).start()
    for n, piece in enumerate(order):
        for k in range(3):
            transfer(1, n, k, piece).wait()


def update_all(grads, extra, arrays, clip_value, step_rate):
    vmem = pltpu.VMEM
    count = len(update_pieces()) + 2
    hbm = pl.BlockSpec(memory_space=pl.ANY)
    results = pl.pallas_call(
        lambda *refs: update_kernel(clip_value, step_rate, *refs),
        out_shape=[jax.ShapeDtypeStruct((1, 1), F32)] * 3
        + [jax.ShapeDtypeStruct(a.shape, F32) for a in arrays],
        in_specs=[pl.BlockSpec(memory_space=vmem)] * 2 + [hbm] * 21,
        out_specs=[pl.BlockSpec(memory_space=pltpu.SMEM)] * 3 + [hbm] * 21,
        scratch_shapes=[vmem(a.shape, F32) for a in arrays]
        + [pltpu.SemaphoreType.DMA((3, count)), pltpu.SemaphoreType.DMA((3, count))],
        compiler_params=pltpu.CompilerParams(vmem_limit_bytes=VMEM_LIMIT),
        name="update",
    )(grads, extra, *arrays)
    return results[:3], results[3:]


def on_device(step_codes, segments, *arrays):
    streams = lax.axis_size("stream")
    groups = lax.axis_size("seq")
    group_seqs = step_codes.shape[0]
    table, qkv, square, up, down, small, head = arrays[:7]
    pos = jnp.asarray(position_rows()).astype(BF)
    grads, extra = run_step(
        step_codes.transpose(1, 2, 0),
        segments.T,
        pos,
        small,
        (table, qkv, square, up, down, head),
        streams,
        groups,
    )
    params_total = sum(w.size for w in arrays[:7])
    clip_value = CLIP_SCALE * (group_seqs * groups * STEPS) ** (-0.5)
    step_rate = STEP_SCALE * params_total**0.5 / clip_value
    stats, updated = update_all(grads, extra, arrays, clip_value, step_rate)
    return (*(s.reshape(()) for s in stats), *updated)


def solution(mesh):
    return jax.shard_map(
        on_device,
        mesh=mesh,
        in_specs=(P("seq", None, "stream"), P("seq", None)) + (P(),) * 21,
        out_specs=(P(),) * 24,
        check_vma=False,
    )
```

```python
import math

import jax
import jax.numpy as jnp
import numpy as np
from jax import lax
from jax.experimental import pallas as pl
from jax.experimental.pallas import tpu as pltpu
from jax.sharding import PartitionSpec as P

D = 256
HEADS = 8
HD = 32
FF = 1024
CATS = 32
CLASSES = 32
NA = 18
STEPS = 16
TOKS = 48
HK = HEADS * TOKS
LAYERS = 2
HCOLS = 1280
TROWS = 1408
CHUNK = 16
GROUP = 8
WIDE = 16
EPSILON = 1e-06
MOMENTUM_RATE = 0.9
AVERAGE_RATE = 0.7
CLIP_SCALE = 0.2
STEP_SCALE = 0.03
MASKED = -1e30
POSITION_SCALE = 0.5
SCALE = HD ** (-0.5)
BF = jnp.bfloat16
F32 = jnp.float32
VMEM_LIMIT = 63 * 1000 * 1000


def dot_nn(a, b):
    return lax.dot_general(a, b, (((1,), (0,)), ((), ())), preferred_element_type=F32)


def dot_nt(a, b):
    return lax.dot_general(a, b, (((1,), (1,)), ((), ())), preferred_element_type=F32)


def dot_tn(a, b):
    return lax.dot_general(a, b, (((0,), (0,)), ((), ())), preferred_element_type=F32)


def iota(shape, dim):
    return lax.broadcasted_iota(jnp.int32, shape, dim)


def position_rows():
    distance = np.arange(TOKS, dtype=np.float32)[:, None]
    rates = np.exp(np.arange(D // 2, dtype=np.float32) * np.float32(-2.0 * math.log(10000.0) / D))
    angle = (distance * rates[None, :].astype(np.float32)).astype(np.float32)
    table = np.float32(POSITION_SCALE) * np.concatenate([np.sin(angle), np.cos(angle)], axis=1)
    rows = np.zeros((3, TOKS, D), np.float32)
    for i in range(3):
        for j in range(3):
            for e in range(STEPS):
                d = 3 * (STEPS - 1 - e) + i - j
                if d >= 0:
                    rows[i, j * STEPS + e] = table[d]
    return rows.reshape(3 * TOKS, D)


def rms(values):
    return lax.rsqrt(jnp.mean(values * values, axis=-1, keepdims=True) + EPSILON)


def head_mask(h, rows):
    lane = iota((rows, 128), 1)
    low = (h % 4) * HD
    return ((lane >= low) & (lane < low + HD)).astype(F32).astype(BF)


def expand(rows):
    zero = jnp.zeros((TOKS, 128), BF)
    parts = []
    for h in range(HEADS):
        half = rows[:, 128 * (h // 4) : 128 * (h // 4) + 128] * head_mask(h, TOKS)
        parts.append(jnp.concatenate([half, zero] if h < 4 else [zero, half], axis=1))
    return jnp.concatenate(parts, axis=0)


def fold(values):
    lane = iota((TOKS, 128), 1)
    halves = []
    for g in range(2):
        total = None
        for h in range(4):
            part = values[(4 * g + h) * TOKS : (4 * g + h + 1) * TOKS, 128 * g : 128 * g + 128]
            total = part if total is None else jnp.where(lane >= h * HD, part, total)
        halves.append(total)
    return jnp.concatenate(halves, axis=1)


def spans(tile):
    found = []
    for h in range(HEADS):
        low, high = max(TOKS * h - 128 * tile, 0), min(TOKS * (h + 1) - 128 * tile, 128)
        if low < high:
            found.append((h, low, high))
    return found


def segment_max(scores):
    rows = scores.shape[0]
    lane = iota((rows, 128), 1)
    tiles = [scores[:, 128 * t : 128 * t + 128] for t in range(3)]
    best = {}
    for t in range(3):
        for h, low, high in spans(t):
            part = jnp.where((lane >= low) & (lane < high), tiles[t], -3e38)
            best[h] = part if h not in best else jnp.maximum(best[h], part)
    best = {h: jnp.max(v, axis=1, keepdims=True) for h, v in best.items()}
    outs = []
    for t in range(3):
        total = None
        for h, low, high in spans(t):
            wide = jnp.broadcast_to(best[h], (rows, 128))
            total = wide if total is None else jnp.where(lane >= low, wide, total)
        outs.append(total)
    return jnp.concatenate(outs, axis=1)


def unskew(values):
    row = iota((STEPS, HK), 0)
    values = jnp.concatenate(
        [pltpu.roll(values[:8], 15, 1), pltpu.roll(values[8:], 7, 1)], axis=0
    )
    for bit in (1, 2, 4):
        values = jnp.where((row & bit) > 0, pltpu.roll(values, HK - bit, 1), values)
    return values


SECTIONS = (2560, 4608, 2048, 4608, 2048, 2560)
DUE = ((1, 3, 5, 7, 9, 10), (3, 6, 8, 10), (7, 9, 11), (9, 12), (), ())


def stage_orders(streams, groups):
    rest, others = [], []
    step = 2
    while step < streams:
        rest.append(("stream", step))
        step *= 2
    step = 1
    while step < groups:
        others.append(("seq", step))
        step *= 2
    near = [tuple(others[:1] + rest)]
    far = [tuple(others[k : k + 2]) for k in range(1, len(others), 2)]
    core = [(("stream", 1),)]
    return [core + near + far, core + far + near]


def exchange_plan(streams, groups):
    unit = 16 * streams * groups
    sections = SECTIONS
    if any(s % unit or s < 2 * unit for s in sections):
        sections = (sum(SECTIONS),)
    orders = stage_orders(streams, groups)
    plan, base, recv, own = [], 0, 0, 0
    for rows in sections:
        units = rows // unit
        last = max(1, round(0.13 * units))
        lanes = []
        for part, order in zip((units - last, last), orders):
            size, sizes, slots = part * unit, [], []
            for bits in order:
                size //= 2 ** len(bits)
                sizes.append(size)
                slots.append(recv)
                recv += size * (2 ** len(bits) - 1)
            lanes.append(dict(base=base, order=order, sizes=sizes, slots=slots, own=own))
            own += size
            base += part * unit
        plan.append(lanes)
    assert base == sum(SECTIONS)
    return plan, recv, own


def place_of(bit):
    axis, step = bit
    return (lax.axis_index(axis) // step) % 2


def flips_of(bits):
    count = len(bits)
    return [tuple((n >> k) % 2 for k in range(count)) for n in range(1, 2**count)]


def partner_of(bits, flips):
    place = {"stream": lax.axis_index("stream"), "seq": lax.axis_index("seq")}
    for bit, flip in zip(bits, flips):
        if flip:
            axis, step = bit
            place[axis] = place[axis] + step * (1 - 2 * place_of(bit))
    return (place["stream"], place["seq"])


def share_of(bits, flips):
    total = 0
    for bit, flip in zip(bits, flips):
        mine = place_of(bit)
        total = 2 * total + ((1 - mine) if flip else mine)
    return total


class Lane:
    def __init__(self, spec, refs, sems, own_sem):
        self.spec, self.sems, self.own_sem = spec, sems, own_sem
        self.g, self.out, self.recv, self.own = refs
        offset = spec["base"]
        self.keep, self.send = [], []
        for bits, size in zip(spec["order"], spec["sizes"]):
            self.send.append(
                [
                    pl.multiple_of(offset + share_of(bits, flips) * size, 16)
                    for flips in flips_of(bits)
                ]
            )
            offset = pl.multiple_of(offset + share_of(bits, (0,) * len(bits)) * size, 16)
            self.keep.append(offset)

    def remote(self, kind, i, n, src, dst):
        bits = self.spec["order"][i]
        return pltpu.make_async_remote_copy(
            src_ref=src,
            dst_ref=dst,
            send_sem=self.sems.at[2 * kind, i, n],
            recv_sem=self.sems.at[2 * kind + 1, i, n],
            device_id=partner_of(bits, flips_of(bits)[n]),
            device_id_type=pl.DeviceIdType.MESH,
        )

    def scatter(self, i):
        size, slot = self.spec["sizes"][i], self.spec["slots"][i]
        return [
            self.remote(
                0, i, n, self.g.at[pl.ds(at, size)], self.recv.at[pl.ds(slot + n * size, size)]
            )
            for n, at in enumerate(self.send[i])
        ]

    def mine(self):
        return self.own.at[pl.ds(self.spec["own"], self.spec["sizes"][-1])]

    def keep_copy(self):
        rows = pl.ds(self.keep[-1], self.spec["sizes"][-1])
        return pltpu.make_async_copy(self.mine(), self.out.at[rows], self.own_sem)

    def gather(self, i):
        rows = pl.ds(self.keep[i], self.spec["sizes"][i])
        last = i + 1 == len(self.keep)
        return [
            self.remote(1, i, n, self.mine() if last else self.out.at[rows], self.out.at[rows])
            for n in range(len(self.send[i]))
        ]

    def add(self, i):
        size, slot = self.spec["sizes"][i], self.spec["slots"][i]
        last = i + 1 == len(self.keep)
        block = 256
        while size % block:
            block //= 2

        @pl.loop(0, size // block)
        def _(j):
            at = pl.ds(pl.multiple_of(self.keep[i] + j * block, 16), block)
            value = self.g[at].astype(F32)
            for n in range(len(self.send[i])):
                got = pl.ds(pl.multiple_of(slot + n * size + j * block, 16), block)
                value = value + self.recv[got].astype(F32)
            if last:
                own = pl.multiple_of(self.spec["own"] + j * block, 16)
                self.own[pl.ds(own, block)] = value.astype(BF)
            else:
                self.g[at] = value.astype(BF)


def start_all(copies):
    for copy in copies:
        copy.start()


def wait_all(copies):
    for copy in copies:
        copy.wait()


class Exchange:
    def __init__(self, streams, groups, g_ref, out_ref, recv_ref, own_ref, sems, own_sems):
        plan, _, _ = exchange_plan(streams, groups)
        refs = (g_ref, out_ref, recv_ref, own_ref)
        self.sections = [
            [
                Lane(spec, refs, sems.at[n, k], own_sems.at[n, k])
                for k, spec in enumerate(lanes)
            ]
            for n, lanes in enumerate(plan)
        ]
        self.order = plan[0][0]["order"]
        self.stages = len(self.order)
        self.active = []
        self.moment = 0

    def open(self, n):
        if len(self.sections) > 1:
            for lane in self.sections[n]:
                start_all(lane.scatter(0))
            self.active.append([n, 0])

    def advance(self, n, stage):
        stages = self.stages
        for lane in self.sections[n]:
            if stage < stages:
                wait_all(lane.scatter(stage))
                lane.add(stage)
                if stage + 1 < stages:
                    start_all(lane.scatter(stage + 1))
                else:
                    start_all(lane.gather(stage))
                    lane.keep_copy().start()
            else:
                i = 2 * stages - 1 - stage
                wait_all(lane.gather(i))
                if i + 1 == stages:
                    lane.keep_copy().wait()
                if i:
                    start_all(lane.gather(i - 1))

    def plan(self, count):
        moments = []
        for _ in range(count):
            self.moment += 1
            ready = [
                item
                for item in self.active
                if item[1] < len(DUE[item[0]]) and DUE[item[0]][item[1]] <= self.moment
            ]
            moments.append(self.step(ready))
        return moments

    def step(self, items):
        taken = [tuple(item) for item in items]
        for item in items:
            item[1] += 1
        self.active = [item for item in self.active if item[1] < 2 * self.stages]
        return taken

    def emit(self, moment):
        for n, stage in moment:
            self.advance(n, stage)

    def tick(self):
        self.emit(self.plan(1)[0])

    def when(self, condition, moment):
        if moment:
            pl.when(condition)(lambda: self.emit(moment))

    def finish(self, slot_ref, got_ref, sems, total_ref):
        last = len(self.sections) - 1

        def extra(i):
            bits = self.order[i]
            return [
                pltpu.make_async_remote_copy(
                    src_ref=slot_ref.at[i],
                    dst_ref=got_ref.at[i, n],
                    send_sem=sems.at[0, i, n],
                    recv_sem=sems.at[1, i, n],
                    device_id=partner_of(bits, flips),
                    device_id_type=pl.DeviceIdType.MESH,
                )
                for n, flips in enumerate(flips_of(bits))
            ]

        for lane in self.sections[last]:
            start_all(lane.scatter(0))
        start_all(extra(0))
        self.active.append([last, 0])
        i = 0
        while self.active:
            self.emit(self.step(list(reversed(self.active))))
            if i < self.stages:
                wait_all(extra(i))
                slot_ref[i + 1] = self.total(slot_ref[i], got_ref, i)
                if i + 1 < self.stages:
                    start_all(extra(i + 1))
            i += 1
        total_ref[...] = slot_ref[self.stages]

    def total(self, mine, got_ref, i):
        bits = self.order[i]
        if len(bits) == 1:
            return mine + got_ref[i, 0]
        return (mine + got_ref[i, 0]) + (got_ref[i, 1] + got_ref[i, 2])

def step_kernel(
    streams,
    groups,
    codes_hbm,
    seg_ref,
    pos_ref,
    small_ref,
    table_hbm,
    qkv_hbm,
    square_hbm,
    up_hbm,
    down_hbm,
    head_hbm,
    out_hbm,
    total_ref,
    x_s,
    att_s,
    pu_s,
    o_s,
    mid_s,
    hb_s,
    gp_s,
    b_s,
    dyl_s,
    dml_s,
    rk_s,
    start_s,
    l_s,
    slope_s,
    table_s,
    tail_s,
    wqkv_s,
    wsq_s,
    wup_s,
    wdown_s,
    whead_s,
    wheadt_s,
    raw_s,
    send_s,
    got_codes_s,
    g_s,
    recv_s,
    own_s,
    slot_s,
    got_s,
    load_sems,
    code_sems,
    sems,
    own_sems,
    extra_sems,
):
    toks = x_s.shape[1]
    seqs = toks // TOKS
    steps_all = seqs * STEPS
    chunks = seqs // CHUNK
    rows_c = CHUNK * TOKS
    me = lax.axis_index("stream")
    table_rows = table_hbm.shape[0]

    raw_load = pltpu.make_async_copy(codes_hbm, raw_s, load_sems.at[0])
    raw_load.start()
    whole = table_rows // 128 * 128
    rest = table_rows - whole
    loads = []

    def load(src, place, targets):
        copy = pltpu.make_async_copy(src, place, load_sems.at[len(loads) + 1])
        loads.append((copy, place, targets))

    table_rows_main = pl.ds(0, whole)
    load(
        table_hbm.at[table_rows_main],
        x_s.at[2, table_rows_main],
        [(table_s.at[table_rows_main], False)],
    )
    load(table_hbm.at[pl.ds(whole, rest)], tail_s, None)
    for layer in range(LAYERS):
        places = [o_s.at[layer, pl.ds(256 * j, 256)] for j in range(6)]
        places += [mid_s.at[layer, pl.ds(256 * j, 256)] for j in range(6)]
        places += [x_s.at[1, pl.ds(256 * layer, 256)]]
        places = iter(places)
        for j in range(3):
            cols = pl.ds(256 * j, 256)
            load(qkv_hbm.at[layer, :, cols], next(places), [(wqkv_s.at[layer, :, cols], False)])
        for j in range(2):
            load(square_hbm.at[layer, j], next(places), [(wsq_s.at[layer, j], False)])
        for j in range(4):
            cols = pl.ds(256 * j, 256)
            load(up_hbm.at[layer, :, cols], next(places), [(wup_s.at[layer, :, cols], False)])
        for j in range(4):
            cols = pl.ds(256 * j, 256)
            load(down_hbm.at[layer, cols], next(places), [(wdown_s.at[layer, cols], False)])
    for j in range(HCOLS // 256):
        cols = pl.ds(256 * j, 256)
        load(
            head_hbm.at[:, cols],
            x_s.at[1, pl.ds(512 + 256 * j, 256)] if j < 4 else l_s.at[pl.ds(0, 256)],
            [(whead_s.at[:, cols], False), (wheadt_s.at[cols], True)],
        )
    for copy, _, _ in loads:
        copy.start()

    comm = Exchange(streams, groups, g_s, out_hbm, recv_s, own_s, sems, own_sems)
    barrier = pltpu.get_barrier_semaphore()
    greeted = [((me + j) % streams, lax.axis_index("seq")) for j in range(1, streams)]
    peers = list(greeted)
    for bits in comm.order:
        for flips in flips_of(bits):
            if any(flip and bit[0] == "seq" for bit, flip in zip(bits, flips)):
                greeted.append(partner_of(bits, flips))
    for peer in greeted:
        pl.semaphore_signal(
            barrier, inc=1, device_id=peer, device_id_type=pl.DeviceIdType.MESH
        )

    raw_load.wait()
    send_s[...] = raw_s[...].astype(F32).astype(BF)
    pl.semaphore_wait(barrier, len(greeted))
    sends = []
    for j, peer in enumerate(peers):
        sends.append(
            pltpu.make_async_remote_copy(
                src_ref=send_s,
                dst_ref=got_codes_s.at[me],
                send_sem=code_sems.at[0, j],
                recv_sem=code_sems.at[1, j],
                device_id=peer,
                device_id_type=pl.DeviceIdType.MESH,
            )
        )
        sends[-1].start()
    got_codes_s[me] = send_s[...]

    group = seg_ref.shape[1]
    step_lane = iota((STEPS, steps_all), 1) % STEPS
    step_row = iota((STEPS, steps_all), 0)
    own_lane = iota((group, steps_all), 1) // STEPS + me * seqs
    pick = (iota((group, steps_all), 0) == own_lane).astype(F32).astype(BF)
    seg = dot_nn(seg_ref[...].astype(F32).astype(BF), pick)
    seg_own = jnp.sum(jnp.where(step_row == step_lane, seg, 0.0), axis=0, keepdims=True)
    start = jnp.sum(jnp.where(seg < seg_own, 1.0, 0.0), axis=0, keepdims=True)
    valid_row = jnp.sum(
        jnp.where((step_row == step_lane + 1) & (seg == seg_own), 1.0, 0.0), axis=0, keepdims=True
    )
    start_low = jnp.broadcast_to(start, (STEPS, steps_all)).astype(BF)
    one_row = (iota((STEPS, 128), 0) == 0).astype(F32).astype(BF)
    start_s[...] = dot_tn(start_low, one_row).reshape(seqs, STEPS, 128)

    table_s[whole:] = jnp.zeros((TROWS - whole, D), BF)
    for copy, place, targets in loads:
        copy.wait()
        if targets is None:
            pad = -rest % 16
            table_s[whole : whole + rest + pad] = jnp.concatenate(
                [place[...], jnp.zeros((pad, D), F32)], axis=0
            ).astype(BF)
            continue
        for target, turned in targets:
            target[...] = (place[...].T if turned else place[...]).astype(BF)
    for copy in sends:
        copy.wait()
    codes = []
    for k in range(4):
        wide = dot_nn(got_codes_s[k].reshape(STEPS * STEPS, group), pick)
        wide = wide.reshape(STEPS, STEPS, steps_all)
        at_step = iota((STEPS, STEPS, steps_all), 0) == iota((STEPS, STEPS, steps_all), 2) % STEPS
        codes.append(jnp.sum(jnp.where(at_step, wide, 0.0), axis=0).astype(BF))

    spread = (iota((STEPS, 512), 1) // CLASSES == iota((STEPS, 512), 0)).astype(F32).astype(BF)
    first = (iota((STEPS, 384), 0) == 0).astype(F32).astype(BF)
    class_lane = (iota((128, 512), 1) % CLASSES).astype(F32)
    lane = iota((128, 384), 1).astype(F32)
    for c in range(steps_all // 128):
        cols = slice(128 * c, 128 * c + 128)
        halves = []
        for k in range(2):
            hot = (dot_tn(codes[k][:, cols], spread) == class_lane).astype(F32).astype(BF)
            piece = dot_nn(hot, table_s[512 * k : 512 * k + 512]).astype(BF).astype(F32)
            halves.append(piece)
        hot = (dot_tn(codes[2][:, cols], first[:, :128]) == lane[:, :128]).astype(F32).astype(BF)
        action = dot_nn(hot, table_s[1024:1152]).astype(BF).astype(F32)
        hot = (dot_tn(codes[3][:, cols], first) + NA == lane).astype(F32).astype(BF)
        reward = dot_nn(hot, table_s[1024:1408]).astype(BF).astype(F32)
        pieces = [p.reshape(8, 1, STEPS, D) for p in (halves[0] + halves[1], action, reward)]
        x_s[0, 384 * c : 384 * c + 384] = jnp.concatenate(pieces, axis=1).reshape(384, D)
    for layer in range(LAYERS):
        rk = dot_nn(pos_ref[...], wsq_s[layer, 1]).astype(BF)
        for k in range(3):
            rk_s[layer, k] = expand(rk[TOKS * k : TOKS * k + TOKS])

    lane_hk = iota((TOKS, HK), 1) % TOKS
    key_step = lane_hk % STEPS
    key_time = 3 * key_step + lane_hk // STEPS
    row_tok = iota((TOKS, HK), 0)
    query_time = 3 * (row_tok % STEPS) + row_tok // STEPS
    causal = key_time <= query_time
    key_step_f = key_step.astype(F32)
    sum_hd = (iota((HK, D), 0) // TOKS == iota((HK, D), 1) // HD).astype(F32).astype(BF)
    sum_hk = (iota((D, HK), 0) // HD == iota((D, HK), 1) // TOKS).astype(F32).astype(BF)

    for layer in range(LAYERS):
        gain_a = small_ref[4 * layer : 4 * layer + 1]
        gain_b = small_ref[4 * layer + 1 : 4 * layer + 2]
        bias_u = small_ref[4 * layer + 2 : 4 * layer + 3]
        bias_v = small_ref[4 * layer + 3 : 4 * layer + 4]

        @pl.loop(0, chunks)
        def _(c):
            rows = pl.ds(pl.multiple_of(c * rows_c, rows_c), rows_c)
            x = x_s[layer, rows]
            low = (x * rms(x) * gain_a).astype(BF)
            q = dot_nn(low, wqkv_s[layer, :, :256]).astype(BF).astype(F32)
            qu = (q + bias_u).astype(BF)
            qv = (q + bias_v).astype(BF)
            key = dot_nn(low, wqkv_s[layer, :, 256:512]).astype(BF)
            val = dot_nn(low, wqkv_s[layer, :, 512:]).astype(BF)
            att_s[layer, rows, 0:256] = qu
            att_s[layer, rows, 256:512] = qv
            att_s[layer, rows, 512:768] = key
            att_s[layer, rows, 768:1024] = val
            qv4 = qv.reshape(CHUNK, 3, STEPS, D)
            place = [
                dot_nt(qv4[:, k].reshape(CHUNK * STEPS, D), rk_s[layer, k]) for k in range(3)
            ]
            start_c = start_s[pl.ds(c * CHUNK, CHUNK)]
            for g in range(0, CHUNK, WIDE):
                members = range(g, g + WIDE)
                spans = {b: slice(TOKS * b, TOKS * b + TOKS) for b in members}
                scores = {b: dot_nt(qu[spans[b]], expand(key[spans[b]])) for b in members}
                for b in members:
                    shifted = [
                        pltpu.roll(
                            place[k][STEPS * b : STEPS * b + STEPS],
                            HK - (STEPS - 1),
                            1,
                            stride=1,
                            stride_axis=0,
                        )
                        for k in range(3)
                    ]
                    begin = jnp.concatenate([start_c[b]] * 3, axis=0)
                    begin = jnp.concatenate([begin] * 3, axis=1)
                    score = (scores[b] + jnp.concatenate(shifted, axis=0)) * SCALE
                    scores[b] = jnp.where(causal & (key_step_f >= begin), score, MASKED)
                tops = {b: segment_max(scores[b]) for b in members}
                probs = {b: jnp.exp(scores[b] - tops[b]).astype(BF) for b in members}
                for b in members:
                    l_s[spans[b]] = dot_nn(probs[b], expand(val[spans[b]]))
                for b in members:
                    pu_s[layer, pl.ds(pl.multiple_of(c * rows_c + TOKS * b, TOKS), TOKS)] = probs[b]
            recip = 1.0 / dot_nn(pu_s[layer, rows], sum_hd)
            out = l_s[...] * recip
            o_s[layer, rows] = out
            mid = x + dot_nn(out.astype(BF), wsq_s[layer, 0])
            mid_s[layer, rows] = mid
            low = (mid * rms(mid) * gain_b).astype(BF)
            for j in range(FF // 256):
                cols = slice(256 * j, 256 * j + 256)
                inner = dot_nn(low, wup_s[layer, :, cols])
                square = inner * inner
                c0 = math.sqrt(2.0 / math.pi)
                tanh = jnp.tanh(c0 * inner * (1.0 + 0.044715 * square))
                half = 0.5 * (1.0 + tanh)
                hb_s[layer, rows, cols] = (inner * half).astype(BF)
                gp_s[layer, rows, cols] = (
                    half
                    + (0.5 * c0) * inner * (1.0 - tanh * tanh) * (1.0 + (3 * 0.044715) * square)
                ).astype(BF)
            nxt = mid + dot_nn(hb_s[layer, rows], wdown_s[layer])
            x_s[layer + 1, rows] = nxt

    gain_f = small_ref[4 * LAYERS : 4 * LAYERS + 1]
    xf = x_s[LAYERS].reshape(seqs, 3, STEPS, D)[:, 1].reshape(steps_all, D)
    feat = (xf * rms(xf) * gain_f).astype(BF)
    spread_t = (iota((512, STEPS), 0) // CLASSES == iota((512, STEPS), 1)).astype(F32).astype(BF)
    class_row = iota((4, CLASSES, steps_all), 1).astype(F32)
    loss = jnp.zeros((4, steps_all), F32)
    ahead = dot_nt(wheadt_s[0:128], feat)
    for k in range(2):
        follow_codes = pltpu.roll(codes[k].astype(F32), steps_all - 1, 1).astype(BF)
        for j in range(4):
            base = 512 * k + 128 * j
            logits = ahead.reshape(4, CLASSES, steps_all)
            after = base + 128
            ahead = dot_nt(wheadt_s[after : after + (128 if after < 1024 else 256)], feat)
            target = dot_nn(spread_t[128 * j : 128 * j + 128], follow_codes)
            hot = target.reshape(4, CLASSES, steps_all) == class_row
            top = jnp.max(logits, axis=1, keepdims=True)
            grown = jnp.exp(logits - top)
            total = jnp.sum(grown, axis=1, keepdims=True)
            picked = jnp.sum(jnp.where(hot, logits, 0.0), axis=1)
            loss = loss + valid_row * (jnp.log(total[:, 0]) + top[:, 0] - picked)
            slope = (grown * (1.0 / total) - jnp.where(hot, 1.0, 0.0)) * valid_row[None]
            slope_s[base : base + 128] = slope.reshape(128, steps_all).astype(BF)
    action_row = codes[2][0:1].astype(F32)
    discount_row = codes[2][1:2].astype(F32)
    reward_row = codes[3][0:1].astype(F32)
    logits = ahead
    row = iota((256, steps_all), 0)
    hot = row == (reward_row + 1.0).astype(jnp.int32)
    disc = logits[:1]
    masked = jnp.where(row == 0, -3e38, logits)
    top = jnp.max(masked, axis=0, keepdims=True)
    grown = jnp.exp(masked - top)
    total = jnp.sum(grown, axis=0, keepdims=True)
    picked = jnp.sum(jnp.where(hot, logits, 0.0), axis=0, keepdims=True)
    fade = jnp.exp(-jnp.abs(disc))
    soft = jnp.maximum(disc, 0.0) + jnp.log(1.0 + fade)
    sigm = jnp.where(disc >= 0.0, 1.0, fade) / (1.0 + fade)
    loss_row = (
        jnp.sum(loss, axis=0, keepdims=True)
        + jnp.log(total)
        + top
        - picked
        + soft
        - discount_row * disc
    )
    slope = grown * (1.0 / total) - jnp.where(hot, 1.0, 0.0)
    slope = jnp.where(row == 0, sigm - discount_row, slope)
    slope_s[1024:1280] = slope.astype(BF)
    loss_sum = jnp.sum(loss_row)
    count = jnp.sum(valid_row) * CATS + 2.0 * steps_all
    slot_s[0, 9:10] = jnp.full((1, D), loss_sum, F32)
    slot_s[0, 10:11] = jnp.full((1, D), count, F32)
    slot_s[0, 11:16] = jnp.zeros((5, D), F32)

    feat_t = feat.astype(F32).T.astype(BF)
    for j in range(5):
        part = dot_nt(feat_t, slope_s[256 * j : 256 * j + 256])
        for k in range(2):
            base = 256 * (2 * j + k)
            g_s[base : base + 256] = part[:, 128 * k : 128 * k + 128].astype(BF)
    comm.open(0)
    dfeat = dot_nn(whead_s[...], slope_s[...]).T
    scale_f = rms(xf)
    hat = xf * scale_f
    slot_s[0, 8:9] = jnp.sum(dfeat * hat, axis=0, keepdims=True)
    inner = dfeat * gain_f
    dxf = scale_f * (inner - hat * jnp.mean(inner * hat, axis=-1, keepdims=True))
    gap = jnp.zeros((seqs, 1, STEPS, D), F32)
    x_s[LAYERS] = jnp.concatenate([gap, dxf.reshape(seqs, 1, STEPS, D), gap], axis=1).reshape(
        toks, D
    )

    for layer in reversed(range(LAYERS)):
        gain_a = small_ref[4 * layer : 4 * layer + 1]
        gain_b = small_ref[4 * layer + 1 : 4 * layer + 2]
        slot_s[0, 4 * layer : 4 * layer + 4] = jnp.zeros((4, D), F32)

        moments = comm.plan(chunks - 1)

        @pl.loop(0, chunks)
        def _(c):
            rows = pl.ds(pl.multiple_of(c * rows_c, rows_c), rows_c)
            for k in range(1, chunks):
                comm.when(c == k, moments[k - 1])
            dy = x_s[LAYERS, rows]
            dyl = dy.astype(BF)
            dyl_s[rows] = dyl
            for j in range(FF // 256):
                cols = slice(256 * j, 256 * j + 256)
                dact = dot_nt(dyl, wdown_s[layer, cols])
                gp_s[layer, rows, cols] = (dact * gp_s[layer, rows, cols].astype(F32)).astype(BF)
            dlow = dot_nt(gp_s[layer, rows], wup_s[layer])
            mid = mid_s[layer, rows]
            scale = rms(mid)
            hat = mid * scale
            b_s[rows] = (hat * gain_b).astype(BF)
            dgain = jnp.sum(dlow * hat, axis=0, keepdims=True)
            inner = dlow * gain_b
            dmid = scale * (inner - hat * jnp.mean(inner * hat, axis=-1, keepdims=True)) + dy
            slot_s[0, 4 * layer + 1 : 4 * layer + 2] += dgain
            mid_s[layer, rows] = dmid
            dml_s[rows] = dmid.astype(BF)

        base = 2560 + 6656 * (LAYERS - 1 - layer)

        def put(offset, value, base=base):
            size = value.shape[0]
            for k in range(2):
                at = base + offset + k * size
                g_s[at : at + size] = value[:, 128 * k : 128 * k + 128].astype(BF)

        comm.tick()
        for j in range(4):
            part = dot_tn(hb_s[layer, :, 256 * j : 256 * j + 256], dyl_s[...])
            for k in range(2):
                at = base + 1024 * k + 256 * j
                g_s[at : at + 256] = part[:, 128 * k : 128 * k + 128].astype(BF)
        for j in range(4):
            put(2048 + 512 * j, dot_tn(b_s[...], gp_s[layer, :, 256 * j : 256 * j + 256]))
        put(4096, dot_tn(o_s[layer].astype(BF), dml_s[...]))
        comm.open(1 + 2 * (LAYERS - 1 - layer))
        moments = comm.plan(seqs // GROUP - 1)
        rows_a = GROUP * TOKS

        @pl.loop(0, seqs // GROUP)
        def _(c):
            rows = pl.ds(pl.multiple_of(c * rows_a, rows_a), rows_a)
            for k in range(1, seqs // GROUP):
                comm.when(c == k, moments[k - 1])
            dmid = mid_s[layer, rows]
            dml = dml_s[rows]
            recip = 1.0 / dot_nn(pu_s[layer, rows], sum_hd)
            do = dot_nt(dml, wsq_s[layer, 0]).astype(BF).astype(F32)
            do = (do * recip).astype(BF)
            mass = do.astype(F32) * o_s[layer, rows]
            mass_hi = mass.astype(BF)
            mass_lo = (mass - mass_hi.astype(F32)).astype(BF)
            delta = dot_nn(mass_hi, sum_hk) + dot_nn(mass_lo, sum_hk)
            qu = att_s[layer, rows, 0:256]
            key = att_s[layer, rows, 512:768]
            val = att_s[layer, rows, 768:1024]
            probs_all = pu_s[layer, rows]
            draws = {}
            for g in range(1):
                members = range(g, g + GROUP)
                spans = {b: slice(TOKS * b, TOKS * b + TOKS) for b in members}
                dprob = {b: dot_nt(do[spans[b]], expand(val[spans[b]])) for b in members}
                dval = {b: dot_tn(probs_all[spans[b]], do[spans[b]]) for b in members}
                dscore = {
                    b: (probs_all[spans[b]].astype(F32) * (dprob[b] - delta[spans[b]])).astype(BF)
                    for b in members
                }
                dkey = {b: dot_tn(dscore[b], qu[spans[b]]) for b in members}
                dque = {b: dot_nn(dscore[b], expand(key[spans[b]])) for b in members}
                for b in members:
                    wide = dscore[b].astype(F32)
                    draws[b] = [
                        unskew(wide[STEPS * k : STEPS * k + STEPS]).astype(BF) for k in range(3)
                    ]
                for b in members:
                    l_s[spans[b]] = dque[b] * SCALE
                for b in members:
                    out_rows = pl.ds(pl.multiple_of(c * rows_a + TOKS * b, TOKS), TOKS)
                    att_s[layer, out_rows, 512:768] = (fold(dkey[b]) * SCALE).astype(BF)
                    att_s[layer, out_rows, 768:1024] = fold(dval[b]).astype(BF)
                    pu_s[layer, out_rows] = jnp.concatenate(draws[b], axis=0)
            dqv = [
                dot_nn(
                    jnp.concatenate([draws[b][k] for b in range(GROUP)], axis=0), rk_s[layer, k]
                ).reshape(GROUP, 1, STEPS, D)
                for k in range(3)
            ]
            dqv = jnp.concatenate(dqv, axis=1).reshape(rows_a, D) * SCALE
            dqu = l_s[0:rows_a]
            slot_s[0, 4 * layer + 2 : 4 * layer + 3] += jnp.sum(dqu, axis=0, keepdims=True)
            slot_s[0, 4 * layer + 3 : 4 * layer + 4] += jnp.sum(dqv, axis=0, keepdims=True)
            dq = (dqu + dqv).astype(BF)
            att_s[layer, rows, 0:256] = dq
            dlow = (
                dot_nt(dq, wqkv_s[layer, :, :256])
                + dot_nt(att_s[layer, rows, 512:768], wqkv_s[layer, :, 256:512])
                + dot_nt(att_s[layer, rows, 768:1024], wqkv_s[layer, :, 512:])
            )
            x = x_s[layer, rows]
            scale = rms(x)
            hat = x * scale
            dyl_s[rows] = (hat * gain_a).astype(BF)
            slot_s[0, 4 * layer : 4 * layer + 1] += jnp.sum(dlow * hat, axis=0, keepdims=True)
            inner = dlow * gain_a
            dx = scale * (inner - hat * jnp.mean(inner * hat, axis=-1, keepdims=True)) + dmid
            x_s[LAYERS, rows] = dx

        comm.tick()
        drk = []
        draw = pu_s[layer].reshape(seqs, 3, STEPS, HK)
        qv = att_s[layer, :, 256:512].reshape(seqs, 3, STEPS, D)
        for k in range(3):
            wide = dot_tn(
                draw[:, k].reshape(steps_all, HK), qv[:, k].reshape(steps_all, D)
            )
            drk.append(fold(wide) * SCALE)
        put(4608, dot_tn(pos_ref[...], jnp.concatenate(drk, axis=0).astype(BF)))
        put(5120, dot_tn(dyl_s[...], att_s[layer, :, 0:256]))
        put(5632, dot_tn(dyl_s[...], att_s[layer, :, 512:768]))
        put(6144, dot_tn(dyl_s[...], att_s[layer, :, 768:1024]))
        comm.open(2 * (LAYERS - layer))

    dtok = x_s[LAYERS].reshape(seqs, 3, STEPS, D).astype(BF)
    dtok = [dtok[:, k].reshape(steps_all, D) for k in range(3)]
    base = 2560 + 6656 * LAYERS
    class_row = (iota((256, steps_all), 0) % CLASSES).astype(F32)
    for k in range(2):
        for j in range(2):
            wide = dot_nn(spread_t[256 * j : 256 * j + 256], codes[k])
            hot = (wide == class_row).astype(F32).astype(BF)
            part = dot_nn(hot, dtok[0])
            for h in range(2):
                at = base + 1280 * h + 512 * k + 256 * j
                g_s[at : at + 256] = part[:, 128 * h : 128 * h + 128].astype(BF)
    row = iota((288, steps_all), 0)
    hot_a = (row == action_row.astype(jnp.int32)).astype(F32).astype(BF)
    hot_r = (row == (reward_row + NA).astype(jnp.int32)).astype(F32).astype(BF)
    part = dot_nn(hot_a, dtok[1]) + dot_nn(hot_r, dtok[2])
    for h in range(2):
        at = base + 1280 * h + 1024
        g_s[at : at + 256] = part[:256, 128 * h : 128 * h + 128].astype(BF)
    slot_s[0, 16:40] = part[256:280]
    comm.finish(slot_s, got_s, extra_sems, total_ref)


def run_step(codes, seg, pos, small, weights, streams, groups):
    seqs = codes.shape[2] // streams
    toks = seqs * TOKS
    plan, recv, own = exchange_plan(streams, groups)
    stages = len(plan[0][0]["order"])
    vmem, dma = pltpu.VMEM, pltpu.SemaphoreType.DMA
    hbm = pl.BlockSpec(memory_space=pl.ANY)
    table, qkv, square, up, down, head = weights
    return pl.pallas_call(
        lambda *refs: step_kernel(streams, groups, *refs),
        out_shape=(
            jax.ShapeDtypeStruct((sum(SECTIONS), 128), BF),
            jax.ShapeDtypeStruct((40, D), F32),
        ),
        in_specs=[hbm] + [pl.BlockSpec(memory_space=vmem)] * 3 + [hbm] * 6,
        out_specs=[hbm, pl.BlockSpec(memory_space=vmem)],
        scratch_shapes=[
            vmem((LAYERS + 1, toks, D), F32),
            vmem((LAYERS, toks, 1024), BF),
            vmem((LAYERS, toks, HK), BF),
            vmem((LAYERS, toks, D), F32),
            vmem((LAYERS, toks, D), F32),
            vmem((LAYERS, toks, FF), BF),
            vmem((LAYERS, toks, FF), BF),
            vmem((toks, D), BF),
            vmem((toks, D), BF),
            vmem((toks, D), BF),
            vmem((LAYERS, 3, HK, D), BF),
            vmem((seqs, STEPS, 128), F32),
            vmem((CHUNK * TOKS, D), F32),
            vmem((HCOLS, seqs * STEPS), BF),
            vmem((TROWS, D), BF),
            vmem((table.shape[0] % 128, D), F32),
            vmem(qkv.shape, BF),
            vmem(square.shape, BF),
            vmem(up.shape, BF),
            vmem(down.shape, BF),
            vmem(head.shape, BF),
            vmem(head.shape[::-1], BF),
            vmem(codes.shape, jnp.int32),
            vmem(codes.shape, BF),
            vmem((streams,) + codes.shape, BF),
            vmem((sum(SECTIONS), 128), BF),
            vmem((recv, 128), BF),
            vmem((own, 128), BF),
            vmem((stages + 1, 40, D), F32),
            vmem((stages, 3, 40, D), F32),
            dma((3 + 13 * LAYERS + 5,)),
            dma((2, streams - 1)),
            dma((len(plan), 2, 4, stages, 3)),
            dma((len(plan), 2)),
            dma((2, stages, 3)),
        ],
        compiler_params=pltpu.CompilerParams(
            collective_id=0, has_side_effects=True, vmem_limit_bytes=VMEM_LIMIT
        ),
        name="step",
    )(codes, seg, pos, small, table, qkv, square, up, down, head)


def update_pieces():
    pieces = []
    for k in range(LAYERS):
        layer = LAYERS - 1 - k
        base = 2560 + 6656 * k
        for half in range(2):
            r = 512 * half
            pieces.append(
                (4, (layer,), r, 512, [(base + 1024 * j + r, 128 * j) for j in range(2)])
            )
        pieces.append((3, (layer,), 0, 256, [(base + 2048 + 256 * j, 128 * j) for j in range(8)]))
        pieces.append((2, (layer, 0), 0, 256, [(base + 4096 + 256 * j, 128 * j) for j in range(2)]))
        pieces.append((2, (layer, 1), 0, 256, [(base + 4608 + 256 * j, 128 * j) for j in range(2)]))
        pieces.append((1, (layer,), 0, 256, [(base + 5120 + 256 * j, 128 * j) for j in range(6)]))
    base = 2560 + 6656 * LAYERS
    first = [(6, (), 0, 256, [(256 * j, 128 * j) for j in range(10)])]
    for r in range(0, 1280, 640):
        first.append((0, (), r, 640, [(base + 1280 * j + r, 128 * j) for j in range(2)]))
    return first + sorted(pieces, key=lambda p: -p[3] * len(p[4]))


def update_kernel(clip_value, step_rate, *refs):
    g_ref, e_ref = refs[:2]
    ins = refs[2:23]
    loss_ref, terms_ref, norm_ref = refs[23:26]
    outs = refs[26:47]
    bufs = refs[47:68]
    isem, osem = refs[68:]
    pieces = update_pieces()
    table_rows = ins[0].shape[0]
    tail = table_rows - 1280

    def view(ref, piece):
        array, lead, first, rows, _ = piece
        if lead:
            ref = ref.at[lead]
        if ref.shape[0] == rows:
            return ref
        return ref.at[pl.ds(first, rows)]

    def transfer(kind, n, k, piece):
        src, dst = (ins, bufs) if kind == 0 else (bufs, outs)
        array = piece[0]
        sem = (isem, osem)[kind].at[k, n]
        return pltpu.make_async_copy(
            view(src[7 * k + array], piece), view(dst[7 * k + array], piece), sem
        )

    specials = [(0, (), 1280, tail, None), (5, (), 0, ins[5].shape[0], None)]
    order = pieces + specials
    for n, piece in enumerate(order):
        for k in range(3):
            transfer(0, n, k, piece).start()

    block = 512
    count = g_ref.shape[0] // block

    def gather(j, total):
        v = g_ref[pl.ds(pl.multiple_of(j * block, block), block)].astype(F32)
        return total + jnp.sum((v * v).reshape(block // 64, 64, 128), axis=0)

    total = lax.fori_loop(0, count, gather, jnp.zeros((64, 128), F32))
    rest = jnp.sum(e_ref[0:9] * e_ref[0:9]) + jnp.sum(e_ref[16:40] * e_ref[16:40])
    loss = jnp.max(e_ref[9:10])
    terms = jnp.max(e_ref[10:11])
    inverse = 1.0 / jnp.full((8, 128), terms, F32)
    norm = jnp.sqrt(jnp.full((8, 128), jnp.sum(total) + rest, F32)) * inverse
    factor = inverse * clip_value / jnp.maximum(norm, clip_value)
    loss_ref[0, 0] = loss
    terms_ref[0, 0] = terms
    norm_ref[0, 0] = jnp.max(norm)
    factor = factor[:1]

    def advance(views, rows, cols, gradient, scale):
        w, m, e = [v[rows, cols] for v in views]
        clipped = gradient * scale
        moment = MOMENTUM_RATE * m + clipped
        weight = w - step_rate * (clipped + MOMENTUM_RATE * moment)
        views[0][rows, cols] = weight
        views[1][rows, cols] = moment
        views[2][rows, cols] = AVERAGE_RATE * e + (1.0 - AVERAGE_RATE) * weight

    for n, piece in enumerate(order):
        array, lead, first, rows, blocks = piece
        for k in range(3):
            transfer(0, n, k, piece).wait()
        views = [bufs[7 * k + array].at[lead] if lead else bufs[7 * k + array] for k in range(3)]
        if blocks is None:
            at = 16 if array == 0 else 0
            wide = jnp.concatenate([factor, factor], axis=1)
            advance(
                views, slice(first, first + rows), slice(0, D), e_ref[at : at + rows], wide
            )
        else:
            step = 64

            @pl.loop(0, rows // step)
            def _(j):
                for source, column in blocks:
                    g = g_ref[pl.ds(pl.multiple_of(source + j * step, step), step)].astype(F32)
                    at = pl.ds(pl.multiple_of(first + j * step, step), step)
                    advance(views, at, slice(column, column + 128), g, factor)

        for k in range(3):
            transfer(1, n, k, piece).start()
    for n, piece in enumerate(order):
        for k in range(3):
            transfer(1, n, k, piece).wait()


def update_all(grads, extra, arrays, clip_value, step_rate):
    vmem = pltpu.VMEM
    count = len(update_pieces()) + 2
    hbm = pl.BlockSpec(memory_space=pl.ANY)
    results = pl.pallas_call(
        lambda *refs: update_kernel(clip_value, step_rate, *refs),
        out_shape=[jax.ShapeDtypeStruct((1, 1), F32)] * 3
        + [jax.ShapeDtypeStruct(a.shape, F32) for a in arrays],
        in_specs=[pl.BlockSpec(memory_space=vmem)] * 2 + [hbm] * 21,
        out_specs=[pl.BlockSpec(memory_space=pltpu.SMEM)] * 3 + [hbm] * 21,
        scratch_shapes=[vmem(a.shape, F32) for a in arrays]
        + [pltpu.SemaphoreType.DMA((3, count)), pltpu.SemaphoreType.DMA((3, count))],
        compiler_params=pltpu.CompilerParams(vmem_limit_bytes=VMEM_LIMIT),
        name="update",
    )(grads, extra, *arrays)
    return results[:3], results[3:]


def on_device(step_codes, segments, *arrays):
    streams = lax.axis_size("stream")
    groups = lax.axis_size("seq")
    group_seqs = step_codes.shape[0]
    table, qkv, square, up, down, small, head = arrays[:7]
    pos = jnp.asarray(position_rows()).astype(BF)
    grads, extra = run_step(
        step_codes.transpose(1, 2, 0),
        segments.T,
        pos,
        small,
        (table, qkv, square, up, down, head),
        streams,
        groups,
    )
    params_total = sum(w.size for w in arrays[:7])
    clip_value = CLIP_SCALE * (group_seqs * groups * STEPS) ** (-0.5)
    step_rate = STEP_SCALE * params_total**0.5 / clip_value
    stats, updated = update_all(grads, extra, arrays, clip_value, step_rate)
    return (*(s.reshape(()) for s in stats), *updated)


def solution(mesh):
    return jax.shard_map(
        on_device,
        mesh=mesh,
        in_specs=(P("seq", None, "stream"), P("seq", None)) + (P(),) * 21,
        out_specs=(P(),) * 24,
        check_vma=False,
    )
```
